256 devices in a mesh: grp: 8 (over y, core), blk: 32 (over z, x).
Axes of the slice: x: 4, y: 4, z: 8, core: 2. Of those that a mesh axis runs over, the one named last changes fastest.
Arguments:
- features: bfloat16 [524288, 128], P(('grp', 'blk')), may hold values from -6 to 6
- w_self: bfloat16 [128, 256], replicated, may hold values from -0.5 to 0.5
- w_neigh: bfloat16 [128, 256], replicated, may hold values from -0.5 to 0.5
- cotangent: bfloat16 [524288, 256], P(('grp', 'blk')), may hold values from -6 to 6
- src_block: int32 [256, 32, 4], P(('grp', 'blk')), may hold values from 0 to 15
- dst_block: int32 [256, 32, 4], P(('grp', 'blk')), may hold values from 0 to 127
- block_count: int32 [256, 32], P(('grp', 'blk')), may hold values from 0 to 4, as said below
- edge_rows: int32 [256, 32, 4, 192], P(('grp', 'blk')), may hold values from 0 to 127
- edge_cols: int32 [256, 32, 4, 192], P(('grp', 'blk')), may hold values from 0 to 127
Outputs:
- activated: bfloat16 [524288, 256], P(('grp', 'blk'))
- grad_features: bfloat16 [524288, 128], P(('grp', 'blk'))
- grad_self: float32 [128, 256], replicated
- grad_neigh: float32 [128, 256], replicated
The draws below stay inside these ranges and needn't reach their ends.
Inputs may be any that keep to these rules, and one draw needn't show every extreme that they name: Slot c of sender d for owner o holds data when c < block_count[d, o]; entries of other slots are ignored. In every draw some owner receives 4 used slots from every device of its group. `dst_block`: the destination row block t of a slot to owner o is local block t % 16 of device (t // 16) * 32 + o.
All inputs are finite; a program needn't handle non-finite values.
Results may differ from the reference program's by a relative error of at most 0.0052.
Values may be sent and summed in bfloat16 or wider, within the bound.
No kernel may reach another device: no remote copies, remote signals or barrier semaphores. Data moves between devices by JAX's collectives and lax.ppermute only.
A program may use at most 64 MiB of HBM per device.

```python
import jax
import jax.numpy as jnp
from jax import lax

F = 128
HID = 256
BS = 128
RB = 16
CAP = 4
EDGES = 192
NODES = 524288
N_GRP = 8
N_BLK = 32


def draw_block_count(key, part):
    key = jax.random.fold_in(key, 7)
    first, second, third = jax.random.split(key, 3)
    counts = jax.random.randint(first, (N_GRP * N_BLK, N_BLK), 0, CAP + 1, dtype=jnp.int32)
    chosen_group = jax.random.randint(second, (), 0, N_GRP, dtype=jnp.int32)
    chosen_owner = jax.random.randint(third, (), 0, N_BLK, dtype=jnp.int32)
    senders = jnp.arange(N_GRP * N_BLK, dtype=jnp.int32) // N_BLK
    filled = (senders == chosen_group)[:, None] & (jnp.arange(N_BLK, dtype=jnp.int32) == chosen_owner)[None, :]
    return jnp.where(filled, CAP, counts).astype(jnp.int32)


def plant(drawn, stream_key, least, largest):
    dims = drawn.shape
    index_at = [jax.random.randint(jax.random.fold_in(stream_key, axis), (), 0, dims[axis]) for axis in range(len(dims))]
    drawn = drawn.at[tuple(index_at)].set(least)
    longest = dims.index(max(dims))
    index_at[longest] = (index_at[longest] + 1) % dims[longest]
    return drawn.at[tuple(index_at)].set(largest)


def levels(own_key, extent, pieces, least, largest):
    def one(dim, blocks):
        heights = jax.random.uniform(jax.random.fold_in(jax.random.fold_in(own_key, 6), dim), (blocks,), jnp.float32, least / len(pieces), largest / len(pieces))
        return jnp.repeat(jnp.exp(heights), extent[dim] // blocks).reshape((-1,) + (1,) * (len(extent) - dim - 1))

    gain = one(*pieces[0])
    for cut in pieces[1:]:
        gain = gain * one(*cut)
    return gain


def normal_values(rng, shape, deviation, reach, shards=(), held_as=jnp.bfloat16):
    entries = deviation * jax.random.normal(rng, shape, jnp.float32)
    if shards:
        entries = entries * levels(rng, shape, shards, -0.22, 0.18)
    return jnp.clip(entries, -reach, reach).astype(held_as)


def setup_inputs(seed: int = 0) -> dict:
    keys = jax.random.split(jax.random.key(seed), 10)
    return {
        "features": normal_values(keys[0], (NODES, F), 1.0, 6.0, ((0, 256),)),
        "w_self": normal_values(keys[1], (F, HID), F ** -0.5, 0.5),
        "w_neigh": normal_values(keys[2], (F, HID), F ** -0.5, 0.5),
        "cotangent": normal_values(keys[3], (NODES, HID), 1.0, 6.0, ((0, 256),)),
        "src_block": plant(jax.random.randint(keys[4], (N_GRP * N_BLK, N_BLK, CAP), 0, RB), jax.random.fold_in(keys[4], 1), 0, RB - 1).astype(jnp.int32),
        "dst_block": plant(jax.random.randint(keys[5], (N_GRP * N_BLK, N_BLK, CAP), 0, N_GRP * RB), jax.random.fold_in(keys[5], 1), 0, (N_GRP * RB) - 1).astype(jnp.int32),
        "block_count": draw_block_count(jax.random.fold_in(keys[9], 71), 0),
        "edge_rows": plant(jax.random.randint(keys[7], (N_GRP * N_BLK, N_BLK, CAP, EDGES), 0, BS), jax.random.fold_in(keys[7], 1), 0, BS - 1).astype(jnp.int32),
        "edge_cols": plant(jax.random.randint(keys[8], (N_GRP * N_BLK, N_BLK, CAP, EDGES), 0, BS), jax.random.fold_in(keys[8], 1), 0, BS - 1).astype(jnp.int32),
    }


def reference(features, w_self, w_neigh, cotangent, src_block, dst_block, block_count, edge_rows, edge_cols):
    node_total = features.shape[0]
    senders = jnp.arange(N_GRP * N_BLK, dtype=jnp.int32)[:, None, None, None]
    owners = jnp.arange(N_BLK, dtype=jnp.int32)[None, :, None, None]
    slot_index = jnp.arange(CAP, dtype=jnp.int32)[None, None, :, None]
    in_use = slot_index < block_count[:, :, None, None]
    target = dst_block[..., None]
    src_node = (senders * RB + src_block[..., None]) * BS + edge_cols
    dst_node = (((target // RB) * N_BLK + owners) * RB + target % RB) * BS + edge_rows
    src_node = src_node.astype(jnp.int32).reshape(N_GRP, -1)
    dst_node = jnp.where(in_use, dst_node, 0).astype(jnp.int32).reshape(N_GRP, -1)
    weights = jnp.broadcast_to(in_use, edge_rows.shape).astype(jnp.float32).reshape(N_GRP, -1)

    def gather_step(carry, piece):
        row_sums, counts = carry
        src_part, dst_part, weight_part = piece
        messages = features[src_part].astype(jnp.float32) * weight_part[:, None]
        row_sums = row_sums.at[dst_part].add(messages)
        counts = counts.at[dst_part].add(weight_part)
        return (row_sums, counts), None

    initial = (jnp.zeros((node_total, F), jnp.float32), jnp.zeros((node_total,), jnp.float32))
    (row_sums, counts), unused = lax.scan(gather_step, initial, (src_node, dst_node, weights))
    divisor = jnp.maximum(counts, 1.0)[:, None]
    neigh_mean = (row_sums / divisor).astype(jnp.bfloat16)
    preact = jnp.dot(features, w_self, preferred_element_type=jnp.float32) + jnp.dot(neigh_mean, w_neigh, preferred_element_type=jnp.float32)
    sigmoids = jax.nn.sigmoid(preact)
    activated = (preact * sigmoids).astype(jnp.bfloat16)
    grad_pre = (cotangent.astype(jnp.float32) * sigmoids * (1.0 + preact * (1.0 - sigmoids))).astype(jnp.bfloat16)
    grad_scale = float(node_total) ** -0.5
    grad_self = jnp.dot(features.T, grad_pre, preferred_element_type=jnp.float32) * grad_scale
    grad_neigh = jnp.dot(neigh_mean.T, grad_pre, preferred_element_type=jnp.float32) * grad_scale
    grad_mean = (jnp.dot(grad_pre, w_neigh.T, preferred_element_type=jnp.float32) / divisor).astype(jnp.bfloat16)

    def scatter_step(carry, piece):
        src_part, dst_part, weight_part = piece
        messages = grad_mean[dst_part].astype(jnp.float32) * weight_part[:, None]
        return carry.at[src_part].add(messages), None

    spread, unused = lax.scan(scatter_step, jnp.zeros((node_total, F), jnp.float32), (src_node, dst_node, weights))
    grad_features = (jnp.dot(grad_pre, w_self.T, preferred_element_type=jnp.float32) + spread).astype(jnp.bfloat16)
    return activated, grad_features, grad_self, grad_neigh
```

```python
import functools

import jax
import jax.numpy as jnp
from jax import lax
from jax.experimental import pallas as pl
from jax.experimental.pallas import tpu as pltpu
from jax.sharding import PartitionSpec as P

BS = 128
PAD = 16
F32 = jnp.float32
BF16 = jnp.bfloat16
VMEM_LIMIT = 48 * 1024 * 1024
NT = (((1,), (1,)), ((), ()))


def dot_nt(a, b):
    return lax.dot_general(a, b, NT, preferred_element_type=F32)


def one_hot_t(row, extent):
    e = row.shape[1]
    ids = lax.broadcasted_iota(jnp.int32, (extent, e), 0)
    return jnp.where(ids == row, 1.0, 0.0).astype(BF16)


def build_kernel(per, cap, src_ref, rows_ref, cols_ref, feat_ref, sum_ref, adj_ref):
    step = pl.program_id(0)
    edges = rows_ref.shape[1]
    for o in range(per):
        counts = jnp.zeros((PAD, BS), F32)
        for c in range(cap):
            s = o * cap + c
            rt = one_hot_t(rows_ref[s : s + 1, :], BS)
            ct = one_hot_t(cols_ref[s : s + 1, :], BS)
            a = dot_nt(rt, ct).astype(BF16)
            adj_ref[s] = dot_nt(ct, rt).astype(BF16)
            x = feat_ref[src_ref[step * per * cap + s]]
            part = jnp.dot(a, x, preferred_element_type=F32)
            sum_ref[o, c * BS : (c + 1) * BS, :] = part.astype(BF16)
            pick = jnp.where(
                lax.broadcasted_iota(jnp.int32, (PAD, edges), 0) == c, 1.0, 0.0
            ).astype(BF16)
            counts = counts + dot_nt(pick, rt)
        sum_ref[o, cap * BS :, :] = counts.astype(BF16)


def build(src, rows, cols, feat, owners, cap):
    per = 4
    slots, edges = rows.shape
    local_blocks = feat.shape[0]
    return pl.pallas_call(
        functools.partial(build_kernel, per, cap),
        grid_spec=pltpu.PrefetchScalarGridSpec(
            num_scalar_prefetch=1,
            grid=(owners // per,),
            in_specs=[
                pl.BlockSpec((per * cap, edges), lambda i, s: (i, 0)),
                pl.BlockSpec((per * cap, edges), lambda i, s: (i, 0)),
                pl.BlockSpec((local_blocks, BS, BS), lambda i, s: (0, 0, 0)),
            ],
            out_specs=[
                pl.BlockSpec((per, cap * BS + PAD, BS), lambda i, s: (i, 0, 0)),
                pl.BlockSpec((per * cap, BS, BS), lambda i, s: (i, 0, 0)),
            ],
        ),
        out_shape=[
            jax.ShapeDtypeStruct((owners, cap * BS + PAD, BS), BF16),
            jax.ShapeDtypeStruct((slots, BS, BS), BF16),
        ],
        compiler_params=pltpu.CompilerParams(vmem_limit_bytes=VMEM_LIMIT),
        cost_estimate=pl.CostEstimate(
            flops=slots * 2 * BS * BS * (2 * edges + BS), bytes_accessed=10 << 20, transcendentals=0
        ),
        name="build",
    )(src, rows, cols, feat)


def gather_kernel(cap, tgt_ref, got_ref, sum_ref, cnt_ref, acc, acc_c):
    targets = sum_ref.shape[0]
    senders = got_ref.shape[0]

    def clear(i, carry):
        acc[i] = jnp.zeros((BS, BS), F32)
        return carry

    lax.fori_loop(0, targets, clear, 0, unroll=4)
    acc_c[...] = jnp.zeros_like(acc_c)

    def add(i, carry):
        for c in range(cap):
            t = tgt_ref[i * cap + c]

            @pl.when(t >= 0)
            def _():
                acc[t] += got_ref[i, c * BS : (c + 1) * BS, :].astype(F32)
                tail = got_ref[i, cap * BS :, :].astype(F32)
                acc_c[pl.ds(t, 1), :] += tail[c : c + 1, :]

        return carry

    lax.fori_loop(0, senders, add, 0)

    def store(i, carry):
        sum_ref[i] = acc[i].astype(BF16)
        return carry

    lax.fori_loop(0, targets, store, 0, unroll=4)
    cnt_ref[...] = acc_c[...]


def gather_sums(tgt, got, targets, cap):
    return pl.pallas_call(
        functools.partial(gather_kernel, cap),
        in_specs=[
            pl.BlockSpec(memory_space=pltpu.SMEM),
            pl.BlockSpec(memory_space=pltpu.VMEM),
        ],
        out_specs=[pl.BlockSpec(memory_space=pltpu.VMEM)] * 2,
        out_shape=[
            jax.ShapeDtypeStruct((targets, BS, BS), BF16),
            jax.ShapeDtypeStruct((targets, BS), F32),
        ],
        scratch_shapes=[pltpu.VMEM((targets, BS, BS), F32), pltpu.VMEM((targets, BS), F32)],
        compiler_params=pltpu.CompilerParams(vmem_limit_bytes=VMEM_LIMIT),
        cost_estimate=pl.CostEstimate(flops=targets * BS * BS, bytes_accessed=10 << 20, transcendentals=0),
        name="gather_sums",
    )(tgt, got)


def spread_kernel(per, src_ref, adj_ref, got_ref, own_ref, out_ref, acc):
    step = pl.program_id(0)

    @pl.when(step == 0)
    def _():
        acc[...] = own_ref[...]

    for s in range(per):
        b = src_ref[step * per + s]
        acc[b] += jnp.dot(adj_ref[s], got_ref[s], preferred_element_type=F32)

    @pl.when(step == pl.num_programs(0) - 1)
    def _():
        out_ref[...] = acc[...].astype(BF16)


def spread(src, adj, got, own):
    per = 16
    slots = adj.shape[0]
    blocks = own.shape[0]
    return pl.pallas_call(
        functools.partial(spread_kernel, per),
        grid_spec=pltpu.PrefetchScalarGridSpec(
            num_scalar_prefetch=1,
            grid=(slots // per,),
            in_specs=[
                pl.BlockSpec((per, BS, BS), lambda i, s: (i, 0, 0)),
                pl.BlockSpec((per, BS, BS), lambda i, s: (i, 0, 0)),
                pl.BlockSpec((blocks, BS, BS), lambda i, s: (0, 0, 0)),
            ],
            out_specs=pl.BlockSpec((blocks, BS, BS), lambda i, s: (0, 0, 0)),
            scratch_shapes=[pltpu.VMEM((blocks, BS, BS), F32)],
        ),
        out_shape=jax.ShapeDtypeStruct((blocks, BS, BS), BF16),
        compiler_params=pltpu.CompilerParams(vmem_limit_bytes=VMEM_LIMIT),
        cost_estimate=pl.CostEstimate(flops=slots * 2 * BS**3, bytes_accessed=10 << 20, transcendentals=0),
        name="spread",
    )(src, adj, got, own)


def on_device(
    features, w_self, w_neigh, cotangent, src_block, dst_block, block_count, edge_rows, edge_cols
):
    owners, cap = src_block.shape[1:]
    edges = edge_rows.shape[-1]
    slots = owners * cap
    local_nodes = features.shape[0]
    local_blocks = local_nodes // BS
    groups = lax.axis_size("grp")
    node_total = local_nodes * groups * owners
    in_use = lax.broadcasted_iota(jnp.int32, (owners, cap), 1) < block_count[0][:, None]
    src = src_block[0].reshape(slots)
    row_ids = jnp.where(in_use[..., None], edge_rows[0], BS).reshape(slots, edges)
    col_ids = jnp.where(in_use[..., None], edge_cols[0], BS).reshape(slots, edges)
    marked = jnp.where(in_use, dst_block[0], -1)
    got_dst = lax.all_to_all(marked, "blk", split_axis=0, concat_axis=0, tiled=True).reshape(slots)
    sums, adj = build(src, row_ids, col_ids, features.reshape(local_blocks, BS, -1), owners, cap)
    got = lax.all_to_all(sums, "blk", split_axis=0, concat_axis=0, tiled=True)
    acc, cnt = gather_sums(got_dst, got, groups * local_blocks, cap)
    own_sums = lax.psum_scatter(acc, "grp", scatter_dimension=0, tiled=True)
    got_cnt = lax.all_to_all(cnt, "grp", split_axis=0, concat_axis=0, tiled=True)
    own_cnt = jnp.sum(got_cnt.reshape(groups, local_blocks, BS), axis=0)
    divisor = jnp.maximum(own_cnt, 1.0).reshape(local_nodes, 1)
    neigh_mean = (own_sums.astype(F32).reshape(local_nodes, -1) / divisor).astype(BF16)
    preact = jnp.dot(features, w_self, preferred_element_type=F32) + jnp.dot(
        neigh_mean, w_neigh, preferred_element_type=F32
    )
    sigmoids = jax.nn.sigmoid(preact)
    activated = (preact * sigmoids).astype(BF16)
    grad_pre = (cotangent.astype(F32) * sigmoids * (1.0 + preact * (1.0 - sigmoids))).astype(BF16)
    grad_mean = (
        jnp.einsum("nh,fh->nf", grad_pre, w_neigh, preferred_element_type=F32) / divisor
    ).astype(BF16)
    mean_all = lax.all_gather(grad_mean.reshape(local_blocks, BS, -1), "grp", axis=0, tiled=True)
    slot_grads = mean_all[jnp.maximum(got_dst, 0)]
    returned = lax.all_to_all(
        slot_grads.reshape(owners, cap, BS, BS), "blk", split_axis=0, concat_axis=0, tiled=True
    )
    both = jnp.concatenate([features, neigh_mean], axis=1)
    grads = jnp.einsum("nf,nh->fh", both, grad_pre, preferred_element_type=F32)
    pieces = lax.all_to_all(grads, "blk", split_axis=0, concat_axis=0, tiled=True)
    piece = jnp.sum(pieces.reshape(owners, grads.shape[0] // owners, -1), axis=0)
    piece = jnp.sum(lax.all_gather(piece, "grp", axis=0, tiled=False), axis=0)
    grads = lax.all_gather(piece, "blk", axis=0, tiled=True) * float(node_total) ** (-0.5)
    own_term = jnp.einsum("nh,fh->nf", grad_pre, w_self, preferred_element_type=F32)
    grad_features = spread(
        src, adj, returned.reshape(slots, BS, BS), own_term.reshape(local_blocks, BS, -1)
    ).reshape(local_nodes, -1)
    f = features.shape[1]
    return (activated, grad_features, grads[:f], grads[f:])


def solution(mesh):
    return jax.shard_map(
        on_device,
        mesh=mesh,
        in_specs=(
            P(("grp", "blk"), None),
            P(),
            P(),
            P(("grp", "blk"), None),
            P(("grp", "blk"), None, None),
            P(("grp", "blk"), None, None),
            P(("grp", "blk"), None),
            P(("grp", "blk"), None, None, None),
            P(("grp", "blk"), None, None, None),
        ),
        out_specs=(P(("grp", "blk"), None), P(("grp", "blk"), None), P(), P()),
        check_vma=False,
    )
```

```python
import functools

import jax
import jax.numpy as jnp
from jax import lax
from jax.experimental import pallas as pl
from jax.experimental.pallas import tpu as pltpu
from jax.sharding import Mesh, PartitionSpec as P

BS = 128
TAIL = 16
Y, C, Z, X = 4, 2, 8, 4
F32 = jnp.float32
BF16 = jnp.bfloat16
VMEM_LIMIT = 48 * 1024 * 1024
NT = (((1,), (1,)), ((), ()))
SMEM_SPEC = pl.BlockSpec(memory_space=pltpu.SMEM)
VMEM_SPEC = pl.BlockSpec(memory_space=pltpu.VMEM)
PARAMS = pltpu.CompilerParams(vmem_limit_bytes=VMEM_LIMIT)


def dot_nt(a, b):
    return lax.dot_general(a, b, NT, preferred_element_type=F32)


def cost(us):
    return pl.CostEstimate(flops=0, bytes_accessed=int(us * 3.5e6), transcendentals=0)


def one_hot_t(row, extent):
    ids = lax.broadcasted_iota(jnp.int32, (extent, row.shape[1]), 0)
    return jnp.where(ids == row, 1.0, 0.0).astype(BF16)


def build_kernel(offsets, cap, edges, src_ref, pos_ref, edge_ref, *refs):
    n = len(offsets)
    feats, outs, adj_ref = refs[:n], refs[n : n + X], refs[n + X]
    z, x = pos_ref[0], pos_ref[1]
    for dx in range(X):
        owner = lax.rem(x + dx, X)
        counts = jnp.zeros((TAIL, BS), F32)
        for j, off in enumerate(offsets):
            sender = lax.rem(z + off + Z, Z)
            packed = edge_ref[sender * X + owner]
            for c in range(cap):
                k = j * cap + c
                e = packed[c : c + 1, :edges]
                rt = one_hot_t(lax.shift_right_logical(e, 7), BS)
                ct = one_hot_t(jnp.bitwise_and(e, BS - 1), BS)
                a = dot_nt(rt, ct).astype(BF16)
                adj_ref[j, dx, c] = dot_nt(ct, rt).astype(BF16)
                src = src_ref[(sender * X + owner) * cap + c]
                part = jnp.dot(a, feats[j][src], preferred_element_type=F32)
                outs[dx][k * BS : (k + 1) * BS, :] = part.astype(BF16)
                pick = jnp.where(
                    lax.broadcasted_iota(jnp.int32, (TAIL, edges), 0) == k, 1.0, 0.0
                ).astype(BF16)
                counts = counts + dot_nt(pick, rt)
        outs[dx][n * cap * BS :, :] = counts.astype(BF16)


def build(offsets, cap, edges, src, pos, edge_list, feats):
    n = len(offsets)
    rows = n * cap * BS + TAIL
    return pl.pallas_call(
        functools.partial(build_kernel, offsets, cap, edges),
        in_specs=[SMEM_SPEC, SMEM_SPEC] + [VMEM_SPEC] * (1 + n),
        out_specs=[VMEM_SPEC] * (X + 1),
        out_shape=[jax.ShapeDtypeStruct((rows, BS), BF16)] * X
        + [jax.ShapeDtypeStruct((n, X, cap, BS, BS), BF16)],
        compiler_params=PARAMS,
        cost_estimate=cost(2.5 * n),
        name="build",
    )(src, pos, edge_list, *feats)


def gather_kernel(batches, cap, tgt_ref, pos_ref, *refs):
    total = len(batches) * X
    got, (sum_ref, cnt_ref, acc, acc_c) = refs[:total], refs[total:]
    targets = sum_ref.shape[0]
    z, x = pos_ref[0], pos_ref[1]

    def clear(i, carry):
        acc[i] = jnp.zeros((BS, BS), F32)
        return carry

    lax.fori_loop(0, targets, clear, 0, unroll=4)
    acc_c[...] = jnp.zeros_like(acc_c)
    for b, offsets in enumerate(batches):
        for dx in range(X):
            ref = got[b * X + dx]
            sender_x = lax.rem(x - dx + X, X)
            tail = ref[len(offsets) * cap * BS :, :].astype(F32)
            for j, off in enumerate(offsets):
                sender_z = lax.rem(z + off + Z, Z)
                for c in range(cap):
                    k = j * cap + c
                    t = tgt_ref[(sender_x * Z + sender_z) * cap + c]

                    @pl.when(t >= 0)
                    def _():
                        acc[t] += ref[k * BS : (k + 1) * BS, :].astype(F32)
                        acc_c[pl.ds(t, 1), :] += tail[k : k + 1, :]

    def store(i, carry):
        sum_ref[i] = acc[i].astype(BF16)
        return carry

    lax.fori_loop(0, targets, store, 0, unroll=4)
    cnt_ref[...] = acc_c[...]


def gather_sums(batches, cap, targets, tgt, pos, got):
    return pl.pallas_call(
        functools.partial(gather_kernel, batches, cap),
        in_specs=[SMEM_SPEC, SMEM_SPEC] + [VMEM_SPEC] * len(got),
        out_specs=[VMEM_SPEC] * 2,
        out_shape=[
            jax.ShapeDtypeStruct((targets, BS, BS), BF16),
            jax.ShapeDtypeStruct((targets, BS), F32),
        ],
        scratch_shapes=[pltpu.VMEM((targets, BS, BS), F32), pltpu.VMEM((targets, BS), F32)],
        compiler_params=PARAMS,
        cost_estimate=cost(6),
        name="gather_sums",
    )(tgt, pos, *got)


def pick_kernel(offsets, cap, tgt_ref, pos_ref, mean_ref, *outs):
    z, x = pos_ref[0], pos_ref[1]
    for dx in range(X):
        sender_x = lax.rem(x - dx + X, X)
        for j, off in enumerate(offsets):
            sender_z = lax.rem(z + off + Z, Z)
            for c in range(cap):
                t = tgt_ref[(sender_x * Z + sender_z) * cap + c]
                outs[dx][j * cap + c] = mean_ref[jnp.maximum(t, 0)]


def pick(offsets, cap, tgt, pos, mean_all):
    n = len(offsets)
    return pl.pallas_call(
        functools.partial(pick_kernel, offsets, cap),
        in_specs=[SMEM_SPEC, SMEM_SPEC, VMEM_SPEC],
        out_specs=[VMEM_SPEC] * X,
        out_shape=[jax.ShapeDtypeStruct((n * cap, BS, BS), BF16)] * X,
        compiler_params=PARAMS,
        cost_estimate=cost(1.5),
        name="pick",
    )(tgt, pos, mean_all)


def spread_kernel(offsets, starts, cap, src_ref, pos_ref, adj_ref, *refs):
    n = len(offsets)
    got, refs = refs[:X], refs[X:]
    inits = []
    for parts in starts:
        inits.append([(lo, hi, refs[i]) for i, (lo, hi) in enumerate(parts)])
        refs = refs[len(parts) :]
    outs, acc = refs[:n], refs[n]
    blocks = acc.shape[0]
    z, x = pos_ref[0], pos_ref[1]
    for j, off in enumerate(offsets):
        covered = 0
        for i, (lo, hi, ref) in enumerate(inits[j]):
            if i == 0:
                if lo > 0:
                    acc[:lo] = jnp.zeros((lo, BS, BS), F32)
                acc[lo:hi] = ref[...].astype(F32)
                if hi < blocks:
                    acc[hi:] = jnp.zeros((blocks - hi, BS, BS), F32)
                covered = blocks
            else:
                acc[lo:hi] += ref[...].astype(F32)
        if covered == 0:
            acc[...] = jnp.zeros_like(acc)
        sender = lax.rem(z + off + Z, Z)
        for dx in range(X):
            owner = lax.rem(x + dx, X)
            for c in range(cap):
                src = src_ref[(sender * X + owner) * cap + c]
                acc[src] += jnp.dot(
                    adj_ref[j, dx, c], got[dx][j * cap + c], preferred_element_type=F32
                )
        outs[j][...] = acc[...].astype(BF16)


def spread(offsets, cap, blocks, src, pos, adj, got, starts):
    n = len(offsets)
    return pl.pallas_call(
        functools.partial(
            spread_kernel, offsets, [[(lo, hi) for lo, hi, _ in s] for s in starts], cap
        ),
        in_specs=[SMEM_SPEC, SMEM_SPEC] + [VMEM_SPEC] * (1 + X + sum(len(s) for s in starts)),
        out_specs=[VMEM_SPEC] * n,
        out_shape=[jax.ShapeDtypeStruct((blocks, BS, BS), BF16)] * n,
        scratch_shapes=[pltpu.VMEM((blocks, BS, BS), F32)],
        compiler_params=PARAMS,
        cost_estimate=cost(2.5 * n),
        name="spread",
    )(src, pos, adj, *got, *[a for s in starts for _, _, a in s])


def shift(value, axis, size, by):
    return lax.ppermute(value, axis, [(i, (i + by) % size) for i in range(size)])


def shift_x(values, sign):
    return [values[0]] + [shift(values[d], "x", X, sign * d) for d in range(1, X)]


def exchange(value, axes):
    return lax.all_to_all(value, axes, split_axis=0, concat_axis=0, tiled=True)


def on_device(
    features, w_self, w_neigh, cotangent, src_block, dst_block, block_count, edge_rows, edge_cols
):
    owners, cap = src_block.shape[1:]
    edges = edge_rows.shape[-1]
    local_nodes = features.shape[0]
    blocks = local_nodes // BS
    half = blocks // 2
    groups = Y * C
    node_total = local_nodes * groups * owners
    pos = jnp.stack([lax.axis_index("z"), lax.axis_index("x")]).astype(jnp.int32)
    feats = features.reshape(blocks, BS, -1)

    in_use = lax.broadcasted_iota(jnp.int32, (owners, cap), 1) < block_count[0][:, None]
    packed = jnp.where(in_use[..., None], edge_rows[0] * BS + edge_cols[0], BS * BS)
    marked = jnp.where(in_use, dst_block[0], -1)
    sent = jnp.concatenate(
        [
            packed,
            src_block[0][..., None],
            marked[..., None],
            jnp.zeros((owners, cap, 62), jnp.int32),
        ],
        axis=-1,
    )
    lists = exchange(sent, "z")
    src = lists[:, :, edges].reshape(owners * cap)
    tgt = lists[:, :, edges + 1].reshape(Z, X, cap).transpose(1, 0, 2)
    tgt = exchange(tgt, "x").reshape(owners * cap)

    batches = [(0,), (-1, 1), (-2, 2), (-3, 3), (4,)]
    sums, adjs = [], []

    def batch(k, srcs, edge_list, arrays):
        *out, adj = build(batches[k], cap, edges, srcs, pos, edge_list, arrays)
        sums.extend(shift_x(out, 1))
        adjs.append(adj)

    up, down = feats, feats
    for k in range(1, 4):
        up, down = shift(up, "z", Z, 1), shift(down, "z", Z, -1)
        if k == 1:
            batch(0, src_block[0].reshape(owners * cap), sent, [feats])
        batch(k, src, lists, [up, down])
    far = jnp.concatenate([shift(up[:half], "z", Z, 1), shift(down[half:], "z", Z, -1)])
    batch(4, src, lists, [far])
    acc, cnt = gather_sums(batches, cap, groups * blocks, tgt, pos, sums)

    own_sums = lax.psum_scatter(acc, ("y", "c"), scatter_dimension=0, tiled=True)
    got_cnt = exchange(cnt, ("y", "c"))
    own_cnt = jnp.sum(got_cnt.reshape(groups, blocks, BS), axis=0)
    divisor = jnp.maximum(own_cnt, 1.0).reshape(local_nodes, 1)
    neigh_mean = (own_sums.astype(F32).reshape(local_nodes, -1) / divisor).astype(BF16)
    preact = jnp.dot(features, w_self, preferred_element_type=F32) + jnp.dot(
        neigh_mean, w_neigh, preferred_element_type=F32
    )
    sigmoids = jax.nn.sigmoid(preact)
    activated = (preact * sigmoids).astype(BF16)
    grad_pre = (cotangent.astype(F32) * sigmoids * (1.0 + preact * (1.0 - sigmoids))).astype(BF16)
    grad_mean = (
        jnp.einsum("nh,fh->nf", grad_pre, w_neigh, preferred_element_type=F32) / divisor
    ).astype(BF16)
    mean_all = lax.all_gather(grad_mean.reshape(blocks, BS, -1), ("y", "c"), axis=0, tiled=True)

    both = jnp.concatenate([features, neigh_mean], axis=1)
    grads = jnp.einsum("nf,nh->fh", both, grad_pre, preferred_element_type=F32)
    rows = grads.shape[0] // owners
    piece = jnp.sum(exchange(grads, ("z", "x")).reshape(owners, rows, -1), axis=0)
    piece = jnp.broadcast_to(piece[None], (groups, rows, piece.shape[1]))
    piece = jnp.sum(exchange(piece, ("y", "c")), axis=0)
    grads = exchange(jnp.broadcast_to(piece[None], (owners, rows, piece.shape[1])), ("z", "x"))
    grads = grads.reshape(owners * rows, -1) * float(node_total) ** (-0.5)

    own_term = jnp.einsum("nh,fh->nf", grad_pre, w_self, preferred_element_type=F32)
    own_term = own_term.reshape(blocks, BS, -1)

    def back(k, starts, srcs=src):
        got = shift_x(pick(batches[k], cap, tgt, pos, mean_all), -1)
        return spread(batches[k], cap, blocks, srcs, pos, adjs[k], got, starts)

    (far,) = back(4, [[]])
    up, down = shift(far[:half], "z", Z, 1), shift(far[half:], "z", Z, -1)
    down, up = back(3, [[(half, blocks, down)], [(0, half, up)]])
    for k in (2, 1):
        up, down = shift(up, "z", Z, 1), shift(down, "z", Z, -1)
        down, up = back(k, [[(0, blocks, down)], [(0, blocks, up)]])
    up, down = shift(up, "z", Z, 1), shift(down, "z", Z, -1)
    (grad_features,) = back(0, [[(0, blocks, own_term), (0, blocks, up), (0, blocks, down)]])
    f = features.shape[1]
    return activated, grad_features.reshape(local_nodes, -1), grads[:f], grads[f:]


def solution(mesh):
    mesh = Mesh(mesh.devices.reshape(Y, C, Z, X), ("y", "c", "z", "x"))
    every = ("y", "c", "z", "x")
    return jax.shard_map(
        on_device,
        mesh=mesh,
        in_specs=(
            P(every, None),
            P(),
            P(),
            P(every, None),
            P(every, None, None),
            P(every, None, None),
            P(every, None),
            P(every, None, None, None),
            P(every, None, None, None),
        ),
        out_specs=(P(every, None), P(every, None), P(), P()),
        check_vma=False,
    )
```

```python
import functools

import jax
import jax.numpy as jnp
from jax import lax
from jax.experimental import pallas as pl
from jax.experimental.pallas import tpu as pltpu
from jax.sharding import Mesh, PartitionSpec as P

BS = 128
TAIL = 16
Y, C, Z, X = 4, 2, 8, 4
F32 = jnp.float32
BF16 = jnp.bfloat16
MIB = 1024 * 1024
NT = (((1,), (1,)), ((), ()))
SMEM_SPEC = pl.BlockSpec(memory_space=pltpu.SMEM)
VMEM_SPEC = pl.BlockSpec(memory_space=pltpu.VMEM)
ANY_SPEC = pl.BlockSpec(memory_space=pl.ANY)
LISTS = 256


def dot_nt(a, b):
    return lax.dot_general(a, b, NT, preferred_element_type=F32)


def params(mib):
    return pltpu.CompilerParams(vmem_limit_bytes=mib * MIB)


def cost(us):
    return pl.CostEstimate(flops=0, bytes_accessed=int(us * 3.5e6), transcendentals=0)


def one_hot_t(row, extent):
    ids = lax.broadcasted_iota(jnp.int32, (extent, row.shape[1]), 0)
    return jnp.where(ids == row, 1.0, 0.0).astype(BF16)


def build_batch(offsets, cap, edges, src_of, z, x, edge_ref, feats, outs, adj_ref):
    n = len(offsets)
    for dx in range(X):
        owner = lax.rem(x + dx, X)
        counts = jnp.zeros((TAIL, BS), F32)
        for j, off in enumerate(offsets):
            sender = lax.rem(z + off + Z, Z)
            packed = edge_ref[sender * X + owner]
            for c in range(cap):
                k = j * cap + c
                e = packed[c : c + 1, :edges]
                rt = one_hot_t(lax.shift_right_logical(e, 7), BS)
                ct = one_hot_t(jnp.bitwise_and(e, BS - 1), BS)
                a = dot_nt(rt, ct).astype(BF16)
                adj_ref[j, dx, c] = dot_nt(ct, rt).astype(BF16)
                src = src_of(sender * X + owner, c)
                part = jnp.dot(a, feats[j][src], preferred_element_type=F32)
                outs[dx][k * BS : (k + 1) * BS, :] = part.astype(BF16)
                pick = jnp.where(
                    lax.broadcasted_iota(jnp.int32, (TAIL, edges), 0) == k, 1.0, 0.0
                ).astype(BF16)
                counts = counts + dot_nt(pick, rt)
        outs[dx][n * cap * BS :, :] = counts.astype(BF16)


def batch_shapes(n, cap):
    return [jax.ShapeDtypeStruct((n * cap * BS + TAIL, BS), BF16)] * X + [
        jax.ShapeDtypeStruct((n, X, cap, BS, BS), BF16)
    ]


def head_kernel(
    cap, edges, src_ref, dst_ref, used_ref, pos_ref, rows_ref, cols_ref, feat_ref, lists_ref, *refs
):
    owners = rows_ref.shape[1]
    slot = lax.broadcasted_iota(jnp.int32, (cap, edges), 0)
    rest = LISTS - edges
    meta_slot = lax.broadcasted_iota(jnp.int32, (cap, rest), 0)
    meta_lane = lax.broadcasted_iota(jnp.int32, (cap, rest), 1)

    def pack(o, carry):
        used = used_ref[0, o]
        packed = rows_ref[0, o] * BS + cols_ref[0, o]
        lists_ref[o, :, :edges] = jnp.where(slot < used, packed, BS * BS)
        meta = jnp.zeros((cap, rest), jnp.int32)
        for c in range(cap):
            to = jnp.where(c < used, dst_ref[0, o, c], -1)
            value = jnp.where(meta_lane == 0, src_ref[0, o, c], to)
            meta = jnp.where(meta_slot == c, value, meta)
        lists_ref[o, :, edges:] = meta
        return carry

    lax.fori_loop(0, owners, pack, 0, unroll=2)
    z, x = pos_ref[0], pos_ref[1]
    build_batch(
        (0,), cap, edges, lambda o, c: src_ref[0, o, c], z, x, lists_ref, [feat_ref], refs[:X], refs[X]
    )


def head(src, dst, used, pos, rows, cols, feats):
    owners, cap, edges = rows.shape[1:]
    return pl.pallas_call(
        functools.partial(head_kernel, cap, edges),
        in_specs=[SMEM_SPEC] * 4 + [VMEM_SPEC] * 3,
        out_specs=[VMEM_SPEC] * (X + 2),
        out_shape=[jax.ShapeDtypeStruct((owners, cap, LISTS), jnp.int32)] + batch_shapes(1, cap),
        compiler_params=params(8),
        cost_estimate=cost(5),
        name="head",
    )(src, dst, used, pos, rows, cols, feats)


def build_kernel(offsets, cap, edges, after, src_ref, pos_ref, edge_ref, *refs):
    n = len(offsets)
    feats, refs = refs[:n], refs[n + after :]
    build_batch(
        offsets,
        cap,
        edges,
        lambda o, c: src_ref[o * cap + c],
        pos_ref[0],
        pos_ref[1],
        edge_ref,
        feats,
        refs[:X],
        refs[X],
    )


def build(offsets, cap, edges, src, pos, edge_list, feats, after):
    n = len(offsets)
    return pl.pallas_call(
        functools.partial(build_kernel, offsets, cap, edges, len(after)),
        in_specs=[SMEM_SPEC, SMEM_SPEC] + [VMEM_SPEC] * (1 + n) + [ANY_SPEC] * len(after),
        out_specs=[VMEM_SPEC] * (X + 1),
        out_shape=batch_shapes(n, cap),
        compiler_params=params(8),
        cost_estimate=cost(2.5 * n),
        name="build",
    )(src, pos, edge_list, *feats, *after)


def follow(arrays, after):
    n = len(arrays)
    return pl.pallas_call(
        lambda *refs: None,
        in_specs=[ANY_SPEC] * (n + 1),
        out_specs=[ANY_SPEC] * n,
        out_shape=[jax.ShapeDtypeStruct(a.shape, a.dtype) for a in arrays],
        input_output_aliases={i: i for i in range(n)},
        compiler_params=params(1),
        cost_estimate=cost(0.3),
        name="follow",
    )(*arrays, after)


def gather_kernel(batches, cap, pos_ref, *refs):
    total = len(batches) * X
    tgts, refs = refs[:X], refs[X:]
    got, (sum_ref, cnt_ref, acc, acc_c) = refs[:total], refs[total:]
    targets = sum_ref.shape[0]
    z, x = pos_ref[0], pos_ref[1]

    def clear(i, carry):
        acc[i] = jnp.zeros((BS, BS), F32)
        return carry

    lax.fori_loop(0, targets, clear, 0, unroll=4)
    acc_c[...] = jnp.zeros_like(acc_c)
    for b, offsets in enumerate(batches):
        for dx in range(X):
            ref = got[b * X + dx]
            tail = ref[len(offsets) * cap * BS :, :].astype(F32)
            for j, off in enumerate(offsets):
                sender_z = lax.rem(z + off + Z, Z)
                for c in range(cap):
                    k = j * cap + c
                    t = tgts[dx][(sender_z * X + x) * cap + c]

                    @pl.when(t >= 0)
                    def _():
                        acc[t] += ref[k * BS : (k + 1) * BS, :].astype(F32)
                        acc_c[pl.ds(t, 1), :] += tail[k : k + 1, :]

    def store(i, carry):
        sum_ref[i] = acc[i].astype(BF16)
        return carry

    lax.fori_loop(0, targets, store, 0, unroll=4)
    cnt_ref[...] = acc_c[...]


def gather_sums(batches, cap, targets, tgts, pos, got):
    return pl.pallas_call(
        functools.partial(gather_kernel, batches, cap),
        in_specs=[SMEM_SPEC] * (1 + X) + [VMEM_SPEC] * len(got),
        out_specs=[VMEM_SPEC] * 2,
        out_shape=[
            jax.ShapeDtypeStruct((targets, BS, BS), BF16),
            jax.ShapeDtypeStruct((targets, BS), F32),
        ],
        scratch_shapes=[pltpu.VMEM((targets, BS, BS), F32), pltpu.VMEM((targets, BS), F32)],
        compiler_params=params(20),
        cost_estimate=cost(6),
        name="gather_sums",
    )(pos, *tgts, *got)


def pick_kernel(sets, cap, pos_ref, *refs):
    tgts, mean_ref, outs = refs[:X], refs[X], refs[X + 2 :]
    z, x = pos_ref[0], pos_ref[1]
    for i, offsets in enumerate(sets):
        for dx in range(X):
            for j, off in enumerate(offsets):
                sender_z = lax.rem(z + off + Z, Z)
                for c in range(cap):
                    t = tgts[dx][(sender_z * X + x) * cap + c]
                    outs[i * X + dx][j * cap + c] = mean_ref[jnp.maximum(t, 0)]


def pick(sets, cap, tgts, pos, mean_all, after):
    shapes = []
    for offsets in sets:
        shapes += [jax.ShapeDtypeStruct((len(offsets) * cap, BS, BS), BF16)] * X
    out = pl.pallas_call(
        functools.partial(pick_kernel, sets, cap),
        in_specs=[SMEM_SPEC] * (1 + X) + [VMEM_SPEC, ANY_SPEC],
        out_specs=[VMEM_SPEC] * len(shapes),
        out_shape=shapes,
        compiler_params=params(8),
        cost_estimate=cost(3),
        name="pick",
    )(pos, *tgts, mean_all, after)
    return [out[i * X : (i + 1) * X] for i in range(len(sets))]


def spread_kernel(offsets, starts, cap, base, src_ref, pos_ref, adj_ref, *refs):
    n = len(offsets)
    got, refs = refs[:X], refs[X:]
    inits = []
    for parts in starts:
        inits.append([(lo, hi, refs[i]) for i, (lo, hi) in enumerate(parts)])
        refs = refs[len(parts) :]
    outs, acc = refs[:n], refs[n]
    blocks = acc.shape[0]
    z, x = pos_ref[0], pos_ref[1]
    for j, off in enumerate(offsets):
        covered = 0
        for i, (lo, hi, ref) in enumerate(inits[j]):
            if i == 0:
                if lo > 0:
                    acc[:lo] = jnp.zeros((lo, BS, BS), F32)
                acc[lo:hi] = ref[...].astype(F32)
                if hi < blocks:
                    acc[hi:] = jnp.zeros((blocks - hi, BS, BS), F32)
                covered = blocks
            else:
                acc[lo:hi] += ref[...].astype(F32)
        if covered == 0:
            acc[...] = jnp.zeros_like(acc)
        sender = lax.rem(z + off + Z, Z)
        for dx in range(X):
            owner = lax.rem(x + dx, X)
            for c in range(cap):
                src = src_ref[(sender * X + owner) * cap + c]
                acc[src] += jnp.dot(
                    adj_ref[j, dx, c], got[dx][base + j * cap + c], preferred_element_type=F32
                )
        outs[j][...] = acc[...].astype(BF16)


def spread(offsets, cap, base, blocks, src, pos, adj, got, starts):
    n = len(offsets)
    return pl.pallas_call(
        functools.partial(
            spread_kernel, offsets, [[(lo, hi) for lo, hi, _ in s] for s in starts], cap, base
        ),
        in_specs=[SMEM_SPEC, SMEM_SPEC] + [VMEM_SPEC] * (1 + X + sum(len(s) for s in starts)),
        out_specs=[VMEM_SPEC] * n,
        out_shape=[jax.ShapeDtypeStruct((blocks, BS, BS), BF16)] * n,
        scratch_shapes=[pltpu.VMEM((blocks, BS, BS), F32)],
        compiler_params=params(8),
        cost_estimate=cost(1.2 * n),
        name="spread",
    )(src, pos, adj, *got, *[a for s in starts for _, _, a in s])


def shift(value, axis, size, by):
    return lax.ppermute(value, axis, [(i, (i + by) % size) for i in range(size)])


def shift_x(values, sign):
    return [values[0]] + [shift(values[d], "x", X, sign * d) for d in range(1, X)]


def exchange(value, axes):
    return lax.all_to_all(value, axes, split_axis=0, concat_axis=0, tiled=True)


def on_device(
    features, w_self, w_neigh, cotangent, src_block, dst_block, block_count, edge_rows, edge_cols
):
    owners, cap = src_block.shape[1:]
    edges = edge_rows.shape[-1]
    local_nodes = features.shape[0]
    blocks = local_nodes // BS
    half = blocks // 2
    groups = Y * C
    node_total = local_nodes * groups * owners
    pos = jnp.stack([lax.axis_index("z"), lax.axis_index("x")]).astype(jnp.int32)
    feats = features.reshape(blocks, BS, -1)

    sent, *own = head(src_block, dst_block, block_count, pos, edge_rows, edge_cols, feats)
    lists = exchange(sent, "z")
    src = lists[:, :, edges].reshape(owners * cap)
    tgt = lists[:, :, edges + 1].reshape(owners * cap)
    tgts = shift_x([tgt] * X, 1)

    batches = [(0,), (-1, 1), (-2, 2), (-3, 3), (4,)]
    sums, adjs = [shift_x(own[:X], 1)], [own[X]]
    up, down, last = feats, feats, own[0]
    for k in range(1, 5):
        if k < 4:
            up, down = follow([shift(up, "z", Z, 1), shift(down, "z", Z, -1)], last)
            arrays = [up, down]
        else:
            up, down = shift(up[:half], "z", Z, 1), shift(down[half:], "z", Z, -1)
            arrays = [jnp.concatenate([up, down])]
        *out, adj = build(
            batches[k], cap, edges, src, pos, lists, arrays, sums[max(k - 2, 0)][1:]
        )
        sums.append(shift_x(out, 1))
        adjs.append(adj)
        last = out[0]
    acc, cnt = gather_sums(batches, cap, groups * blocks, tgts, pos, sum(sums, []))

    own_sums = lax.psum_scatter(acc, ("y", "c"), scatter_dimension=0, tiled=True)
    got_cnt = exchange(cnt, ("y", "c"))
    own_cnt = jnp.sum(got_cnt.reshape(groups, blocks, BS), axis=0)
    divisor = jnp.maximum(own_cnt, 1.0).reshape(local_nodes, 1)
    neigh_mean = (own_sums.astype(F32).reshape(local_nodes, -1) / divisor).astype(BF16)
    preact = jnp.dot(features, w_self, preferred_element_type=F32) + jnp.dot(
        neigh_mean, w_neigh, preferred_element_type=F32
    )
    sigmoids = jax.nn.sigmoid(preact)
    activated = (preact * sigmoids).astype(BF16)
    grad_pre = (cotangent.astype(F32) * sigmoids * (1.0 + preact * (1.0 - sigmoids))).astype(BF16)
    grad_mean = (
        jnp.einsum("nh,fh->nf", grad_pre, w_neigh, preferred_element_type=F32) / divisor
    ).astype(BF16)
    mean_all = lax.all_gather(grad_mean.reshape(blocks, BS, -1), ("y", "c"), axis=0, tiled=True)

    both = jnp.concatenate([features, neigh_mean], axis=1)
    grads = jnp.einsum("nf,nh->fh", both, grad_pre, preferred_element_type=F32)
    rows = grads.shape[0] // owners
    piece = jnp.sum(exchange(grads, ("z", "x")).reshape(owners, rows, -1), axis=0)
    piece = jnp.broadcast_to(piece[None], (groups, rows, piece.shape[1]))
    piece = jnp.sum(exchange(piece, ("y", "c")), axis=0)
    sets = [(4,), (-3, 3), (-2, 2), (-1, 1, 0)]
    picked = pick(sets, cap, tgts, pos, mean_all, piece)
    grads = exchange(jnp.broadcast_to(piece[None], (owners, rows, piece.shape[1])), ("z", "x"))
    grads = grads.reshape(owners * rows, -1) * float(node_total) ** (-0.5)

    own_term = jnp.einsum("nh,fh->nf", grad_pre, w_self, preferred_element_type=F32)
    own_term = own_term.reshape(blocks, BS, -1)

    got = [shift_x(p, -1) for p in picked]

    def back(k, starts):
        i, base = (3, 2 * cap) if k == 0 else (4 - k, 0)
        return spread(batches[k], cap, base, blocks, src, pos, adjs[k], got[i], starts)

    (far,) = back(4, [[]])
    up, down = shift(far[:half], "z", Z, 1), shift(far[half:], "z", Z, -1)
    down, up = back(3, [[(half, blocks, down)], [(0, half, up)]])
    for k in (2, 1):
        up, down = shift(up, "z", Z, 1), shift(down, "z", Z, -1)
        down, up = back(k, [[(0, blocks, down)], [(0, blocks, up)]])
    up, down = shift(up, "z", Z, 1), shift(down, "z", Z, -1)
    (grad_features,) = back(0, [[(0, blocks, own_term), (0, blocks, up), (0, blocks, down)]])
    f = features.shape[1]
    return activated, grad_features.reshape(local_nodes, -1), grads[:f], grads[f:]


def solution(mesh):
    mesh = Mesh(mesh.devices.reshape(Y, C, Z, X), ("y", "c", "z", "x"))
    every = ("y", "c", "z", "x")
    return jax.shard_map(
        on_device,
        mesh=mesh,
        in_specs=(
            P(every, None),
            P(),
            P(),
            P(every, None),
            P(every, None, None),
            P(every, None, None),
            P(every, None),
            P(every, None, None, None),
            P(every, None, None, None),
        ),
        out_specs=(P(every, None), P(every, None), P(), P()),
        check_vma=False,
    )
```

```python
import functools

import jax
import jax.numpy as jnp
from jax import lax
from jax.experimental import pallas as pl
from jax.experimental.pallas import tpu as pltpu
from jax.sharding import Mesh, PartitionSpec as P

BS = 128
TAIL = 16
Y, C, Z, X = 4, 2, 8, 4
F32 = jnp.float32
BF16 = jnp.bfloat16
MIB = 1024 * 1024
NT = (((1,), (1,)), ((), ()))
SMEM_SPEC = pl.BlockSpec(memory_space=pltpu.SMEM)
VMEM_SPEC = pl.BlockSpec(memory_space=pltpu.VMEM)
ANY_SPEC = pl.BlockSpec(memory_space=pl.ANY)
LISTS = 256


def dot_nt(a, b):
    return lax.dot_general(a, b, NT, preferred_element_type=F32)


def params(mib):
    return pltpu.CompilerParams(vmem_limit_bytes=mib * MIB)


def cost(us):
    return pl.CostEstimate(flops=0, bytes_accessed=int(us * 3.5e6), transcendentals=0)


def one_hot_t(row, extent):
    ids = lax.broadcasted_iota(jnp.int32, (extent, row.shape[1]), 0)
    return jnp.where(ids == row, 1.0, 0.0).astype(BF16)


def build_batch(offsets, cap, edges, src_of, z, x, edge_ref, feats, sum_refs, adj_ref, tgt_ref=None):
    n = len(offsets)

    def owner_step(dx, carry):
        owner = lax.rem(x + dx, X)
        counts = jnp.zeros((TAIL, BS), F32)
        if tgt_ref is not None:
            last = lax.broadcasted_iota(jnp.int32, (TAIL, BS), 0) == TAIL - 1
            counts = jnp.where(last, tgt_ref[...].astype(F32), 0.0)
        parts = []
        for j, off in enumerate(offsets):
            row = lax.rem(z + off + Z, Z) * X + owner
            packed = edge_ref[row]
            for c in range(cap):
                k = j * cap + c
                e = packed[c : c + 1, :edges]
                rt = one_hot_t(lax.shift_right_logical(e, 7), BS)
                ct = one_hot_t(jnp.bitwise_and(e, BS - 1), BS)
                a = dot_nt(rt, ct).astype(BF16)
                adj_ref[j, dx, c] = dot_nt(ct, rt).astype(BF16)
                part = jnp.dot(a, feats[j][src_of(row, c)], preferred_element_type=F32)
                parts.append(part.astype(BF16))
                pick = jnp.where(
                    lax.broadcasted_iota(jnp.int32, (TAIL, edges), 0) == k, 1.0, 0.0
                ).astype(BF16)
                counts = counts + dot_nt(pick, rt)
        parts.append(counts.astype(BF16))
        for d, out in enumerate(sum_refs):

            @pl.when(dx == d)
            def _(out=out):
                for k, part in enumerate(parts):
                    out[k * BS : k * BS + part.shape[0], :] = part

        return carry

    lax.fori_loop(0, X, owner_step, 0)


def batch_shapes(n, cap):
    return [jax.ShapeDtypeStruct((n * cap * BS + TAIL, BS), BF16)] * X + [
        jax.ShapeDtypeStruct((n, X, cap, BS, BS), BF16)
    ]


def pack_kernel(cap, edges, src_ref, dst_ref, used_ref, rows_ref, cols_ref, lists_ref):
    owners = rows_ref.shape[1]
    rest = LISTS - edges
    meta_slot = lax.broadcasted_iota(jnp.int32, (cap, rest), 0)
    meta_lane = lax.broadcasted_iota(jnp.int32, (cap, rest), 1)
    slot = lax.broadcasted_iota(jnp.int32, (cap, edges), 0)

    def pack(o, carry):
        packed = rows_ref[0, o] * BS + cols_ref[0, o]
        meta = jnp.zeros((cap, rest), jnp.int32)
        for c in range(cap):
            to = jnp.where(c < used_ref[0, o], dst_ref[c, o], -1)
            packed = jnp.where(jnp.logical_and(slot == c, to < 0), BS * BS, packed)
            value = jnp.where(meta_lane == 0, src_ref[c, o], to)
            meta = jnp.where(meta_slot == c, value, meta)
        lists_ref[o, :, :edges] = packed
        lists_ref[o, :, edges:] = meta
        return carry

    lax.fori_loop(0, owners, pack, 0, unroll=4)


def pack(src, dst, used, rows, cols):
    owners, cap, edges = rows.shape[1:]
    whole = pl.BlockSpec(rows.shape, lambda i: (0, 0, 0, 0))
    return pl.pallas_call(
        functools.partial(pack_kernel, cap, edges),
        grid=(1,),
        in_specs=[SMEM_SPEC] * 3 + [whole] * 2,
        out_specs=VMEM_SPEC,
        out_shape=jax.ShapeDtypeStruct((owners, cap, LISTS), jnp.int32),
        compiler_params=params(4),
        cost_estimate=cost(2),
        name="pack",
    )(src, dst, used, rows, cols)


def build_kernel(offsets, cap, edges, own, extra, after, src_ref, pos_ref, edge_ref, *refs):
    n = len(offsets)
    feats, refs = refs[:n], refs[n:]
    tgt_ref = refs[0] if extra else None
    refs = refs[extra + after :]

    def src_of(row, c):
        if own:
            return src_ref[c, row]
        return src_ref[row * cap + c]

    build_batch(
        offsets,
        cap,
        edges,
        src_of,
        pos_ref[0],
        pos_ref[1],
        edge_ref,
        feats,
        refs[:X],
        refs[X],
        tgt_ref,
    )


def build(offsets, cap, edges, src, pos, edge_list, feats, after, own=False, extra=()):
    n = len(offsets)
    return pl.pallas_call(
        functools.partial(build_kernel, offsets, cap, edges, own, len(extra), len(after)),
        in_specs=[SMEM_SPEC, SMEM_SPEC] + [VMEM_SPEC] * (1 + n + len(extra)) + [ANY_SPEC] * len(after),
        out_specs=[VMEM_SPEC] * (X + 1),
        out_shape=batch_shapes(n, cap),
        compiler_params=params(8),
        cost_estimate=cost(2.5 * n),
        name="build",
    )(src, pos, edge_list, *feats, *extra, *after)


def follow(arrays, after):
    n = len(arrays)
    return pl.pallas_call(
        lambda *refs: None,
        in_specs=[ANY_SPEC] * (n + len(after)),
        out_specs=[ANY_SPEC] * n,
        out_shape=[jax.ShapeDtypeStruct(a.shape, a.dtype) for a in arrays],
        input_output_aliases={i: i for i in range(n)},
        compiler_params=params(1),
        cost_estimate=cost(0.3),
        name="follow",
    )(*arrays, *after)


def gather_kernel(batches, cap, pos_ref, *refs):
    total = len(batches) * X
    got, refs = refs[:total], refs[total:]
    sum_ref, cnt_ref, tgt_out, acc, acc_c, tgt_ref, sem = refs
    targets = sum_ref.shape[0]
    z, x = pos_ref[0], pos_ref[1]
    rows = [got[X + d][-TAIL:, :].astype(F32)[TAIL - 1 :, :] for d in range(X)]
    tgt_out[...] = jnp.concatenate(rows + rows, axis=0).astype(jnp.int32)
    copy = pltpu.make_async_copy(tgt_out, tgt_ref, sem)
    copy.start()

    def clear(i, carry):
        acc[i] = jnp.zeros((BS, BS), F32)
        return carry

    lax.fori_loop(0, targets, clear, 0, unroll=4)
    acc_c[...] = jnp.zeros_like(acc_c)
    copy.wait()
    for b, offsets in enumerate(batches):
        n = len(offsets)
        for dx in range(X):
            ref = got[b * X + dx]
            tail = ref[n * cap * BS :, :].astype(F32)
            first = lax.rem(z + offsets[0] + Z, Z)
            apart = offsets[-1] - offsets[0]

            def add(j, carry, ref=ref, dx=dx, tail=tail, first=first, apart=apart):
                sender_z = lax.rem(first + j * apart, Z)
                for c in range(cap):
                    k = j * cap + c
                    t = tgt_ref[dx, (sender_z * X + x) * cap + c]

                    @pl.when(t >= 0)
                    def _():
                        rows = ref[pl.ds(pl.multiple_of(k * BS, BS), BS), :]
                        acc[t] += rows.astype(F32)
                        here = lax.broadcasted_iota(jnp.int32, tail.shape, 0) == k
                        count = jnp.sum(jnp.where(here, tail, 0.0), axis=0, keepdims=True)
                        acc_c[pl.ds(t, 1), :] += count

                return carry

            lax.fori_loop(0, n, add, 0)

    def store(i, carry):
        sum_ref[i] = acc[i].astype(BF16)
        return carry

    lax.fori_loop(0, targets, store, 0, unroll=4)
    cnt_ref[...] = acc_c[...]


def gather_sums(batches, cap, targets, pos, got):
    return pl.pallas_call(
        functools.partial(gather_kernel, batches, cap),
        in_specs=[SMEM_SPEC] + [VMEM_SPEC] * len(got),
        out_specs=[VMEM_SPEC] * 3,
        out_shape=[
            jax.ShapeDtypeStruct((targets, BS, BS), BF16),
            jax.ShapeDtypeStruct((targets, BS), F32),
            jax.ShapeDtypeStruct((2 * X, BS), jnp.int32),
        ],
        scratch_shapes=[
            pltpu.VMEM((targets, BS, BS), F32),
            pltpu.VMEM((targets, BS), F32),
            pltpu.SMEM((2 * X, BS), jnp.int32),
            pltpu.SemaphoreType.DMA,
        ],
        compiler_params=params(16),
        cost_estimate=cost(5),
        name="gather_sums",
    )(pos, *got)


def pick_kernel(sets, cap, pos_ref, *refs):
    tgt_ref, mean_ref, outs = refs[0], refs[1], refs[3:]
    z, x = pos_ref[0], pos_ref[1]
    for i, offsets in enumerate(sets):
        for dx in range(X):
            for j, off in enumerate(offsets):
                sender_z = lax.rem(z + off + Z, Z)
                for c in range(cap):
                    t = tgt_ref[dx, (sender_z * X + x) * cap + c]
                    outs[i * X + dx][j * cap + c] = mean_ref[jnp.maximum(t, 0)]


def pick(sets, cap, tgt, pos, mean_all, after):
    shapes = []
    for offsets in sets:
        shapes += [jax.ShapeDtypeStruct((len(offsets) * cap, BS, BS), BF16)] * X
    out = pl.pallas_call(
        functools.partial(pick_kernel, sets, cap),
        in_specs=[SMEM_SPEC, SMEM_SPEC, VMEM_SPEC, ANY_SPEC],
        out_specs=[VMEM_SPEC] * len(shapes),
        out_shape=shapes,
        compiler_params=params(8),
        cost_estimate=cost(3),
        name="pick",
    )(pos, tgt, mean_all, after)
    return [out[i * X : (i + 1) * X] for i in range(len(sets))]


def spread_kernel(offsets, starts, cap, src_ref, pos_ref, adj_ref, *refs):
    n = len(offsets)
    got, refs = refs[:X], refs[X:]
    inits = []
    for parts in starts:
        inits.append([(lo, hi, refs[i]) for i, (lo, hi) in enumerate(parts)])
        refs = refs[len(parts) :]
    outs, acc = refs[:n], refs[n]
    blocks = acc.shape[1]
    z, x = pos_ref[0], pos_ref[1]
    for j in range(n):
        if len(inits[j]) == 0 or inits[j][0][:2] != (0, blocks):
            acc[j] = jnp.zeros(acc.shape[1:], F32)
        for i, (lo, hi, ref) in enumerate(inits[j]):
            if i == 0:
                acc[j, lo:hi] = ref[...].astype(F32)
            else:
                acc[j, lo:hi] += ref[...].astype(F32)
    first = lax.rem(z + offsets[0] + Z, Z)
    apart = offsets[-1] - offsets[0]

    def add(j, carry):
        sender = lax.rem(first + j * apart, Z)
        for dx in range(X):
            owner = lax.rem(x + dx, X)
            for c in range(cap):
                src = src_ref[(sender * X + owner) * cap + c]
                acc[j, src] += jnp.dot(
                    adj_ref[j, dx, c], got[dx][j * cap + c], preferred_element_type=F32
                )
        return carry

    lax.fori_loop(0, n, add, 0)
    for j in range(n):
        outs[j][...] = acc[j].astype(BF16)


def spread(offsets, cap, blocks, src, pos, adj, got, starts):
    n = len(offsets)
    return pl.pallas_call(
        functools.partial(
            spread_kernel, offsets, [[(lo, hi) for lo, hi, _ in s] for s in starts], cap
        ),
        in_specs=[SMEM_SPEC, SMEM_SPEC] + [VMEM_SPEC] * (1 + X + sum(len(s) for s in starts)),
        out_specs=[VMEM_SPEC] * n,
        out_shape=[jax.ShapeDtypeStruct((blocks, BS, BS), BF16)] * n,
        scratch_shapes=[pltpu.VMEM((n, blocks, BS, BS), F32)],
        compiler_params=params(8),
        cost_estimate=cost(1.2 * n),
        name="spread",
    )(src, pos, adj, *got, *[a for s in starts for _, _, a in s])


def shift(value, axis, size, by):
    return lax.ppermute(value, axis, [(i, (i + by) % size) for i in range(size)])


def shift_x(values, sign):
    return [values[0]] + [shift(values[d], "x", X, sign * d) for d in range(1, X)]


def exchange(value, axes):
    return lax.all_to_all(value, axes, split_axis=0, concat_axis=0, tiled=True)


def on_device(
    features, w_self, w_neigh, cotangent, src_block, dst_block, block_count, edge_rows, edge_cols
):
    owners, cap = src_block.shape[1:]
    edges = edge_rows.shape[-1]
    local_nodes = features.shape[0]
    blocks = local_nodes // BS
    half = blocks // 2
    groups = Y * C
    node_total = local_nodes * groups * owners
    pos = jnp.stack([lax.axis_index("z"), lax.axis_index("x")]).astype(jnp.int32)
    feats = features.reshape(blocks, BS, -1)

    own_src = src_block[0].T
    sent = pack(own_src, dst_block[0].T, block_count, edge_rows, edge_cols)
    lists = exchange(sent, "z")
    src = lists[:, :, edges].reshape(owners * cap)
    tgt = lists[:, :, edges + 1].reshape(1, owners * cap)

    batches = [(0,), (-1, 1), (-2, 2), (-3, 3), (4,)]
    *part, adj = build(batches[0], cap, edges, own_src, pos, sent, [feats], [], own=True)
    sums, adjs = [shift_x(part, 1)], [adj]
    up, down, last = feats, feats, sums[0][1:] + [lists]
    for k in range(1, 5):
        if k < 4:
            up, down = follow([shift(up, "z", Z, 1), shift(down, "z", Z, -1)], last)
            arrays = [up, down]
        else:
            up, down = shift(up[:half], "z", Z, 1), shift(down[half:], "z", Z, -1)
            arrays = [jnp.concatenate([up, down])]
        after = sums[max(k - 2, 0)][1:]
        *part, adj = build(batches[k], cap, edges, src, pos, lists, arrays, after, extra=[tgt] if k == 1 else ())
        sums.append(shift_x(part, 1))
        adjs.append(adj)
        last = part[:1]
    acc, cnt, tgt = gather_sums(batches, cap, groups * blocks, pos, sum(sums, []))

    own_sums = lax.psum_scatter(acc, ("y", "c"), scatter_dimension=0, tiled=True)
    got_cnt = exchange(cnt, ("y", "c"))
    own_cnt = jnp.sum(got_cnt.reshape(groups, blocks, BS), axis=0)
    divisor = jnp.maximum(own_cnt, 1.0).reshape(local_nodes, 1)
    neigh_mean = (own_sums.astype(F32).reshape(local_nodes, -1) / divisor).astype(BF16)
    preact = jnp.dot(features, w_self, preferred_element_type=F32) + jnp.dot(
        neigh_mean, w_neigh, preferred_element_type=F32
    )
    sigmoids = jax.nn.sigmoid(preact)
    activated = (preact * sigmoids).astype(BF16)
    grad_pre = (cotangent.astype(F32) * sigmoids * (1.0 + preact * (1.0 - sigmoids))).astype(BF16)
    grad_mean = (
        jnp.einsum("nh,fh->nf", grad_pre, w_neigh, preferred_element_type=F32) / divisor
    ).astype(BF16)
    mean_all = lax.all_gather(grad_mean.reshape(blocks, BS, -1), ("y", "c"), axis=0, tiled=True)

    both = jnp.concatenate([features, neigh_mean], axis=1)
    grads = jnp.einsum("nf,nh->fh", both, grad_pre, preferred_element_type=F32)
    rows = grads.shape[0] // owners
    piece = jnp.sum(exchange(grads, ("z", "x")).reshape(owners, rows, -1), axis=0)
    piece = jnp.broadcast_to(piece[None], (groups, rows, piece.shape[1]))
    piece = jnp.sum(exchange(piece, ("y", "c")), axis=0)
    sets = [(4,), (-3, 3), (-2, 2), (-1, 1), (0,)]
    picked = pick(sets, cap, tgt, pos, mean_all, piece)
    grads = exchange(jnp.broadcast_to(piece[None], (owners, rows, piece.shape[1])), ("z", "x"))
    grads = grads.reshape(owners * rows, -1) * float(node_total) ** (-0.5)

    own_term = jnp.einsum("nh,fh->nf", grad_pre, w_self, preferred_element_type=F32)
    own_term = own_term.reshape(blocks, BS, -1)

    got = [shift_x(p, -1) for p in picked]

    def back(k, starts):
        return spread(batches[k], cap, blocks, src, pos, adjs[k], got[4 - k], starts)

    (far,) = back(4, [[]])
    up, down = shift(far[:half], "z", Z, 1), shift(far[half:], "z", Z, -1)
    down, up = back(3, [[(half, blocks, down)], [(0, half, up)]])
    for k in (2, 1):
        up, down = shift(up, "z", Z, 1), shift(down, "z", Z, -1)
        down, up = back(k, [[(0, blocks, down)], [(0, blocks, up)]])
    up, down = shift(up, "z", Z, 1), shift(down, "z", Z, -1)
    (grad_features,) = back(0, [[(0, blocks, own_term), (0, blocks, up), (0, blocks, down)]])
    f = features.shape[1]
    return activated, grad_features.reshape(local_nodes, -1), grads[:f], grads[f:]


def solution(mesh):
    mesh = Mesh(mesh.devices.reshape(Y, C, Z, X), ("y", "c", "z", "x"))
    every = ("y", "c", "z", "x")
    return jax.shard_map(
        on_device,
        mesh=mesh,
        in_specs=(
            P(every, None),
            P(),
            P(),
            P(every, None),
            P(every, None, None),
            P(every, None, None),
            P(every, None),
            P(every, None, None, None),
            P(every, None, None, None),
        ),
        out_specs=(P(every, None), P(every, None), P(), P()),
        check_vma=False,
    )
```

```python
import functools

import jax
import jax.numpy as jnp
from jax import lax
from jax.experimental import pallas as pl
from jax.experimental.pallas import tpu as pltpu
from jax.sharding import Mesh, PartitionSpec as P

BS = 128
TAIL = 16
Y, C, Z, X = 4, 2, 8, 4
F32 = jnp.float32
BF16 = jnp.bfloat16
MIB = 1024 * 1024
NT = (((1,), (1,)), ((), ()))
SMEM_SPEC = pl.BlockSpec(memory_space=pltpu.SMEM)
VMEM_SPEC = pl.BlockSpec(memory_space=pltpu.VMEM)
ANY_SPEC = pl.BlockSpec(memory_space=pl.ANY)
LISTS = 256
META = 64


def dot_nt(a, b):
    return lax.dot_general(a, b, NT, preferred_element_type=F32)


def params(mib):
    return pltpu.CompilerParams(vmem_limit_bytes=mib * MIB)


def cost(us):
    return pl.CostEstimate(flops=0, bytes_accessed=int(us * 3.5e6), transcendentals=0)


def one_hot_t(row, extent):
    ids = lax.broadcasted_iota(jnp.int32, (extent, row.shape[1]), 0)
    return jnp.where(ids == row, 1.0, 0.0).astype(BF16)


def pack_kernel(cap, edges, src_hbm, dst_hbm, used_hbm, rows_hbm, cols_hbm, pos_ref, *refs):
    outs, (rows_ref, cols_ref, src_ref, dst_ref, used_ref, sem) = refs[:Z], refs[Z:]
    copies = [
        pltpu.make_async_copy(from_ref, to_ref, sem.at[i])
        for i, (from_ref, to_ref) in enumerate(
            [
                (rows_hbm, rows_ref),
                (cols_hbm, cols_ref),
                (src_hbm, src_ref),
                (dst_hbm, dst_ref),
                (used_hbm, used_ref),
            ]
        )
    ]
    for copy in copies:
        copy.start()
    rest = LISTS - edges
    meta_slot = lax.broadcasted_iota(jnp.int32, (cap, rest), 0)
    meta_lane = lax.broadcasted_iota(jnp.int32, (cap, rest), 1)
    slot = lax.broadcasted_iota(jnp.int32, (cap, edges), 0)
    z = pos_ref[0]
    for copy in copies:
        copy.wait()
    for d, out in enumerate(outs):
        first = lax.rem(z + d, Z) * X

        def pack(i, carry, out=out, first=first):
            o = first + i
            packed = rows_ref[0, o] * BS + cols_ref[0, o]
            meta = jnp.zeros((cap, rest), jnp.int32)
            for c in range(cap):
                to = jnp.where(c < used_ref[0, o], dst_ref[c, o], -1)
                packed = jnp.where(jnp.logical_and(slot == c, to < 0), BS * BS, packed)
                value = jnp.where(meta_lane == 0, src_ref[c, o], to)
                meta = jnp.where(meta_slot == c, value, meta)
            out[i, :, :edges] = packed
            out[i, :, edges:] = meta
            return carry

        lax.fori_loop(0, X, pack, 0, unroll=2)


def pack(src, dst, used, rows, cols, pos):
    owners, cap, edges = rows.shape[1:]
    hbm = pl.BlockSpec(memory_space=pltpu.HBM)
    return pl.pallas_call(
        functools.partial(pack_kernel, cap, edges),
        in_specs=[hbm] * 5 + [SMEM_SPEC],
        out_specs=[VMEM_SPEC] * Z,
        out_shape=[jax.ShapeDtypeStruct((X, cap, LISTS), jnp.int32)] * Z,
        scratch_shapes=[
            pltpu.VMEM(rows.shape, jnp.int32),
            pltpu.VMEM(cols.shape, jnp.int32),
            pltpu.SMEM(src.shape, jnp.int32),
            pltpu.SMEM(dst.shape, jnp.int32),
            pltpu.SMEM(used.shape, jnp.int32),
            pltpu.SemaphoreType.DMA((5,)),
        ],
        compiler_params=params(4),
        cost_estimate=cost(3),
        name="pack",
    )(src, dst, used, rows, cols, pos)


def copy_meta(lists, smem, sem):
    copies = []
    for j, ref in enumerate(lists):
        piece = ref.at[:, :, pl.ds(LISTS - BS, BS)]
        copies.append(pltpu.make_async_copy(piece, smem.at[j], sem.at[j]))
        copies[-1].start()
    return copies


def build_kernel(n, sets, cap, edges, after, pos_ref, *refs):
    lists, feats, refs = refs[:n], refs[n : 2 * n], refs[2 * n + after :]
    sums, (adj_ref, smem, sem) = refs[: X * len(sets)], refs[X * len(sets) :]
    x = pos_ref[1]
    for copy in copy_meta(lists, smem, sem):
        copy.wait()
    row_id = lax.broadcasted_iota(jnp.int32, (TAIL, BS), 0)
    edge_row = lax.broadcasted_iota(jnp.int32, (TAIL, edges), 0)

    def slots(dx, senders):
        owner = lax.rem(x + dx, X)
        used = len(senders) * cap
        tail = jnp.zeros((TAIL, BS), F32)
        parts = []
        for i, j in enumerate(senders):
            packed = lists[j][owner]
            for c in range(cap):
                k = i * cap + c
                e = packed[c : c + 1, :edges]
                rt = one_hot_t(lax.shift_right_logical(e, 7), BS)
                ct = one_hot_t(jnp.bitwise_and(e, BS - 1), BS)
                a = dot_nt(rt, ct).astype(BF16)
                adj_ref[j, dx, c] = dot_nt(ct, rt).astype(BF16)
                block = feats[j][smem[j, owner, c, META]]
                parts.append(jnp.dot(a, block, preferred_element_type=F32).astype(BF16))
                tail = tail + dot_nt(jnp.where(edge_row == k, 1.0, 0.0).astype(BF16), rt)
                to = smem[j, owner, c, META + 1].astype(F32)
                tail = jnp.where(row_id == used + k, to, tail)
        return parts + [tail.astype(BF16)]

    def store(out, parts):
        for k, part in enumerate(parts):
            out[k * BS : k * BS + part.shape[0], :] = part

    for i, senders in enumerate(sets):

        def step(dx, carry, i=i, senders=senders):
            parts = slots(dx, senders)
            for d in range(X):
                pl.when(dx == d)(functools.partial(store, sums[i * X + d], parts))
            return carry

        lax.fori_loop(0, X, step, 0)


def build(cap, edges, pos, lists, feats, sets=None, after=()):
    n = len(lists)
    sets = [tuple(range(n))] if sets is None else sets
    *out, adj = pl.pallas_call(
        functools.partial(build_kernel, n, sets, cap, edges, len(after)),
        in_specs=[SMEM_SPEC] + [VMEM_SPEC] * (2 * n) + [ANY_SPEC] * len(after),
        out_specs=[VMEM_SPEC] * (X * len(sets) + 1),
        out_shape=[
            jax.ShapeDtypeStruct((len(s) * cap * BS + TAIL, BS), BF16) for s in sets for _ in range(X)
        ]
        + [jax.ShapeDtypeStruct((n, X, cap, BS, BS), BF16)],
        scratch_shapes=[
            pltpu.SMEM((n, X, cap, BS), jnp.int32),
            pltpu.SemaphoreType.DMA((n,)),
        ],
        compiler_params=params(8),
        cost_estimate=cost(2.5 * n),
        name="build",
    )(pos, *lists, *feats, *after)
    return [out[i * X : (i + 1) * X] for i in range(len(sets))], adj


def follow(arrays, after):
    n = len(arrays)
    return pl.pallas_call(
        lambda *refs: None,
        in_specs=[ANY_SPEC] * (n + len(after)),
        out_specs=[ANY_SPEC] * n,
        out_shape=[jax.ShapeDtypeStruct(a.shape, a.dtype) for a in arrays],
        input_output_aliases={i: i for i in range(n)},
        compiler_params=params(1),
        cost_estimate=cost(0.3),
        name="follow",
    )(*arrays, *after)


def gather_kernel(sizes, cap, *refs):
    total = len(sizes) * X
    got, refs = refs[:total], refs[total:]
    sum_ref, cnt_ref, tgt_out, acc, acc_c, tgt_ref, sem = refs
    targets = sum_ref.shape[0]
    lane = lax.broadcasted_iota(jnp.int32, tgt_out.shape, 1)
    tgt = jnp.zeros(tgt_out.shape, F32)
    for a, ref in enumerate(got):
        n = sizes[a // X] * cap
        tail = ref[n * BS :, :].astype(F32)
        rows = tail[n : 2 * n, :]
        if n < tgt_out.shape[0]:
            rows = jnp.concatenate([rows, rows], axis=0)
        tgt = jnp.where(lane == a, rows, tgt)
    tgt_out[...] = tgt.astype(jnp.int32)
    copy = pltpu.make_async_copy(tgt_out, tgt_ref, sem)
    copy.start()

    def clear(i, carry):
        acc[i] = jnp.zeros((BS, BS), F32)
        return carry

    lax.fori_loop(0, targets, clear, 0, unroll=4)
    acc_c[...] = jnp.zeros_like(acc_c)
    copy.wait()
    for a, ref in enumerate(got):
        n = sizes[a // X] * cap
        tail = ref[n * BS :, :].astype(F32)
        for k in range(n):
            t = tgt_ref[k, a]

            @pl.when(t >= 0)
            def _(ref=ref, tail=tail, k=k, t=t):
                acc[t] += ref[k * BS : (k + 1) * BS, :].astype(F32)
                acc_c[pl.ds(t, 1), :] += tail[k : k + 1, :]

    def store(i, carry):
        sum_ref[i] = acc[i].astype(BF16)
        return carry

    lax.fori_loop(0, targets, store, 0, unroll=4)
    cnt_ref[...] = acc_c[...]


def gather_sums(sizes, cap, targets, got):
    return pl.pallas_call(
        functools.partial(gather_kernel, sizes, cap),
        in_specs=[VMEM_SPEC] * len(got),
        out_specs=[VMEM_SPEC] * 3,
        out_shape=[
            jax.ShapeDtypeStruct((targets, BS, BS), BF16),
            jax.ShapeDtypeStruct((targets, BS), F32),
            jax.ShapeDtypeStruct((2 * cap, BS), jnp.int32),
        ],
        scratch_shapes=[
            pltpu.VMEM((targets, BS, BS), F32),
            pltpu.VMEM((targets, BS), F32),
            pltpu.SMEM((2 * cap, BS), jnp.int32),
            pltpu.SemaphoreType.DMA,
        ],
        compiler_params=params(16),
        cost_estimate=cost(5),
        name="gather_sums",
    )(*got)


def pick_kernel(sets, cap, tgt_ref, mean_ref, after_ref, *outs):
    for i, senders in enumerate(sets):
        for dx in range(X):
            for j, (payload, first) in enumerate(senders):
                for c in range(cap):
                    t = tgt_ref[first + c, payload * X + dx]
                    outs[i * X + dx][j * cap + c] = mean_ref[jnp.maximum(t, 0)]


def pick(sets, cap, tgt, mean_all, after):
    shapes = []
    for senders in sets:
        shapes += [jax.ShapeDtypeStruct((len(senders) * cap, BS, BS), BF16)] * X
    out = pl.pallas_call(
        functools.partial(pick_kernel, sets, cap),
        in_specs=[SMEM_SPEC, VMEM_SPEC, ANY_SPEC],
        out_specs=[VMEM_SPEC] * len(shapes),
        out_shape=shapes,
        compiler_params=params(8),
        cost_estimate=cost(3),
        name="pick",
    )(tgt, mean_all, after)
    return [out[i * X : (i + 1) * X] for i in range(len(sets))]


def spread_kernel(starts, cap, pos_ref, *refs):
    n = len(starts)
    lists, adj_ref, got, refs = refs[:n], refs[n], refs[n + 1 : n + 1 + X], refs[n + 1 + X :]
    inits = []
    for parts in starts:
        inits.append([(lo, hi, refs[i]) for i, (lo, hi) in enumerate(parts)])
        refs = refs[len(parts) :]
    outs, (acc, smem, sem) = refs[:n], refs[n:]
    blocks = acc.shape[1]
    x = pos_ref[1]
    copies = copy_meta(lists, smem, sem)
    for j in range(n):
        if len(inits[j]) == 0 or inits[j][0][:2] != (0, blocks):
            acc[j] = jnp.zeros(acc.shape[1:], F32)
        for i, (lo, hi, ref) in enumerate(inits[j]):
            if i == 0:
                acc[j, lo:hi] = ref[...].astype(F32)
            else:
                acc[j, lo:hi] += ref[...].astype(F32)
    for copy in copies:
        copy.wait()

    def add(j, carry):
        for dx in range(X):
            owner = lax.rem(x + dx, X)
            for c in range(cap):
                src = smem[j, owner, c, META]
                acc[j, src] += jnp.dot(
                    adj_ref[j, dx, c], got[dx][j * cap + c], preferred_element_type=F32
                )
        return carry

    lax.fori_loop(0, n, add, 0)
    for j in range(n):
        outs[j][...] = acc[j].astype(BF16)


def spread(cap, blocks, lists, pos, adj, got, starts):
    n = len(starts)
    return pl.pallas_call(
        functools.partial(spread_kernel, [[(lo, hi) for lo, hi, _ in s] for s in starts], cap),
        in_specs=[SMEM_SPEC]
        + [ANY_SPEC] * n
        + [VMEM_SPEC] * (1 + X + sum(len(s) for s in starts)),
        out_specs=[VMEM_SPEC] * n,
        out_shape=[jax.ShapeDtypeStruct((blocks, BS, BS), BF16)] * n,
        scratch_shapes=[
            pltpu.VMEM((n, blocks, BS, BS), F32),
            pltpu.SMEM((n, X, cap, BS), jnp.int32),
            pltpu.SemaphoreType.DMA((n,)),
        ],
        compiler_params=params(8),
        cost_estimate=cost(1.2 * n),
        name="spread",
    )(pos, *lists, adj, *got, *[a for s in starts for _, _, a in s])


def shift(value, axis, size, by):
    return lax.ppermute(value, axis, [(i, (i + by) % size) for i in range(size)])


def shift_x(values, sign):
    return [values[0]] + [shift(values[d], "x", X, sign * d) for d in range(1, X)]


def exchange(value, axes):
    return lax.all_to_all(value, axes, split_axis=0, concat_axis=0, tiled=True)


def on_device(
    features, w_self, w_neigh, cotangent, src_block, dst_block, block_count, edge_rows, edge_cols
):
    owners, cap = src_block.shape[1:]
    edges = edge_rows.shape[-1]
    local_nodes = features.shape[0]
    blocks = local_nodes // BS
    half = blocks // 2
    groups = Y * C
    node_total = local_nodes * groups * owners
    pos = jnp.stack([lax.axis_index("z"), lax.axis_index("x")]).astype(jnp.int32)
    feats = features.reshape(blocks, BS, -1)

    sent = pack(src_block[0].T, dst_block[0].T, block_count, edge_rows, edge_cols, pos)
    lists = [sent[:1]]
    for k in range(1, 4):
        lists.append([shift(sent[k], "z", Z, k), shift(sent[Z - k], "z", Z, -k)])
    lists.append([shift(sent[Z // 2], "z", Z, Z // 2)])

    parts, adj = build(cap, edges, pos, lists[0], [feats])
    sums, adjs = [shift_x(parts[0], 1)], [adj]
    up, down, last = feats, feats, parts[0][:1]
    for k in range(1, 5):
        if k < 4:
            up, down = shift(up, "z", Z, 1), shift(down, "z", Z, -1)
            up, down = follow([up, down], last + lists[k] + (lists[4] if k == 3 else []))
            arrays = [up, down]
        else:
            up, down = shift(up[:half], "z", Z, 1), shift(down[half:], "z", Z, -1)
            arrays = [jnp.concatenate([up, down])]
        parts, adj = build(cap, edges, pos, lists[k], arrays)
        sums += [shift_x(p, 1) for p in parts]
        last = sums[-1][1:] + sums[-2][1:]
        adjs.append(adj)
    acc, cnt, tgt = gather_sums([1, 2, 2, 2, 1], cap, groups * blocks, sum(sums, []))

    own_sums = lax.psum_scatter(acc, ("y", "c"), scatter_dimension=0, tiled=True)
    got_cnt = exchange(cnt, ("y", "c"))
    own_cnt = jnp.sum(got_cnt.reshape(groups, blocks, BS), axis=0)
    divisor = jnp.maximum(own_cnt, 1.0).reshape(local_nodes, 1)
    neigh_mean = (own_sums.astype(F32).reshape(local_nodes, -1) / divisor).astype(BF16)
    preact = jnp.dot(features, w_self, preferred_element_type=F32) + jnp.dot(
        neigh_mean, w_neigh, preferred_element_type=F32
    )
    sigmoids = jax.nn.sigmoid(preact)
    activated = (preact * sigmoids).astype(BF16)
    grad_pre = (cotangent.astype(F32) * sigmoids * (1.0 + preact * (1.0 - sigmoids))).astype(BF16)
    grad_mean = (
        jnp.einsum("nh,fh->nf", grad_pre, w_neigh, preferred_element_type=F32) / divisor
    ).astype(BF16)
    mean_all = lax.all_gather(grad_mean.reshape(blocks, BS, -1), ("y", "c"), axis=0, tiled=True)

    both = jnp.concatenate([features, neigh_mean], axis=1)
    grads = jnp.einsum("nf,nh->fh", both, grad_pre, preferred_element_type=F32)
    rows = grads.shape[0] // owners
    piece = jnp.sum(exchange(grads, ("z", "x")).reshape(owners, rows, -1), axis=0)
    piece = jnp.broadcast_to(piece[None], (groups, rows, piece.shape[1]))
    piece = jnp.sum(exchange(piece, ("y", "c")), axis=0)
    sets = [[(4, 0)], [(3, 0), (3, cap)], [(2, 0), (2, cap)], [(1, 0), (1, cap)], [(0, 0)]]
    picked = pick(sets, cap, tgt, mean_all, piece)
    grads = exchange(jnp.broadcast_to(piece[None], (owners, rows, piece.shape[1])), ("z", "x"))
    grads = grads.reshape(owners * rows, -1) * float(node_total) ** (-0.5)

    own_term = jnp.einsum("nh,fh->nf", grad_pre, w_self, preferred_element_type=F32)
    own_term = own_term.reshape(blocks, BS, -1)

    got = [shift_x(picked[0], -1)]
    picked[1] = follow(picked[1], got[0][1:])
    got += [shift_x(p, -1) for p in picked[1:]]

    def back(k, starts):
        return spread(cap, blocks, lists[k], pos, adjs[k], got[4 - k], starts)

    (far,) = back(4, [[]])
    up, down = shift(far[:half], "z", Z, 1), shift(far[half:], "z", Z, -1)
    down, up = back(3, [[(half, blocks, down)], [(0, half, up)]])
    for k in (2, 1):
        up, down = shift(up, "z", Z, 1), shift(down, "z", Z, -1)
        down, up = back(k, [[(0, blocks, down)], [(0, blocks, up)]])
    up, down = shift(up, "z", Z, 1), shift(down, "z", Z, -1)
    (grad_features,) = back(0, [[(0, blocks, own_term), (0, blocks, up), (0, blocks, down)]])
    f = features.shape[1]
    return activated, grad_features.reshape(local_nodes, -1), grads[:f], grads[f:]


def solution(mesh):
    mesh = Mesh(mesh.devices.reshape(Y, C, Z, X), ("y", "c", "z", "x"))
    every = ("y", "c", "z", "x")
    return jax.shard_map(
        on_device,
        mesh=mesh,
        in_specs=(
            P(every, None),
            P(),
            P(),
            P(every, None),
            P(every, None, None),
            P(every, None, None),
            P(every, None),
            P(every, None, None, None),
            P(every, None, None, None),
        ),
        out_specs=(P(every, None), P(every, None), P(), P()),
        check_vma=False,
    )
```

```python
import functools

import jax
import jax.numpy as jnp
from jax import lax
from jax.experimental import pallas as pl
from jax.experimental.pallas import tpu as pltpu
from jax.sharding import Mesh, PartitionSpec as P

BS = 128
TAIL = 16
Y, C, Z, X = 4, 2, 8, 4
F32 = jnp.float32
BF16 = jnp.bfloat16
MIB = 1024 * 1024
NT = (((1,), (1,)), ((), ()))
SMEM_SPEC = pl.BlockSpec(memory_space=pltpu.SMEM)
VMEM_SPEC = pl.BlockSpec(memory_space=pltpu.VMEM)
ANY_SPEC = pl.BlockSpec(memory_space=pl.ANY)
LISTS = 256


def dot_nt(a, b):
    return lax.dot_general(a, b, NT, preferred_element_type=F32)


def params(mib):
    return pltpu.CompilerParams(vmem_limit_bytes=mib * MIB)


def cost(us):
    return pl.CostEstimate(flops=0, bytes_accessed=int(us * 3.5e6), transcendentals=0)


def one_hot_t(row, extent):
    ids = lax.broadcasted_iota(jnp.int32, (extent, row.shape[1]), 0)
    return jnp.where(ids == row, 1.0, 0.0).astype(BF16)


def build_batch(offsets, cap, edges, src_of, z, x, edge_ref, feats, sum_refs, adj_ref, tgt_ref=None):
    n = len(offsets)

    def owner_step(dx, carry):
        owner = lax.rem(x + dx, X)
        counts = jnp.zeros((TAIL, BS), F32)
        if tgt_ref is not None:
            last = lax.broadcasted_iota(jnp.int32, (TAIL, BS), 0) == TAIL - 1
            counts = jnp.where(last, tgt_ref[...].astype(F32), 0.0)
        parts = []
        for j, off in enumerate(offsets):
            row = lax.rem(z + off + Z, Z) * X + owner
            packed = edge_ref[row]
            for c in range(cap):
                k = j * cap + c
                e = packed[c : c + 1, :edges]
                rt = one_hot_t(lax.shift_right_logical(e, 7), BS)
                ct = one_hot_t(jnp.bitwise_and(e, BS - 1), BS)
                a = dot_nt(rt, ct).astype(BF16)
                adj_ref[j, dx, c] = dot_nt(ct, rt).astype(BF16)
                part = jnp.dot(a, feats[j][src_of(row, c)], preferred_element_type=F32)
                parts.append(part.astype(BF16))
                pick = jnp.where(
                    lax.broadcasted_iota(jnp.int32, (TAIL, edges), 0) == k, 1.0, 0.0
                ).astype(BF16)
                counts = counts + dot_nt(pick, rt)
        parts.append(counts.astype(BF16))
        for d, out in enumerate(sum_refs):

            @pl.when(dx == d)
            def _(out=out):
                for k, part in enumerate(parts):
                    out[k * BS : k * BS + part.shape[0], :] = part

        return carry

    lax.fori_loop(0, X, owner_step, 0)


def batch_shapes(n, cap):
    return [jax.ShapeDtypeStruct((n * cap * BS + TAIL, BS), BF16)] * X + [
        jax.ShapeDtypeStruct((n, X, cap, BS, BS), BF16)
    ]


def pack_kernel(cap, edges, src_ref, dst_ref, used_ref, rows_ref, cols_ref, lists_ref):
    owners = rows_ref.shape[1]
    rest = LISTS - edges
    meta_slot = lax.broadcasted_iota(jnp.int32, (cap, rest), 0)
    meta_lane = lax.broadcasted_iota(jnp.int32, (cap, rest), 1)
    slot = lax.broadcasted_iota(jnp.int32, (cap, edges), 0)

    def pack(o, carry):
        packed = rows_ref[0, o] * BS + cols_ref[0, o]
        meta = jnp.zeros((cap, rest), jnp.int32)
        for c in range(cap):
            to = jnp.where(c < used_ref[0, o], dst_ref[c, o], -1)
            packed = jnp.where(jnp.logical_and(slot == c, to < 0), BS * BS, packed)
            value = jnp.where(meta_lane == 0, src_ref[c, o], to)
            meta = jnp.where(meta_slot == c, value, meta)
        lists_ref[o, :, :edges] = packed
        lists_ref[o, :, edges:] = meta
        return carry

    lax.fori_loop(0, owners, pack, 0, unroll=4)


def pack(src, dst, used, rows, cols):
    owners, cap, edges = rows.shape[1:]
    whole = pl.BlockSpec(rows.shape, lambda i: (0, 0, 0, 0))
    return pl.pallas_call(
        functools.partial(pack_kernel, cap, edges),
        grid=(1,),
        in_specs=[SMEM_SPEC] * 3 + [whole] * 2,
        out_specs=VMEM_SPEC,
        out_shape=jax.ShapeDtypeStruct((owners, cap, LISTS), jnp.int32),
        compiler_params=params(4),
        cost_estimate=cost(2),
        name="pack",
    )(src, dst, used, rows, cols)


def build_kernel(offsets, cap, edges, own, extra, after, src_ref, pos_ref, edge_ref, *refs):
    n = len(offsets)
    feats, refs = refs[:n], refs[n:]
    tgt_ref = refs[0] if extra else None
    refs = refs[extra + after :]

    def src_of(row, c):
        if own:
            return src_ref[c, row]
        return src_ref[row * cap + c]

    build_batch(
        offsets,
        cap,
        edges,
        src_of,
        pos_ref[0],
        pos_ref[1],
        edge_ref,
        feats,
        refs[:X],
        refs[X],
        tgt_ref,
    )


def build(offsets, cap, edges, src, pos, edge_list, feats, after, own=False, extra=()):
    n = len(offsets)
    return pl.pallas_call(
        functools.partial(build_kernel, offsets, cap, edges, own, len(extra), len(after)),
        in_specs=[SMEM_SPEC, SMEM_SPEC] + [VMEM_SPEC] * (1 + n + len(extra)) + [ANY_SPEC] * len(after),
        out_specs=[VMEM_SPEC] * (X + 1),
        out_shape=batch_shapes(n, cap),
        compiler_params=params(8),
        cost_estimate=cost(2.5 * n),
        name="build",
    )(src, pos, edge_list, *feats, *extra, *after)


def follow(arrays, after):
    n = len(arrays)
    return pl.pallas_call(
        lambda *refs: None,
        in_specs=[ANY_SPEC] * (n + len(after)),
        out_specs=[ANY_SPEC] * n,
        out_shape=[jax.ShapeDtypeStruct(a.shape, a.dtype) for a in arrays],
        input_output_aliases={i: i for i in range(n)},
        compiler_params=params(1),
        cost_estimate=cost(0.3),
        name="follow",
    )(*arrays, *after)


def gather_kernel(batches, cap, pos_ref, *refs):
    total = len(batches) * X
    got, refs = refs[:total], refs[total:]
    keeps, sends, (tgt_out, acc, acc_c, tgt_ref, sem) = refs[:Y], refs[Y : 2 * Y], refs[2 * Y :]
    targets = acc.shape[0]
    z, x, y, core = pos_ref[0], pos_ref[1], pos_ref[2], pos_ref[3]
    rows = [got[X + d][-TAIL:, :].astype(F32)[TAIL - 1 :, :] for d in range(X)]
    tgt_out[...] = jnp.concatenate(rows + rows, axis=0).astype(jnp.int32)
    copy = pltpu.make_async_copy(tgt_out, tgt_ref, sem)
    copy.start()

    def clear(i, carry):
        acc[i] = jnp.zeros((BS, BS), F32)
        return carry

    lax.fori_loop(0, targets, clear, 0, unroll=4)
    acc_c[...] = jnp.zeros_like(acc_c)
    copy.wait()
    for b, offsets in enumerate(batches):
        n = len(offsets)
        for dx in range(X):
            ref = got[b * X + dx]
            tail = ref[n * cap * BS :, :].astype(F32)
            first = lax.rem(z + offsets[0] + Z, Z)
            apart = offsets[-1] - offsets[0]

            def add(j, carry, ref=ref, dx=dx, tail=tail, first=first, apart=apart):
                sender_z = lax.rem(first + j * apart, Z)
                for c in range(cap):
                    k = j * cap + c
                    t = tgt_ref[dx, (sender_z * X + x) * cap + c]

                    @pl.when(t >= 0)
                    def _():
                        rows = ref[pl.ds(pl.multiple_of(k * BS, BS), BS), :]
                        acc[t] += rows.astype(F32)
                        here = lax.broadcasted_iota(jnp.int32, tail.shape, 0) == k
                        count = jnp.sum(jnp.where(here, tail, 0.0), axis=0, keepdims=True)
                        acc_c[pl.ds(t, 1), :] += count

                return carry

            lax.fori_loop(0, n, add, 0)

    blocks = targets // (Y * C)
    for dy in range(Y):
        for out, to_core in ((keeps[dy], core), (sends[dy], 1 - core)):
            first = (lax.rem(y + dy, Y) * C + to_core) * blocks

            def store(i, carry, out=out, first=first):
                out[pl.ds(pl.multiple_of(i * BS, BS), BS), :] = acc[first + i].astype(BF16)
                return carry

            lax.fori_loop(0, blocks, store, 0, unroll=4)
            count = acc_c[pl.ds(pl.multiple_of(first, blocks), blocks), :]
            put_counts(out, count, blocks)


def put_counts(out, count, blocks):
    high = jnp.floor(count * (1.0 / 256.0))
    out[blocks * BS : blocks * (BS + 1), :] = high.astype(BF16)
    out[blocks * (BS + 1) :, :] = (count - 256.0 * high).astype(BF16)


def get_counts(total, blocks):
    return 256.0 * total[blocks * BS : blocks * (BS + 1)] + total[blocks * (BS + 1) :]


def gather_sums(batches, cap, targets, pos, got):
    blocks = targets // (Y * C)
    part = jax.ShapeDtypeStruct((blocks * (BS + 2), BS), BF16)
    out = pl.pallas_call(
        functools.partial(gather_kernel, batches, cap),
        in_specs=[SMEM_SPEC] + [VMEM_SPEC] * len(got),
        out_specs=[VMEM_SPEC] * (2 * Y + 1),
        out_shape=[part] * (2 * Y) + [jax.ShapeDtypeStruct((2 * X, BS), jnp.int32)],
        scratch_shapes=[
            pltpu.VMEM((targets, BS, BS), F32),
            pltpu.VMEM((targets, BS), F32),
            pltpu.SMEM((2 * X, BS), jnp.int32),
            pltpu.SemaphoreType.DMA,
        ],
        compiler_params=params(16),
        cost_estimate=cost(5),
        name="gather_sums",
    )(pos, *got)
    return out[:Y], out[Y : 2 * Y], out[2 * Y]


def join_kernel(a_ref, b_ref, out_ref):
    blocks = out_ref.shape[0] // (BS + 2)

    def add(i, carry):
        rows = pl.ds(pl.multiple_of(i * BS, BS), BS)
        out_ref[rows, :] = (a_ref[rows, :].astype(F32) + b_ref[rows, :].astype(F32)).astype(BF16)
        return carry

    lax.fori_loop(0, blocks, add, 0, unroll=2)
    digits = slice(blocks * BS, None)
    total = a_ref[digits, :].astype(F32) + b_ref[digits, :].astype(F32)
    put_counts(out_ref, 256.0 * total[:blocks] + total[blocks:], blocks)


def join(a, b):
    return pl.pallas_call(
        join_kernel,
        in_specs=[VMEM_SPEC] * 2,
        out_specs=VMEM_SPEC,
        out_shape=jax.ShapeDtypeStruct(a.shape, BF16),
        compiler_params=params(4),
        cost_estimate=cost(0.6),
        name="join",
    )(a, b)


def pick_kernel(sets, cap, tgt_ref, pos_ref, *refs):
    means, outs, mean_ref = refs[: Y * C], refs[Y * C + 1 : -1], refs[-1]
    z, x, y, core = pos_ref[0], pos_ref[1], pos_ref[2], pos_ref[3]
    blocks = means[0].shape[0]
    for i, ref in enumerate(means):
        from_core = core if i % C == 0 else 1 - core
        group = lax.rem(y - i // C + Y, Y) * C + from_core

        def place(r, carry, ref=ref, group=group):
            mean_ref[group * blocks + r] = ref[r]
            return carry

        lax.fori_loop(0, blocks, place, 0, unroll=4)
    for i, offsets in enumerate(sets):
        for dx in range(X):
            for j, off in enumerate(offsets):
                sender_z = lax.rem(z + off + Z, Z)
                for c in range(cap):
                    t = tgt_ref[dx, (sender_z * X + x) * cap + c]
                    outs[i * X + dx][j * cap + c] = mean_ref[jnp.maximum(t, 0)]


def pick(sets, cap, tgt, pos, means, after):
    shapes = []
    for offsets in sets:
        shapes += [jax.ShapeDtypeStruct((len(offsets) * cap, BS, BS), BF16)] * X
    out = pl.pallas_call(
        functools.partial(pick_kernel, sets, cap),
        in_specs=[SMEM_SPEC, SMEM_SPEC] + [VMEM_SPEC] * len(means) + [ANY_SPEC],
        out_specs=[VMEM_SPEC] * len(shapes),
        out_shape=shapes,
        scratch_shapes=[pltpu.VMEM((len(means) * means[0].shape[0], BS, BS), BF16)],
        compiler_params=params(8),
        cost_estimate=cost(3),
        name="pick",
    )(tgt, pos, *means, after)
    return [out[i * X : (i + 1) * X] for i in range(len(sets))]


def spread_kernel(offsets, starts, cap, src_ref, pos_ref, adj_ref, *refs):
    n = len(offsets)
    got, refs = refs[:X], refs[X:]
    inits = []
    for parts in starts:
        inits.append([(lo, hi, refs[i]) for i, (lo, hi) in enumerate(parts)])
        refs = refs[len(parts) :]
    outs, acc = refs[:n], refs[n]
    blocks = acc.shape[1]
    z, x = pos_ref[0], pos_ref[1]
    for j in range(n):
        if len(inits[j]) == 0 or inits[j][0][:2] != (0, blocks):
            acc[j] = jnp.zeros(acc.shape[1:], F32)
        for i, (lo, hi, ref) in enumerate(inits[j]):
            if i == 0:
                acc[j, lo:hi] = ref[...].astype(F32)
            else:
                acc[j, lo:hi] += ref[...].astype(F32)
    first = lax.rem(z + offsets[0] + Z, Z)
    apart = offsets[-1] - offsets[0]

    def add(j, carry):
        sender = lax.rem(first + j * apart, Z)
        for dx in range(X):
            owner = lax.rem(x + dx, X)
            for c in range(cap):
                src = src_ref[(sender * X + owner) * cap + c]
                acc[j, src] += jnp.dot(
                    adj_ref[j, dx, c], got[dx][j * cap + c], preferred_element_type=F32
                )
        return carry

    lax.fori_loop(0, n, add, 0)
    for j in range(n):
        outs[j][...] = acc[j].astype(BF16)


def spread(offsets, cap, blocks, src, pos, adj, got, starts):
    n = len(offsets)
    return pl.pallas_call(
        functools.partial(
            spread_kernel, offsets, [[(lo, hi) for lo, hi, _ in s] for s in starts], cap
        ),
        in_specs=[SMEM_SPEC, SMEM_SPEC] + [VMEM_SPEC] * (1 + X + sum(len(s) for s in starts)),
        out_specs=[VMEM_SPEC] * n,
        out_shape=[jax.ShapeDtypeStruct((blocks, BS, BS), BF16)] * n,
        scratch_shapes=[pltpu.VMEM((n, blocks, BS, BS), F32)],
        compiler_params=params(8),
        cost_estimate=cost(1.2 * n),
        name="spread",
    )(src, pos, adj, *got, *[a for s in starts for _, _, a in s])


def shift(value, axis, size, by):
    return lax.ppermute(value, axis, [(i, (i + by) % size) for i in range(size)])


def shift_x(values, sign):
    return [values[0]] + [shift(values[d], "x", X, sign * d) for d in range(1, X)]


def exchange(value, axes):
    return lax.all_to_all(value, axes, split_axis=0, concat_axis=0, tiled=True)


def on_device(
    features, w_self, w_neigh, cotangent, src_block, dst_block, block_count, edge_rows, edge_cols
):
    owners, cap = src_block.shape[1:]
    edges = edge_rows.shape[-1]
    local_nodes = features.shape[0]
    blocks = local_nodes // BS
    half = blocks // 2
    groups = Y * C
    node_total = local_nodes * groups * owners
    pos = jnp.stack([lax.axis_index(a) for a in ("z", "x", "y", "c")]).astype(jnp.int32)
    feats = features.reshape(blocks, BS, -1)

    own_src = src_block[0].T
    sent = pack(own_src, dst_block[0].T, block_count, edge_rows, edge_cols)
    lists = exchange(sent, "z")
    src = lists[:, :, edges].reshape(owners * cap)
    tgt = lists[:, :, edges + 1].reshape(1, owners * cap)

    batches = [(0,), (-1, 1), (-2, 2), (-3, 3), (4,)]
    *part, adj = build(batches[0], cap, edges, own_src, pos, sent, [feats], [], own=True)
    sums, adjs = [shift_x(part, 1)], [adj]
    up, down, last = feats, feats, [part[0], lists]
    for k in range(1, 5):
        if k < 4:
            up, down = follow([shift(up, "z", Z, 1), shift(down, "z", Z, -1)], last)
            arrays = [up, down]
        else:
            up, down = shift(up[:half], "z", Z, 1), shift(down[half:], "z", Z, -1)
            arrays = [jnp.concatenate([up, down])]
        after = sums[k - 2][1:] if k > 1 else []
        *part, adj = build(batches[k], cap, edges, src, pos, lists, arrays, after, extra=[tgt] if k == 1 else ())
        sums.append(shift_x(part, 1))
        adjs.append(adj)
        last = part[:1] + (sums[0][1:] if k == 1 else [])
    keeps, sends, tgt = gather_sums(batches, cap, groups * blocks, pos, sum(sums, []))

    arrived = []
    for dy in (2, 1, 3):
        joined = join(keeps[dy], shift(sends[dy], "c", C, 1))
        arrived.append(shift(joined, "y", Y, dy))
    arrived += [keeps[0], shift(sends[0], "c", C, 1)]
    total = sum(a.astype(F32) for a in arrived)
    own_sums, own_cnt = total[:local_nodes], get_counts(total, blocks)
    divisor = jnp.maximum(own_cnt, 1.0).reshape(local_nodes, 1)
    neigh_mean = (own_sums / divisor).astype(BF16)
    preact = jnp.dot(features, w_self, preferred_element_type=F32) + jnp.dot(
        neigh_mean, w_neigh, preferred_element_type=F32
    )
    sigmoids = jax.nn.sigmoid(preact)
    activated = (preact * sigmoids).astype(BF16)
    grad_pre = (cotangent.astype(F32) * sigmoids * (1.0 + preact * (1.0 - sigmoids))).astype(BF16)
    grad_mean = (
        jnp.einsum("nh,fh->nf", grad_pre, w_neigh, preferred_element_type=F32) / divisor
    ).astype(BF16)
    grad_mean = grad_mean.reshape(blocks, BS, -1)
    means = [grad_mean] + [shift(grad_mean, "y", Y, dy) for dy in range(1, Y)]

    both = jnp.concatenate([features, neigh_mean], axis=1)
    grads = jnp.einsum("nf,nh->fh", both, grad_pre, preferred_element_type=F32)
    rows = grads.shape[0] // owners
    piece = jnp.sum(exchange(grads, ("z", "x")).reshape(owners, rows, -1), axis=0)
    first_piece = piece
    means[1:] = follow(means[1:], [first_piece])
    means = [m for mean in means for m in (mean, shift(mean, "c", C, 1))]
    piece = jnp.broadcast_to(piece[None], (groups, rows, piece.shape[1]))
    piece = jnp.sum(exchange(piece, ("y", "c")), axis=0)
    sets = [(4,), (-3, 3), (-2, 2), (-1, 1), (0,)]
    picked = pick(sets, cap, tgt, pos, means, first_piece)
    grads = exchange(jnp.broadcast_to(piece[None], (owners, rows, piece.shape[1])), ("z", "x"))
    grads = grads.reshape(owners * rows, -1) * float(node_total) ** (-0.5)

    own_term = jnp.einsum("nh,fh->nf", grad_pre, w_self, preferred_element_type=F32)
    own_term = own_term.reshape(blocks, BS, -1)

    got = [shift_x(p, -1) for p in picked]

    def back(k, starts):
        return spread(batches[k], cap, blocks, src, pos, adjs[k], got[4 - k], starts)

    (far,) = back(4, [[]])
    up, down = shift(far[:half], "z", Z, 1), shift(far[half:], "z", Z, -1)
    down, up = back(3, [[(half, blocks, down)], [(0, half, up)]])
    for k in (2, 1):
        up, down = shift(up, "z", Z, 1), shift(down, "z", Z, -1)
        down, up = back(k, [[(0, blocks, down)], [(0, blocks, up)]])
    up, down = shift(up, "z", Z, 1), shift(down, "z", Z, -1)
    (grad_features,) = back(0, [[(0, blocks, own_term), (0, blocks, up), (0, blocks, down)]])
    f = features.shape[1]
    return activated, grad_features.reshape(local_nodes, -1), grads[:f], grads[f:]


def solution(mesh):
    mesh = Mesh(mesh.devices.reshape(Y, C, Z, X), ("y", "c", "z", "x"))
    every = ("y", "c", "z", "x")
    return jax.shard_map(
        on_device,
        mesh=mesh,
        in_specs=(
            P(every, None),
            P(),
            P(),
            P(every, None),
            P(every, None, None),
            P(every, None, None),
            P(every, None),
            P(every, None, None, None),
            P(every, None, None, None),
        ),
        out_specs=(P(every, None), P(every, None), P(), P()),
        check_vma=False,
    )
```

```python
import functools

import jax
import jax.numpy as jnp
from jax import lax
from jax.experimental import pallas as pl
from jax.experimental.pallas import tpu as pltpu
from jax.sharding import Mesh, PartitionSpec as P

BS = 128
TAIL = 16
Y, C, Z, X = 4, 2, 8, 4
F32 = jnp.float32
BF16 = jnp.bfloat16
MIB = 1024 * 1024
NT = (((1,), (1,)), ((), ()))
SMEM_SPEC = pl.BlockSpec(memory_space=pltpu.SMEM)
VMEM_SPEC = pl.BlockSpec(memory_space=pltpu.VMEM)
ANY_SPEC = pl.BlockSpec(memory_space=pl.ANY)
LISTS = 256
META = 64


def dot_nt(a, b):
    return lax.dot_general(a, b, NT, preferred_element_type=F32)


def params(mib):
    return pltpu.CompilerParams(vmem_limit_bytes=mib * MIB)


def cost(us):
    return pl.CostEstimate(flops=0, bytes_accessed=int(us * 3.5e6), transcendentals=0)


def one_hot_t(row, extent):
    ids = lax.broadcasted_iota(jnp.int32, (extent, row.shape[1]), 0)
    return jnp.where(ids == row, 1.0, 0.0).astype(BF16)


def copy_meta(list_ref, z, offsets, smem, sem):
    copies = []
    for j, off in enumerate(offsets):
        row = lax.rem(z + off + Z, Z) * X
        piece = list_ref.at[pl.ds(row, X), :, pl.ds(LISTS - BS, BS)]
        copies.append(pltpu.make_async_copy(piece, smem.at[j], sem.at[j]))
        copies[-1].start()
    return copies


def build_kernel(offsets, cap, edges, static, n_feats, after, pos_ref, list_ref, *refs):
    n = len(offsets)
    feats, refs = refs[:n_feats], refs[n_feats + after :]
    sums, (adj_out, adj_ref, smem, sem, out_sem) = refs[:X], refs[X:]
    z, x = pos_ref[0], pos_ref[1]
    edge_row = lax.broadcasted_iota(jnp.int32, (TAIL, edges), 0)
    row_id = lax.broadcasted_iota(jnp.int32, (TAIL, BS), 0)
    for copy in copy_meta(list_ref, z, offsets, smem, sem):
        copy.wait()

    def block_of(j, src):
        if n_feats == n:
            return feats[j][src]
        low, high = feats
        half = low.shape[0]
        return jnp.where(src < half, low[jnp.minimum(src, half - 1)], high[jnp.maximum(src - half, 0)])

    def slots(dx):
        owner = lax.rem(x + dx, X)
        tail = jnp.zeros((TAIL, BS), F32)
        parts = []
        for j, off in enumerate(offsets):
            packed = list_ref[lax.rem(z + off + Z, Z) * X + owner]
            for c in range(cap):
                k = j * cap + c
                e = packed[c : c + 1, :edges]
                rt = one_hot_t(lax.shift_right_logical(e, 7), BS)
                ct = one_hot_t(jnp.bitwise_and(e, BS - 1), BS)
                a = dot_nt(rt, ct).astype(BF16)
                adj_ref[dx, j * cap + c] = dot_nt(ct, rt).astype(BF16)
                block = block_of(j, smem[j, owner, c, META])
                parts.append(jnp.dot(a, block, preferred_element_type=F32).astype(BF16))
                pick = jnp.where(edge_row == k, 1.0, 0.0).astype(BF16)
                tail = tail + dot_nt(pick, rt)
                to = smem[j, owner, c, META + 1].astype(F32)
                tail = jnp.where(row_id == n * cap + k, to, tail)
        return parts + [tail.astype(BF16)]

    def store(out, parts):
        for k, part in enumerate(parts):
            out[k * BS : k * BS + part.shape[0], :] = part

    def keep(dx):
        return pltpu.make_async_copy(adj_ref.at[dx], adj_out.at[dx], out_sem.at[dx])

    if static:
        for d in range(X):
            store(sums[d], slots(d))
            keep(d).start()
    else:

        def step(dx, carry):
            parts = slots(dx)
            for d in range(X):
                pl.when(dx == d)(functools.partial(store, sums[d], parts))
            keep(dx).start()
            return carry

        lax.fori_loop(0, X, step, 0)
    for d in range(X):
        keep(d).wait()


def build(offsets, cap, edges, pos, edge_list, feats, after=(), static=False):
    n = len(offsets)
    return pl.pallas_call(
        functools.partial(build_kernel, offsets, cap, edges, static, len(feats), len(after)),
        in_specs=[SMEM_SPEC] + [VMEM_SPEC] * (1 + len(feats)) + [ANY_SPEC] * len(after),
        out_specs=[VMEM_SPEC] * X + [ANY_SPEC],
        out_shape=[jax.ShapeDtypeStruct((n * cap * BS + TAIL, BS), BF16)] * X
        + [jax.ShapeDtypeStruct((X, n * cap, BS, BS), BF16)],
        scratch_shapes=[
            pltpu.VMEM((X, n * cap, BS, BS), BF16),
            pltpu.SMEM((n, X, cap, BS), jnp.int32),
            pltpu.SemaphoreType.DMA((n,)),
            pltpu.SemaphoreType.DMA((X,)),
        ],
        compiler_params=params(8),
        cost_estimate=cost(2.5 * n),
        name="build",
    )(pos, edge_list, *feats, *after)


def pack_kernel(cap, edges, src_ref, dst_ref, used_ref, rows_ref, cols_ref, lists_ref):
    owners = rows_ref.shape[1]
    rest = LISTS - edges
    meta_slot = lax.broadcasted_iota(jnp.int32, (cap, rest), 0)
    meta_lane = lax.broadcasted_iota(jnp.int32, (cap, rest), 1)
    slot = lax.broadcasted_iota(jnp.int32, (cap, edges), 0)

    def pack(o, carry):
        packed = rows_ref[0, o] * BS + cols_ref[0, o]
        meta = jnp.zeros((cap, rest), jnp.int32)
        for c in range(cap):
            to = jnp.where(c < used_ref[0, o], dst_ref[c, o], -1)
            packed = jnp.where(jnp.logical_and(slot == c, to < 0), BS * BS, packed)
            value = jnp.where(meta_lane == 0, src_ref[c, o], to)
            meta = jnp.where(meta_slot == c, value, meta)
        lists_ref[o, :, :edges] = packed
        lists_ref[o, :, edges:] = meta
        return carry

    lax.fori_loop(0, owners, pack, 0, unroll=4)


def pack(src, dst, used, rows, cols):
    owners, cap, edges = rows.shape[1:]
    whole = pl.BlockSpec(rows.shape, lambda i: (0, 0, 0, 0))
    return pl.pallas_call(
        functools.partial(pack_kernel, cap, edges),
        grid=(1,),
        in_specs=[SMEM_SPEC] * 3 + [whole] * 2,
        out_specs=VMEM_SPEC,
        out_shape=jax.ShapeDtypeStruct((owners, cap, LISTS), jnp.int32),
        compiler_params=params(4),
        cost_estimate=cost(2),
        name="pack",
    )(src, dst, used, rows, cols)


def follow(arrays, after):
    n = len(arrays)
    return pl.pallas_call(
        lambda *refs: None,
        in_specs=[ANY_SPEC] * (n + len(after)),
        out_specs=[ANY_SPEC] * n,
        out_shape=[jax.ShapeDtypeStruct(a.shape, a.dtype) for a in arrays],
        input_output_aliases={i: i for i in range(n)},
        compiler_params=params(1),
        cost_estimate=cost(0.3),
        name="follow",
    )(*arrays, *after)


def gather_kernel(sizes, cap, pos_ref, *refs):
    total = len(sizes) * X
    got, refs = refs[:total], refs[total:]
    keeps, sends, (tgt_out, acc, acc_c, tgt_ref, sem) = refs[:Y], refs[Y : 2 * Y], refs[2 * Y :]
    targets = acc.shape[0]
    y, core = pos_ref[2], pos_ref[3]
    lane = lax.broadcasted_iota(jnp.int32, tgt_out.shape, 1)
    tgt = jnp.zeros(tgt_out.shape, F32)
    for a, ref in enumerate(got):
        n = sizes[a // X] * cap
        rows = ref[n * BS :, :].astype(F32)[n : 2 * n, :]
        if n < tgt_out.shape[0]:
            rows = jnp.concatenate([rows, rows], axis=0)
        tgt = jnp.where(lane == a, rows, tgt)
    tgt_out[...] = tgt.astype(jnp.int32)
    copy = pltpu.make_async_copy(tgt_out, tgt_ref, sem)
    copy.start()

    def clear(i, carry):
        acc[i] = jnp.zeros((BS, BS), F32)
        return carry

    lax.fori_loop(0, targets, clear, 0, unroll=4)
    acc_c[...] = jnp.zeros_like(acc_c)
    copy.wait()
    for a, ref in enumerate(got):
        n = sizes[a // X] * cap
        tail = ref[n * BS :, :].astype(F32)
        for k in range(n):
            t = tgt_ref[k, a]

            @pl.when(t >= 0)
            def _(ref=ref, tail=tail, k=k, t=t):
                acc[t] += ref[k * BS : (k + 1) * BS, :].astype(F32)
                acc_c[pl.ds(t, 1), :] += tail[k : k + 1, :]

    blocks = targets // (Y * C)
    for dy in range(Y):
        for out, to_core in ((keeps[dy], core), (sends[dy], 1 - core)):
            first = (lax.rem(y + dy, Y) * C + to_core) * blocks

            def store(i, carry, out=out, first=first):
                out[pl.ds(pl.multiple_of(i * BS, BS), BS), :] = acc[first + i].astype(BF16)
                return carry

            lax.fori_loop(0, blocks, store, 0, unroll=4)
            count = acc_c[pl.ds(pl.multiple_of(first, blocks), blocks), :]
            put_counts(out, count, blocks)


def put_counts(out, count, blocks):
    high = jnp.floor(count * (1.0 / 256.0))
    out[blocks * BS : blocks * (BS + 1), :] = high.astype(BF16)
    out[blocks * (BS + 1) :, :] = (count - 256.0 * high).astype(BF16)


def get_counts(total, blocks):
    return 256.0 * total[blocks * BS : blocks * (BS + 1)] + total[blocks * (BS + 1) :]


def gather_sums(sizes, cap, targets, pos, got):
    blocks = targets // (Y * C)
    part = jax.ShapeDtypeStruct((blocks * (BS + 2), BS), BF16)
    out = pl.pallas_call(
        functools.partial(gather_kernel, sizes, cap),
        in_specs=[SMEM_SPEC] + [VMEM_SPEC] * len(got),
        out_specs=[VMEM_SPEC] * (2 * Y + 1),
        out_shape=[part] * (2 * Y) + [jax.ShapeDtypeStruct((2 * cap, BS), jnp.int32)],
        scratch_shapes=[
            pltpu.VMEM((targets, BS, BS), F32),
            pltpu.VMEM((targets, BS), F32),
            pltpu.SMEM((2 * cap, BS), jnp.int32),
            pltpu.SemaphoreType.DMA,
        ],
        compiler_params=params(16),
        cost_estimate=cost(5),
        name="gather_sums",
    )(pos, *got)
    return out[:Y], out[Y : 2 * Y], out[2 * Y]


def join_kernel(a_ref, b_ref, out_ref):
    blocks = out_ref.shape[0] // (BS + 2)

    def add(i, carry):
        rows = pl.ds(pl.multiple_of(i * BS, BS), BS)
        out_ref[rows, :] = (a_ref[rows, :].astype(F32) + b_ref[rows, :].astype(F32)).astype(BF16)
        return carry

    lax.fori_loop(0, blocks, add, 0, unroll=2)
    digits = slice(blocks * BS, None)
    total = a_ref[digits, :].astype(F32) + b_ref[digits, :].astype(F32)
    put_counts(out_ref, 256.0 * total[:blocks] + total[blocks:], blocks)


def join(a, b):
    return pl.pallas_call(
        join_kernel,
        in_specs=[VMEM_SPEC] * 2,
        out_specs=VMEM_SPEC,
        out_shape=jax.ShapeDtypeStruct(a.shape, BF16),
        compiler_params=params(4),
        cost_estimate=cost(0.6),
        name="join",
    )(a, b)


def pick_kernel(sets, near, cap, tgt_ref, pos_ref, *refs):
    means, outs = refs[: Y * C], refs[Y * C + 1 : -3]
    mean_ref, in_sem, out_sem = refs[-3:]
    y, core = pos_ref[2], pos_ref[3]
    blocks = means[0].shape[0]
    copies = []
    for i, ref in enumerate(means):
        from_core = core if i % C == 0 else 1 - core
        first = (lax.rem(y - i // C + Y, Y) * C + from_core) * blocks
        copies.append(
            pltpu.make_async_copy(ref, mean_ref.at[pl.ds(first, blocks)], in_sem.at[i])
        )
        copies[-1].start()
    for copy in copies:
        copy.wait()
    copies = []
    for i in sorted(range(len(sets)), key=lambda i: i < near):
        for dx in range(X):
            out = outs[i * X + dx]
            payload, n = sets[i]
            for k in range(n * cap):
                t = jnp.maximum(tgt_ref[k, payload * X + dx], 0)
                if i < near:
                    out[k] = mean_ref[t]
                else:
                    copies.append(
                        pltpu.make_async_copy(mean_ref.at[t], out.at[k], out_sem.at[len(copies)])
                    )
                    copies[-1].start()
    for copy in copies:
        copy.wait()


def pick(sets, near, cap, tgt, pos, means, after):
    shapes = [jax.ShapeDtypeStruct((n * cap, BS, BS), BF16) for _, n in sets for _ in range(X)]
    far = sum(n for _, n in sets[near:]) * X * cap
    out = pl.pallas_call(
        functools.partial(pick_kernel, sets, near, cap),
        in_specs=[SMEM_SPEC, SMEM_SPEC] + [ANY_SPEC] * (len(means) + 1),
        out_specs=[VMEM_SPEC] * (near * X) + [ANY_SPEC] * ((len(sets) - near) * X),
        out_shape=shapes,
        scratch_shapes=[
            pltpu.VMEM((len(means) * means[0].shape[0], BS, BS), BF16),
            pltpu.SemaphoreType.DMA((len(means),)),
            pltpu.SemaphoreType.DMA((far,)),
        ],
        compiler_params=params(8),
        cost_estimate=cost(3),
        name="pick",
    )(tgt, pos, *means, after)
    return [out[i * X : (i + 1) * X] for i in range(len(sets))]


def spread_kernel(offsets, starts, cap, cuts, pos_ref, list_ref, adj_ref, *refs):
    n = len(offsets)
    got, refs = refs[:X], refs[X:]
    inits = []
    for parts in starts:
        inits.append([(lo, hi, refs[i]) for i, (lo, hi) in enumerate(parts)])
        refs = refs[len(parts) :]
    outs, (acc, smem, sem) = refs[: len(cuts)], refs[len(cuts) :]
    blocks = acc.shape[1]
    z, x = pos_ref[0], pos_ref[1]
    copies = copy_meta(list_ref, z, offsets, smem, sem)
    for j in range(n):
        if len(inits[j]) == 0 or inits[j][0][:2] != (0, blocks):
            acc[j] = jnp.zeros(acc.shape[1:], F32)
        for i, (lo, hi, ref) in enumerate(inits[j]):
            if i == 0:
                acc[j, lo:hi] = ref[...].astype(F32)
            else:
                acc[j, lo:hi] += ref[...].astype(F32)
    for copy in copies:
        copy.wait()

    def add(j, carry):
        for dx in range(X):
            owner = lax.rem(x + dx, X)
            for c in range(cap):
                src = smem[j, owner, c, META]
                acc[j, src] += jnp.dot(
                    adj_ref[dx, j * cap + c], got[dx][j * cap + c], preferred_element_type=F32
                )
        return carry

    lax.fori_loop(0, n, add, 0)
    for out, (j, lo, hi) in zip(outs, cuts):
        out[...] = acc[j, lo:hi].astype(BF16)


def spread(offsets, cap, blocks, lists, pos, adj, got, starts, cuts=None):
    n = len(offsets)
    cuts = [(j, 0, blocks) for j in range(n)] if cuts is None else cuts
    return pl.pallas_call(
        functools.partial(
            spread_kernel, offsets, [[(lo, hi) for lo, hi, _ in s] for s in starts], cap, cuts
        ),
        in_specs=[SMEM_SPEC, ANY_SPEC] + [VMEM_SPEC] * (1 + X + sum(len(s) for s in starts)),
        out_specs=[VMEM_SPEC] * len(cuts),
        out_shape=[jax.ShapeDtypeStruct((hi - lo, BS, BS), BF16) for _, lo, hi in cuts],
        scratch_shapes=[
            pltpu.VMEM((n, blocks, BS, BS), F32),
            pltpu.SMEM((n, X, cap, BS), jnp.int32),
            pltpu.SemaphoreType.DMA((n,)),
        ],
        compiler_params=params(8),
        cost_estimate=cost(1.2 * n),
        name="spread",
    )(pos, lists, adj, *got, *[a for s in starts for _, _, a in s])


def halves(up, down):
    half = up.shape[0] // 2

    def kernel(up_ref, down_ref, low_ref, high_ref):
        low_ref[...] = up_ref[:half]
        high_ref[...] = down_ref[half:]

    return pl.pallas_call(
        kernel,
        in_specs=[VMEM_SPEC] * 2,
        out_specs=[VMEM_SPEC] * 2,
        out_shape=[jax.ShapeDtypeStruct((half,) + up.shape[1:], up.dtype)] * 2,
        compiler_params=params(4),
        cost_estimate=cost(0.3),
        name="halves",
    )(up, down)


def sum_copies(parts, copies):
    def kernel(in_ref, out_ref):
        total = jnp.sum(in_ref[...], axis=0)
        for i in range(copies):
            out_ref[i] = total

    return pl.pallas_call(
        kernel,
        in_specs=[VMEM_SPEC],
        out_specs=VMEM_SPEC,
        out_shape=jax.ShapeDtypeStruct((copies,) + parts.shape[1:], F32),
        compiler_params=params(4),
        cost_estimate=cost(0.5),
        name="sum_copies",
    )(parts)


def scale_split(grads, scale):
    rows, width = grads.shape
    half = rows // 2

    def kernel(in_ref, a_ref, b_ref):
        a_ref[...] = in_ref[:half] * scale
        b_ref[...] = in_ref[half:] * scale

    return pl.pallas_call(
        kernel,
        in_specs=[VMEM_SPEC],
        out_specs=[VMEM_SPEC] * 2,
        out_shape=[jax.ShapeDtypeStruct((half, width), F32)] * 2,
        compiler_params=params(4),
        cost_estimate=cost(0.5),
        name="scale_split",
    )(grads)


def own_part(grad_pre, w_self, blocks):
    def kernel(grad_ref, w_ref, out_ref):
        for i in range(blocks):
            out_ref[i] = dot_nt(grad_ref[i * BS : (i + 1) * BS, :], w_ref[...])

    return pl.pallas_call(
        kernel,
        in_specs=[VMEM_SPEC] * 2,
        out_specs=VMEM_SPEC,
        out_shape=jax.ShapeDtypeStruct((blocks, BS, BS), F32),
        compiler_params=params(8),
        cost_estimate=cost(1.5),
        name="own_part",
    )(grad_pre, w_self)


def shift(value, axis, size, by):
    return lax.ppermute(value, axis, [(i, (i + by) % size) for i in range(size)])


def shift_x(values, sign):
    return [values[0]] + [shift(values[d], "x", X, sign * d) for d in range(1, X)]


def exchange(value, axes):
    return lax.all_to_all(value, axes, split_axis=0, concat_axis=0, tiled=True)


def on_device(
    features, w_self, w_neigh, cotangent, src_block, dst_block, block_count, edge_rows, edge_cols
):
    owners, cap = src_block.shape[1:]
    edges = edge_rows.shape[-1]
    local_nodes = features.shape[0]
    blocks = local_nodes // BS
    half = blocks // 2
    groups = Y * C
    node_total = local_nodes * groups * owners
    pos = jnp.stack([lax.axis_index(a) for a in ("z", "x", "y", "c")]).astype(jnp.int32)
    feats = features.reshape(blocks, BS, -1)

    sent = pack(src_block[0].T, dst_block[0].T, block_count, edge_rows, edge_cols)
    lists = exchange(sent, "z")

    batches = [(0,), (-1, 1), (-2, 2), (-3, 3), (4,)]
    *part, adj = build(batches[0], cap, edges, pos, sent, [feats])
    sums, adjs = [shift_x(part, 1)], [adj]
    up, down, last = feats, feats, [part[0], lists]
    for k in range(1, 5):
        if k < 4:
            up, down = follow([shift(up, "z", Z, 1), shift(down, "z", Z, -1)], last)
            arrays = [up, down]
        else:
            low, high = halves(up, down)
            arrays = [shift(low, "z", Z, 1), shift(high, "z", Z, -1)]
        after = sums[k - 2][1:] if k > 1 else []
        *part, adj = build(
            batches[k],
            cap,
            edges,
            pos,
            lists,
            arrays,
            after,
            static=k == 1,
        )
        sums.append(shift_x(part, 1))
        adjs.append(adj)
        last = part[:1] + (sums[0][1:] if k == 1 else [])
    keeps, sends, tgt = gather_sums(
        [len(b) for b in batches], cap, groups * blocks, pos, sum(sums, [])
    )

    arrived = []
    for dy in (2, 1, 3):
        joined = join(keeps[dy], shift(sends[dy], "c", C, 1))
        arrived.append(shift(joined, "y", Y, dy))
    arrived += [keeps[0], shift(sends[0], "c", C, 1)]
    total = sum(a.astype(F32) for a in arrived)
    own_sums, own_cnt = total[:local_nodes], get_counts(total, blocks)
    divisor = jnp.maximum(own_cnt, 1.0).reshape(local_nodes, 1)
    neigh_mean = (own_sums / divisor).astype(BF16)
    preact = jnp.dot(features, w_self, preferred_element_type=F32) + jnp.dot(
        neigh_mean, w_neigh, preferred_element_type=F32
    )
    sigmoids = jax.nn.sigmoid(preact)
    activated = (preact * sigmoids).astype(BF16)
    grad_pre = (cotangent.astype(F32) * sigmoids * (1.0 + preact * (1.0 - sigmoids))).astype(BF16)
    grad_mean = (
        jnp.einsum("nh,fh->nf", grad_pre, w_neigh, preferred_element_type=F32) / divisor
    ).astype(BF16)
    grad_mean = grad_mean.reshape(blocks, BS, -1)
    means = [grad_mean] + [shift(grad_mean, "y", Y, dy) for dy in range(1, Y)]

    both = jnp.concatenate([features, neigh_mean], axis=1)
    grads = jnp.einsum("nf,nh->fh", both, grad_pre, preferred_element_type=F32)
    piece = sum_copies(exchange(grads, ("z", "x")).reshape(owners, -1, grads.shape[1]), groups)
    first_piece = piece
    means[1:] = follow(means[1:], [first_piece])
    means = [m for mean in means for m in (mean, shift(mean, "c", C, 1))]
    sets = [(k, len(batches[k])) for k in (4, 3, 2, 1, 0)]
    picked = pick(sets, 2, cap, tgt, pos, means, first_piece)
    piece = sum_copies(exchange(piece, ("y", "c")), owners)
    grads = exchange(piece, ("z", "x")).reshape(grads.shape)

    own_term = own_part(grad_pre, w_self, blocks)
    got = [shift_x(p, -1) for p in picked]

    def back(k, starts, cuts=None):
        return spread(batches[k], cap, blocks, lists, pos, adjs[k], got[4 - k], starts, cuts)

    low, high = back(4, [[]], [(0, 0, half), (0, half, blocks)])
    up, down = shift(low, "z", Z, 1), shift(high, "z", Z, -1)
    down, up = back(3, [[(half, blocks, down)], [(0, half, up)]])
    for k in (2, 1):
        up, down = shift(up, "z", Z, 1), shift(down, "z", Z, -1)
        down, up = back(k, [[(0, blocks, down)], [(0, blocks, up)]])
    up, down = shift(up, "z", Z, 1), shift(down, "z", Z, -1)
    (grad_features,) = back(0, [[(0, blocks, own_term), (0, blocks, up), (0, blocks, down)]])
    grad_self, grad_neigh = scale_split(grads, float(node_total) ** (-0.5))
    return activated, grad_features.reshape(local_nodes, -1), grad_self, grad_neigh


def solution(mesh):
    mesh = Mesh(mesh.devices.reshape(Y, C, Z, X), ("y", "c", "z", "x"))
    every = ("y", "c", "z", "x")
    return jax.shard_map(
        on_device,
        mesh=mesh,
        in_specs=(
            P(every, None),
            P(),
            P(),
            P(every, None),
            P(every, None, None),
            P(every, None, None),
            P(every, None),
            P(every, None, None, None),
            P(every, None, None, None),
        ),
        out_specs=(P(every, None), P(every, None), P(), P()),
        check_vma=False,
    )
```

```python
import functools

import jax
import jax.numpy as jnp
from jax import lax
from jax.experimental import pallas as pl
from jax.experimental.pallas import tpu as pltpu
from jax.sharding import Mesh, PartitionSpec as P

BS = 128
TAIL = 16
Y, C, Z, X = 4, 2, 8, 4
F32 = jnp.float32
BF16 = jnp.bfloat16
MIB = 1024 * 1024
NT = (((1,), (1,)), ((), ()))
SMEM_SPEC = pl.BlockSpec(memory_space=pltpu.SMEM)
VMEM_SPEC = pl.BlockSpec(memory_space=pltpu.VMEM)
ANY_SPEC = pl.BlockSpec(memory_space=pl.ANY)
LISTS = 256


def dot_nt(a, b):
    return lax.dot_general(a, b, NT, preferred_element_type=F32)


def params(mib):
    return pltpu.CompilerParams(vmem_limit_bytes=mib * MIB)


def cost(us):
    return pl.CostEstimate(flops=0, bytes_accessed=int(us * 3.5e6), transcendentals=0)


def one_hot_t(row, extent):
    ids = lax.broadcasted_iota(jnp.int32, (extent, row.shape[1]), 0)
    return jnp.where(ids == row, 1.0, 0.0).astype(BF16)


def build_batch(offsets, cap, edges, src_of, z, x, edge_ref, feats, sum_refs, adj_ref, tgt_ref=None):
    n = len(offsets)

    def block_of(j, src):
        if len(feats) == n:
            return feats[j][src]
        low, high = feats
        half = low.shape[0]
        return jnp.where(src < half, low[jnp.minimum(src, half - 1)], high[jnp.maximum(src - half, 0)])


    def owner_step(dx, carry):
        owner = lax.rem(x + dx, X)
        counts = jnp.zeros((TAIL, BS), F32)
        if tgt_ref is not None:
            last = lax.broadcasted_iota(jnp.int32, (TAIL, BS), 0) == TAIL - 1
            counts = jnp.where(last, tgt_ref[...].astype(F32), 0.0)
        parts = []
        for j, off in enumerate(offsets):
            row = lax.rem(z + off + Z, Z) * X + owner
            packed = edge_ref[row]
            for c in range(cap):
                k = j * cap + c
                e = packed[c : c + 1, :edges]
                rt = one_hot_t(lax.shift_right_logical(e, 7), BS)
                ct = one_hot_t(jnp.bitwise_and(e, BS - 1), BS)
                a = dot_nt(rt, ct).astype(BF16)
                adj_ref[j, dx, c] = dot_nt(ct, rt).astype(BF16)
                part = jnp.dot(a, block_of(j, src_of(row, c)), preferred_element_type=F32)
                parts.append(part.astype(BF16))
                pick = jnp.where(
                    lax.broadcasted_iota(jnp.int32, (TAIL, edges), 0) == k, 1.0, 0.0
                ).astype(BF16)
                counts = counts + dot_nt(pick, rt)
        parts.append(counts.astype(BF16))
        for d, out in enumerate(sum_refs):

            @pl.when(dx == d)
            def _(out=out):
                for k, part in enumerate(parts):
                    out[k * BS : k * BS + part.shape[0], :] = part

        return carry

    lax.fori_loop(0, X, owner_step, 0)


def batch_shapes(n, cap):
    return [jax.ShapeDtypeStruct((n * cap * BS + TAIL, BS), BF16)] * X + [
        jax.ShapeDtypeStruct((n, X, cap, BS, BS), BF16)
    ]


def pack_kernel(cap, edges, src_ref, dst_ref, used_ref, rows_ref, cols_ref, lists_ref):
    owners = rows_ref.shape[1]
    rest = LISTS - edges
    meta_slot = lax.broadcasted_iota(jnp.int32, (cap, rest), 0)
    meta_lane = lax.broadcasted_iota(jnp.int32, (cap, rest), 1)
    slot = lax.broadcasted_iota(jnp.int32, (cap, edges), 0)

    def pack(o, carry):
        packed = rows_ref[0, o] * BS + cols_ref[0, o]
        meta = jnp.zeros((cap, rest), jnp.int32)
        for c in range(cap):
            to = jnp.where(c < used_ref[0, o], dst_ref[c, o], -1)
            packed = jnp.where(jnp.logical_and(slot == c, to < 0), BS * BS, packed)
            value = jnp.where(meta_lane == 0, src_ref[c, o], to)
            meta = jnp.where(meta_slot == c, value, meta)
        lists_ref[o, :, :edges] = packed
        lists_ref[o, :, edges:] = meta
        return carry

    lax.fori_loop(0, owners, pack, 0, unroll=4)


def pack(src, dst, used, rows, cols):
    owners, cap, edges = rows.shape[1:]
    whole = pl.BlockSpec(rows.shape, lambda i: (0, 0, 0, 0))
    return pl.pallas_call(
        functools.partial(pack_kernel, cap, edges),
        grid=(1,),
        in_specs=[SMEM_SPEC] * 3 + [whole] * 2,
        out_specs=VMEM_SPEC,
        out_shape=jax.ShapeDtypeStruct((owners, cap, LISTS), jnp.int32),
        compiler_params=params(4),
        cost_estimate=cost(2),
        name="pack",
    )(src, dst, used, rows, cols)


def build_kernel(offsets, cap, edges, own, n_feats, extra, after, src_ref, pos_ref, edge_ref, *refs):
    feats, refs = refs[:n_feats], refs[n_feats:]
    tgt_ref = refs[0] if extra else None
    refs = refs[extra + after :]

    def src_of(row, c):
        if own:
            return src_ref[c, row]
        return src_ref[row * cap + c]

    build_batch(
        offsets,
        cap,
        edges,
        src_of,
        pos_ref[0],
        pos_ref[1],
        edge_ref,
        feats,
        refs[:X],
        refs[X],
        tgt_ref,
    )


def build(offsets, cap, edges, src, pos, edge_list, feats, after, own=False, extra=()):
    n = len(offsets)
    return pl.pallas_call(
        functools.partial(
            build_kernel, offsets, cap, edges, own, len(feats), len(extra), len(after)
        ),
        in_specs=[SMEM_SPEC, SMEM_SPEC] + [VMEM_SPEC] * (1 + len(feats) + len(extra)) + [ANY_SPEC] * len(after),
        out_specs=[VMEM_SPEC] * (X + 1),
        out_shape=batch_shapes(n, cap),
        compiler_params=params(8),
        cost_estimate=cost(2.5 * n),
        name="build",
    )(src, pos, edge_list, *feats, *extra, *after)


def follow(arrays, after):
    n = len(arrays)
    return pl.pallas_call(
        lambda *refs: None,
        in_specs=[ANY_SPEC] * (n + len(after)),
        out_specs=[ANY_SPEC] * n,
        out_shape=[jax.ShapeDtypeStruct(a.shape, a.dtype) for a in arrays],
        input_output_aliases={i: i for i in range(n)},
        compiler_params=params(1),
        cost_estimate=cost(0.3),
        name="follow",
    )(*arrays, *after)


def gather_kernel(batches, cap, pos_ref, *refs):
    total = len(batches) * X
    got, refs = refs[:total], refs[total:]
    keeps, sends, (tgt_out, acc, acc_c, tgt_ref, sem) = refs[:Y], refs[Y : 2 * Y], refs[2 * Y :]
    targets = acc.shape[0]
    z, x, y, core = pos_ref[0], pos_ref[1], pos_ref[2], pos_ref[3]
    rows = [got[2 * X + d][-TAIL:, :].astype(F32)[TAIL - 1 :, :] for d in range(X)]
    tgt_out[...] = jnp.concatenate(rows + rows, axis=0).astype(jnp.int32)
    copy = pltpu.make_async_copy(tgt_out, tgt_ref, sem)
    copy.start()

    def clear(i, carry):
        acc[i] = jnp.zeros((BS, BS), F32)
        return carry

    lax.fori_loop(0, targets, clear, 0, unroll=4)
    acc_c[...] = jnp.zeros_like(acc_c)
    copy.wait()
    for b, offsets in enumerate(batches):
        n = len(offsets)
        for dx in range(X):
            ref = got[b * X + dx]
            tail = ref[n * cap * BS :, :].astype(F32)
            first = lax.rem(z + offsets[0] + Z, Z)
            apart = offsets[-1] - offsets[0]

            def add(j, carry, ref=ref, dx=dx, tail=tail, first=first, apart=apart):
                sender_z = lax.rem(first + j * apart, Z)
                for c in range(cap):
                    k = j * cap + c
                    t = tgt_ref[dx, (sender_z * X + x) * cap + c]

                    @pl.when(t >= 0)
                    def _():
                        rows = ref[pl.ds(pl.multiple_of(k * BS, BS), BS), :]
                        acc[t] += rows.astype(F32)
                        here = lax.broadcasted_iota(jnp.int32, tail.shape, 0) == k
                        count = jnp.sum(jnp.where(here, tail, 0.0), axis=0, keepdims=True)
                        acc_c[pl.ds(t, 1), :] += count

                return carry

            lax.fori_loop(0, n, add, 0)

    blocks = targets // (Y * C)
    for dy in range(Y):
        for out, to_core in ((keeps[dy], core), (sends[dy], 1 - core)):
            first = (lax.rem(y + dy, Y) * C + to_core) * blocks

            def store(i, carry, out=out, first=first):
                out[pl.ds(pl.multiple_of(i * BS, BS), BS), :] = acc[first + i].astype(BF16)
                return carry

            lax.fori_loop(0, blocks, store, 0, unroll=4)
            count = acc_c[pl.ds(pl.multiple_of(first, blocks), blocks), :]
            put_counts(out, count, blocks)


def put_counts(out, count, blocks):
    high = jnp.floor(count * (1.0 / 256.0))
    out[blocks * BS : blocks * (BS + 1), :] = high.astype(BF16)
    out[blocks * (BS + 1) :, :] = (count - 256.0 * high).astype(BF16)


def get_counts(total, blocks):
    return 256.0 * total[blocks * BS : blocks * (BS + 1)] + total[blocks * (BS + 1) :]


def gather_sums(batches, cap, targets, pos, got):
    blocks = targets // (Y * C)
    part = jax.ShapeDtypeStruct((blocks * (BS + 2), BS), BF16)
    out = pl.pallas_call(
        functools.partial(gather_kernel, batches, cap),
        in_specs=[SMEM_SPEC] + [VMEM_SPEC] * len(got),
        out_specs=[VMEM_SPEC] * (2 * Y + 1),
        out_shape=[part] * (2 * Y) + [jax.ShapeDtypeStruct((2 * X, BS), jnp.int32)],
        scratch_shapes=[
            pltpu.VMEM((targets, BS, BS), F32),
            pltpu.VMEM((targets, BS), F32),
            pltpu.SMEM((2 * X, BS), jnp.int32),
            pltpu.SemaphoreType.DMA,
        ],
        compiler_params=params(16),
        cost_estimate=cost(5),
        name="gather_sums",
    )(pos, *got)
    return out[:Y], out[Y : 2 * Y], out[2 * Y]


def join_kernel(a_ref, b_ref, out_ref):
    blocks = out_ref.shape[0] // (BS + 2)

    def add(i, carry):
        rows = pl.ds(pl.multiple_of(i * BS, BS), BS)
        out_ref[rows, :] = (a_ref[rows, :].astype(F32) + b_ref[rows, :].astype(F32)).astype(BF16)
        return carry

    lax.fori_loop(0, blocks, add, 0, unroll=2)
    digits = slice(blocks * BS, None)
    total = a_ref[digits, :].astype(F32) + b_ref[digits, :].astype(F32)
    put_counts(out_ref, 256.0 * total[:blocks] + total[blocks:], blocks)


def join(a, b):
    return pl.pallas_call(
        join_kernel,
        in_specs=[VMEM_SPEC] * 2,
        out_specs=VMEM_SPEC,
        out_shape=jax.ShapeDtypeStruct(a.shape, BF16),
        compiler_params=params(4),
        cost_estimate=cost(0.6),
        name="join",
    )(a, b)


def pick_kernel(sets, cap, tgt_ref, pos_ref, *refs):
    means, outs, (mean_ref, sem) = refs[: Y * C], refs[Y * C + 1 : -2], refs[-2:]
    z, x, y, core = pos_ref[0], pos_ref[1], pos_ref[2], pos_ref[3]
    blocks = means[0].shape[0]
    copies = []
    for i, ref in enumerate(means):
        from_core = core if i % C == 0 else 1 - core
        first = (lax.rem(y - i // C + Y, Y) * C + from_core) * blocks
        copies.append(pltpu.make_async_copy(ref, mean_ref.at[pl.ds(first, blocks)], sem.at[i]))
        copies[-1].start()
    for copy in copies:
        copy.wait()
    for i, offsets in enumerate(sets):
        for dx in range(X):
            for j, off in enumerate(offsets):
                sender_z = lax.rem(z + off + Z, Z)
                for c in range(cap):
                    t = tgt_ref[dx, (sender_z * X + x) * cap + c]
                    outs[i * X + dx][j * cap + c] = mean_ref[jnp.maximum(t, 0)]


def pick(sets, cap, tgt, pos, means, after):
    shapes = []
    for offsets in sets:
        shapes += [jax.ShapeDtypeStruct((len(offsets) * cap, BS, BS), BF16)] * X
    out = pl.pallas_call(
        functools.partial(pick_kernel, sets, cap),
        in_specs=[SMEM_SPEC, SMEM_SPEC] + [ANY_SPEC] * (len(means) + 1),
        out_specs=[VMEM_SPEC] * len(shapes),
        out_shape=shapes,
        scratch_shapes=[
            pltpu.VMEM((len(means) * means[0].shape[0], BS, BS), BF16),
            pltpu.SemaphoreType.DMA((len(means),)),
        ],
        compiler_params=params(8),
        cost_estimate=cost(3),
        name="pick",
    )(tgt, pos, *means, after)
    return [out[i * X : (i + 1) * X] for i in range(len(sets))]


def spread_kernel(offsets, starts, cap, cuts, after, src_ref, pos_ref, adj_ref, *refs):
    n = len(offsets)
    got, refs = refs[:X], refs[X:]
    inits = []
    for parts in starts:
        inits.append([(lo, hi, refs[i]) for i, (lo, hi) in enumerate(parts)])
        refs = refs[len(parts) :]
    outs, acc = refs[after:-1], refs[-1]
    blocks = acc.shape[1]
    z, x = pos_ref[0], pos_ref[1]
    for j in range(n):
        if len(inits[j]) == 0 or inits[j][0][:2] != (0, blocks):
            acc[j] = jnp.zeros(acc.shape[1:], F32)
        for i, (lo, hi, ref) in enumerate(inits[j]):
            if i == 0:
                acc[j, lo:hi] = ref[...].astype(F32)
            else:
                acc[j, lo:hi] += ref[...].astype(F32)
    first = lax.rem(z + offsets[0] + Z, Z)
    apart = offsets[-1] - offsets[0]

    def add(j, carry):
        sender = lax.rem(first + j * apart, Z)
        for dx in range(X):
            owner = lax.rem(x + dx, X)
            for c in range(cap):
                src = src_ref[(sender * X + owner) * cap + c]
                acc[j, src] += jnp.dot(
                    adj_ref[j, dx, c], got[dx][j * cap + c], preferred_element_type=F32
                )
        return carry

    lax.fori_loop(0, n, add, 0)
    for out, (j, lo, hi) in zip(outs, cuts):
        out[...] = acc[j, lo:hi].astype(BF16)


def spread(offsets, cap, blocks, src, pos, adj, got, starts, cuts=None, after=()):
    n = len(offsets)
    cuts = [(j, 0, blocks) for j in range(n)] if cuts is None else cuts
    return pl.pallas_call(
        functools.partial(
            spread_kernel, offsets, [[(lo, hi) for lo, hi, _ in s] for s in starts], cap, cuts, len(after)
        ),
        in_specs=[SMEM_SPEC, SMEM_SPEC] + [VMEM_SPEC] * (1 + X + sum(len(s) for s in starts))
        + [ANY_SPEC] * len(after),
        out_specs=[VMEM_SPEC] * len(cuts),
        out_shape=[jax.ShapeDtypeStruct((hi - lo, BS, BS), BF16) for _, lo, hi in cuts],
        scratch_shapes=[pltpu.VMEM((n, blocks, BS, BS), F32)],
        compiler_params=params(8),
        cost_estimate=cost(1.2 * n),
        name="spread",
    )(src, pos, adj, *got, *[a for s in starts for _, _, a in s], *after)


def halves(up, down):
    half = up.shape[0] // 2

    def kernel(up_ref, down_ref, low_ref, high_ref):
        low_ref[...] = up_ref[:half]
        high_ref[...] = down_ref[half:]

    return pl.pallas_call(
        kernel,
        in_specs=[VMEM_SPEC] * 2,
        out_specs=[VMEM_SPEC] * 2,
        out_shape=[jax.ShapeDtypeStruct((half,) + up.shape[1:], up.dtype)] * 2,
        compiler_params=params(4),
        cost_estimate=cost(0.3),
        name="halves",
    )(up, down)


def sum_copies(parts, copies):
    def kernel(in_ref, out_ref):
        total = jnp.sum(in_ref[...], axis=0)
        for i in range(copies):
            out_ref[i] = total

    return pl.pallas_call(
        kernel,
        in_specs=[VMEM_SPEC],
        out_specs=VMEM_SPEC,
        out_shape=jax.ShapeDtypeStruct((copies,) + parts.shape[1:], F32),
        compiler_params=params(4),
        cost_estimate=cost(0.5),
        name="sum_copies",
    )(parts)


def scale_split(grads, scale):
    rows, width = grads.shape
    half = rows // 2

    def kernel(in_ref, a_ref, b_ref):
        a_ref[...] = in_ref[:half] * scale
        b_ref[...] = in_ref[half:] * scale

    return pl.pallas_call(
        kernel,
        in_specs=[VMEM_SPEC],
        out_specs=[VMEM_SPEC] * 2,
        out_shape=[jax.ShapeDtypeStruct((half, width), F32)] * 2,
        compiler_params=params(4),
        cost_estimate=cost(0.5),
        name="scale_split",
    )(grads)


def own_part(grad_pre, w_self, blocks):
    def kernel(grad_ref, w_ref, out_ref):
        for i in range(blocks):
            out_ref[i] = dot_nt(grad_ref[i * BS : (i + 1) * BS, :], w_ref[...])

    return pl.pallas_call(
        kernel,
        in_specs=[VMEM_SPEC] * 2,
        out_specs=VMEM_SPEC,
        out_shape=jax.ShapeDtypeStruct((blocks, BS, BS), F32),
        compiler_params=params(8),
        cost_estimate=cost(1.5),
        name="own_part",
    )(grad_pre, w_self)


def shift(value, axis, size, by):
    return lax.ppermute(value, axis, [(i, (i + by) % size) for i in range(size)])


def shift_x(values, sign):
    return [values[0]] + [shift(values[d], "x", X, sign * d) for d in range(1, X)]


def exchange(value, axes):
    return lax.all_to_all(value, axes, split_axis=0, concat_axis=0, tiled=True)


def on_device(
    features, w_self, w_neigh, cotangent, src_block, dst_block, block_count, edge_rows, edge_cols
):
    owners, cap = src_block.shape[1:]
    edges = edge_rows.shape[-1]
    local_nodes = features.shape[0]
    blocks = local_nodes // BS
    half = blocks // 2
    groups = Y * C
    node_total = local_nodes * groups * owners
    pos = jnp.stack([lax.axis_index(a) for a in ("z", "x", "y", "c")]).astype(jnp.int32)
    feats = features.reshape(blocks, BS, -1)

    own_src = src_block[0].T
    sent = pack(own_src, dst_block[0].T, block_count, edge_rows, edge_cols)
    lists = exchange(sent, "z")
    src = lists[:, :, edges].reshape(owners * cap)
    tgt = lists[:, :, edges + 1].reshape(1, owners * cap)

    batches = [(0,), (-1, 1), (-2, 2), (-3, 3), (4,)]
    *part, adj = build(batches[0], cap, edges, own_src, pos, sent, [feats], [], own=True)
    sums, adjs = [shift_x(part, 1)], [adj]
    up, down, last = feats, feats, [part[0], lists]
    for k in range(1, 5):
        if k < 4:
            up, down = follow([shift(up, "z", Z, 1), shift(down, "z", Z, -1)], last)
            arrays = [up, down]
        else:
            low, high = halves(up, down)
            arrays = [shift(low, "z", Z, 1), shift(high, "z", Z, -1)]
        after = sums[k - 2][1:] if k > 1 else []
        *part, adj = build(batches[k], cap, edges, src, pos, lists, arrays, after, extra=[tgt] if k == 2 else ())
        sums.append(shift_x(part, 1))
        adjs.append(adj)
        last = part[:1] + (sums[0][1:] if k == 1 else [])
    keeps, sends, tgt = gather_sums(batches, cap, groups * blocks, pos, sum(sums, []))

    arrived = []
    for dy in (2, 1, 3):
        joined = join(keeps[dy], shift(sends[dy], "c", C, 1))
        arrived.append(shift(joined, "y", Y, dy))
    arrived += [keeps[0], shift(sends[0], "c", C, 1)]
    total = sum(a.astype(F32) for a in arrived)
    own_sums, own_cnt = total[:local_nodes], get_counts(total, blocks)
    divisor = jnp.maximum(own_cnt, 1.0).reshape(local_nodes, 1)
    neigh_mean = (own_sums / divisor).astype(BF16)
    preact = jnp.dot(features, w_self, preferred_element_type=F32) + jnp.dot(
        neigh_mean, w_neigh, preferred_element_type=F32
    )
    sigmoids = jax.nn.sigmoid(preact)
    activated = (preact * sigmoids).astype(BF16)
    grad_pre = (cotangent.astype(F32) * sigmoids * (1.0 + preact * (1.0 - sigmoids))).astype(BF16)
    grad_mean = (
        jnp.einsum("nh,fh->nf", grad_pre, w_neigh, preferred_element_type=F32) / divisor
    ).astype(BF16)
    grad_mean = grad_mean.reshape(blocks, BS, -1)
    means = [grad_mean] + [shift(grad_mean, "y", Y, dy) for dy in range(1, Y)]

    both = jnp.concatenate([features, neigh_mean], axis=1)
    grads = jnp.einsum("nf,nh->fh", both, grad_pre, preferred_element_type=F32)
    piece = sum_copies(exchange(grads, ("z", "x")).reshape(owners, -1, grads.shape[1]), groups)
    first_piece = piece
    means[1:] = follow(means[1:], [first_piece])
    means = [m for mean in means for m in (mean, shift(mean, "c", C, 1))]
    sets = [(4,), (-3, 3), (-2, 2), (-1, 1), (0,)]
    picked = pick(sets, cap, tgt, pos, means, first_piece)
    piece = sum_copies(exchange(piece, ("y", "c")), owners)
    grads = exchange(piece, ("z", "x")).reshape(grads.shape)

    own_term = own_part(grad_pre, w_self, blocks)
    got = [shift_x(p, -1) for p in picked]

    def back(k, starts, cuts=None, after=()):
        return spread(
            batches[k], cap, blocks, src, pos, adjs[k], got[4 - k], starts, cuts, after
        )

    low, high = back(4, [[]], [(0, 0, half), (0, half, blocks)])
    up, down = shift(low, "z", Z, 1), shift(high, "z", Z, -1)
    down, up = back(3, [[(half, blocks, down)], [(0, half, up)]])
    for k in (2, 1):
        up, down = shift(up, "z", Z, 1), shift(down, "z", Z, -1)
        after = [piece] if k == 2 else []
        down, up = back(k, [[(0, blocks, down)], [(0, blocks, up)]], after=after)
    up, down = shift(up, "z", Z, 1), shift(down, "z", Z, -1)
    (grad_features,) = back(0, [[(0, blocks, own_term), (0, blocks, up), (0, blocks, down)]])
    grad_self, grad_neigh = scale_split(grads, float(node_total) ** (-0.5))
    return activated, grad_features.reshape(local_nodes, -1), grad_self, grad_neigh


def solution(mesh):
    mesh = Mesh(mesh.devices.reshape(Y, C, Z, X), ("y", "c", "z", "x"))
    every = ("y", "c", "z", "x")
    return jax.shard_map(
        on_device,
        mesh=mesh,
        in_specs=(
            P(every, None),
            P(),
            P(),
            P(every, None),
            P(every, None, None),
            P(every, None, None),
            P(every, None),
            P(every, None, None, None),
            P(every, None, None, None),
        ),
        out_specs=(P(every, None), P(every, None), P(), P()),
        check_vma=False,
    )
```

```python
import functools

import jax
import jax.numpy as jnp
from jax import lax
from jax.experimental import pallas as pl
from jax.experimental.pallas import tpu as pltpu
from jax.sharding import Mesh, PartitionSpec as P

BS = 128
TAIL = 16
Y, C, Z, X = 4, 2, 8, 4
F32 = jnp.float32
BF16 = jnp.bfloat16
MIB = 1024 * 1024
NT = (((1,), (1,)), ((), ()))
SMEM_SPEC = pl.BlockSpec(memory_space=pltpu.SMEM)
VMEM_SPEC = pl.BlockSpec(memory_space=pltpu.VMEM)
ANY_SPEC = pl.BlockSpec(memory_space=pl.ANY)
LISTS = 256


def dot_nt(a, b):
    return lax.dot_general(a, b, NT, preferred_element_type=F32)


def params(mib):
    return pltpu.CompilerParams(vmem_limit_bytes=mib * MIB)


def cost(us):
    return pl.CostEstimate(flops=0, bytes_accessed=int(us * 3.5e6), transcendentals=0)


def one_hot_t(row, extent):
    ids = lax.broadcasted_iota(jnp.int32, (extent, row.shape[1]), 0)
    return jnp.where(ids == row, 1.0, 0.0).astype(BF16)


def build_batch(offsets, cap, edges, src_of, z, x, edge_ref, feats, sum_refs, adj_ref, tgt_ref=None):
    n = len(offsets)

    def block_of(j, src):
        if len(feats) == n:
            return feats[j][src]
        low, high = feats
        half = low.shape[0]
        return jnp.where(src < half, low[jnp.minimum(src, half - 1)], high[jnp.maximum(src - half, 0)])


    def owner_step(dx, carry):
        owner = lax.rem(x + dx, X)
        counts = jnp.zeros((TAIL, BS), F32)
        if tgt_ref is not None:
            last = lax.broadcasted_iota(jnp.int32, (TAIL, BS), 0) == TAIL - 1
            counts = jnp.where(last, tgt_ref[...].astype(F32), 0.0)
        parts = []
        for j, off in enumerate(offsets):
            row = lax.rem(z + off + Z, Z) * X + owner
            packed = edge_ref[row]
            for c in range(cap):
                k = j * cap + c
                e = packed[c : c + 1, :edges]
                rt = one_hot_t(lax.shift_right_logical(e, 7), BS)
                ct = one_hot_t(jnp.bitwise_and(e, BS - 1), BS)
                a = dot_nt(rt, ct).astype(BF16)
                adj_ref[j, dx, c] = dot_nt(ct, rt).astype(BF16)
                part = jnp.dot(a, block_of(j, src_of(row, c)), preferred_element_type=F32)
                parts.append(part.astype(BF16))
                pick = jnp.where(
                    lax.broadcasted_iota(jnp.int32, (TAIL, edges), 0) == k, 1.0, 0.0
                ).astype(BF16)
                counts = counts + dot_nt(pick, rt)
        parts.append(counts.astype(BF16))
        for d, out in enumerate(sum_refs):

            @pl.when(dx == d)
            def _(out=out):
                for k, part in enumerate(parts):
                    out[k * BS : k * BS + part.shape[0], :] = part

        return carry

    lax.fori_loop(0, X, owner_step, 0)


def batch_shapes(n, cap):
    return [jax.ShapeDtypeStruct((n * cap * BS + TAIL, BS), BF16)] * X + [
        jax.ShapeDtypeStruct((n, X, cap, BS, BS), BF16)
    ]


def pack_kernel(cap, edges, src_ref, dst_ref, used_ref, rows_ref, cols_ref, lists_ref):
    owners = rows_ref.shape[1]
    rest = LISTS - edges
    meta_slot = lax.broadcasted_iota(jnp.int32, (cap, rest), 0)
    meta_lane = lax.broadcasted_iota(jnp.int32, (cap, rest), 1)
    slot = lax.broadcasted_iota(jnp.int32, (cap, edges), 0)

    def pack(o, carry):
        packed = rows_ref[0, o] * BS + cols_ref[0, o]
        meta = jnp.zeros((cap, rest), jnp.int32)
        for c in range(cap):
            to = jnp.where(c < used_ref[0, o], dst_ref[c, o], -1)
            packed = jnp.where(jnp.logical_and(slot == c, to < 0), BS * BS, packed)
            value = jnp.where(meta_lane == 0, src_ref[c, o], to)
            meta = jnp.where(meta_slot == c, value, meta)
        lists_ref[o, :, :edges] = packed
        lists_ref[o, :, edges:] = meta
        return carry

    lax.fori_loop(0, owners, pack, 0, unroll=4)


def pack(src, dst, used, rows, cols):
    owners, cap, edges = rows.shape[1:]
    whole = pl.BlockSpec(rows.shape, lambda i: (0, 0, 0, 0))
    return pl.pallas_call(
        functools.partial(pack_kernel, cap, edges),
        grid=(1,),
        in_specs=[SMEM_SPEC] * 3 + [whole] * 2,
        out_specs=VMEM_SPEC,
        out_shape=jax.ShapeDtypeStruct((owners, cap, LISTS), jnp.int32),
        compiler_params=params(4),
        cost_estimate=cost(2),
        name="pack",
    )(src, dst, used, rows, cols)


def build_kernel(offsets, cap, edges, own, n_feats, extra, after, src_ref, pos_ref, edge_ref, *refs):
    feats, refs = refs[:n_feats], refs[n_feats:]
    tgt_ref = refs[0] if extra else None
    refs = refs[extra + after :]

    def src_of(row, c):
        if own:
            return src_ref[c, row]
        return src_ref[row * cap + c]

    build_batch(
        offsets,
        cap,
        edges,
        src_of,
        pos_ref[0],
        pos_ref[1],
        edge_ref,
        feats,
        refs[:X],
        refs[X],
        tgt_ref,
    )


def build(offsets, cap, edges, src, pos, edge_list, feats, after, own=False, extra=()):
    n = len(offsets)
    return pl.pallas_call(
        functools.partial(
            build_kernel, offsets, cap, edges, own, len(feats), len(extra), len(after)
        ),
        in_specs=[SMEM_SPEC, SMEM_SPEC] + [VMEM_SPEC] * (1 + len(feats) + len(extra)) + [ANY_SPEC] * len(after),
        out_specs=[VMEM_SPEC] * (X + 1),
        out_shape=batch_shapes(n, cap),
        compiler_params=params(8),
        cost_estimate=cost(2.5 * n),
        name="build",
    )(src, pos, edge_list, *feats, *extra, *after)


def follow(arrays, after):
    n = len(arrays)
    return pl.pallas_call(
        lambda *refs: None,
        in_specs=[ANY_SPEC] * (n + len(after)),
        out_specs=[ANY_SPEC] * n,
        out_shape=[jax.ShapeDtypeStruct(a.shape, a.dtype) for a in arrays],
        input_output_aliases={i: i for i in range(n)},
        compiler_params=params(1),
        cost_estimate=cost(0.3),
        name="follow",
    )(*arrays, *after)


def gather_kernel(batches, cap, pos_ref, *refs):
    total = len(batches) * X
    got, refs = refs[:total], refs[total:]
    keeps, sends, (tgt_out, acc, acc_c, tgt_ref, sem) = refs[:Y], refs[Y : 2 * Y], refs[2 * Y :]
    targets = acc.shape[0]
    z, x, y, core = pos_ref[0], pos_ref[1], pos_ref[2], pos_ref[3]
    rows = [got[2 * X + d][-TAIL:, :].astype(F32)[TAIL - 1 :, :] for d in range(X)]
    tgt_out[...] = jnp.concatenate(rows + rows, axis=0).astype(jnp.int32)
    copy = pltpu.make_async_copy(tgt_out, tgt_ref, sem)
    copy.start()

    def clear(i, carry):
        acc[i] = jnp.zeros((BS, BS), F32)
        return carry

    lax.fori_loop(0, targets, clear, 0, unroll=4)
    acc_c[...] = jnp.zeros_like(acc_c)
    copy.wait()
    for b, offsets in enumerate(batches):
        n = len(offsets)
        for dx in range(X):
            ref = got[b * X + dx]
            tail = ref[n * cap * BS :, :].astype(F32)
            first = lax.rem(z + offsets[0] + Z, Z)
            apart = offsets[-1] - offsets[0]

            def add(j, carry, ref=ref, dx=dx, tail=tail, first=first, apart=apart):
                sender_z = lax.rem(first + j * apart, Z)
                for c in range(cap):
                    k = j * cap + c
                    t = tgt_ref[dx, (sender_z * X + x) * cap + c]

                    @pl.when(t >= 0)
                    def _():
                        rows = ref[pl.ds(pl.multiple_of(k * BS, BS), BS), :]
                        acc[t] += rows.astype(F32)
                        here = lax.broadcasted_iota(jnp.int32, tail.shape, 0) == k
                        count = jnp.sum(jnp.where(here, tail, 0.0), axis=0, keepdims=True)
                        acc_c[pl.ds(t, 1), :] += count

                return carry

            lax.fori_loop(0, n, add, 0)

    blocks = targets // (Y * C)
    for dy in range(Y):
        for out, to_core in ((keeps[dy], core), (sends[dy], 1 - core)):
            first = (lax.rem(y + dy, Y) * C + to_core) * blocks

            def store(i, carry, out=out, first=first):
                out[pl.ds(pl.multiple_of(i * BS, BS), BS), :] = acc[first + i].astype(BF16)
                return carry

            lax.fori_loop(0, blocks, store, 0, unroll=4)
            count = acc_c[pl.ds(pl.multiple_of(first, blocks), blocks), :]
            put_counts(out, count, blocks)


def put_counts(out, count, blocks):
    high = jnp.floor(count * (1.0 / 256.0))
    out[blocks * BS : blocks * (BS + 1), :] = high.astype(BF16)
    out[blocks * (BS + 1) :, :] = (count - 256.0 * high).astype(BF16)


def get_counts(total, blocks):
    return 256.0 * total[blocks * BS : blocks * (BS + 1)] + total[blocks * (BS + 1) :]


def gather_sums(batches, cap, targets, pos, got):
    blocks = targets // (Y * C)
    part = jax.ShapeDtypeStruct((blocks * (BS + 2), BS), BF16)
    out = pl.pallas_call(
        functools.partial(gather_kernel, batches, cap),
        in_specs=[SMEM_SPEC] + [VMEM_SPEC] * len(got),
        out_specs=[VMEM_SPEC] * (2 * Y + 1),
        out_shape=[part] * (2 * Y) + [jax.ShapeDtypeStruct((2 * X, BS), jnp.int32)],
        scratch_shapes=[
            pltpu.VMEM((targets, BS, BS), F32),
            pltpu.VMEM((targets, BS), F32),
            pltpu.SMEM((2 * X, BS), jnp.int32),
            pltpu.SemaphoreType.DMA,
        ],
        compiler_params=params(16),
        cost_estimate=cost(5),
        name="gather_sums",
    )(pos, *got)
    return out[:Y], out[Y : 2 * Y], out[2 * Y]


def join_kernel(a_ref, b_ref, out_ref):
    blocks = out_ref.shape[0] // (BS + 2)

    def add(i, carry):
        rows = pl.ds(pl.multiple_of(i * BS, BS), BS)
        out_ref[rows, :] = (a_ref[rows, :].astype(F32) + b_ref[rows, :].astype(F32)).astype(BF16)
        return carry

    lax.fori_loop(0, blocks, add, 0, unroll=2)
    digits = slice(blocks * BS, None)
    total = a_ref[digits, :].astype(F32) + b_ref[digits, :].astype(F32)
    put_counts(out_ref, 256.0 * total[:blocks] + total[blocks:], blocks)


def join(a, b):
    return pl.pallas_call(
        join_kernel,
        in_specs=[VMEM_SPEC] * 2,
        out_specs=VMEM_SPEC,
        out_shape=jax.ShapeDtypeStruct(a.shape, BF16),
        compiler_params=params(4),
        cost_estimate=cost(0.6),
        name="join",
    )(a, b)


def pick_kernel(sets, cap, tgt_ref, pos_ref, *refs):
    means, outs, (mean_ref, sem) = refs[: Y * C], refs[Y * C + 1 : -2], refs[-2:]
    z, x, y, core = pos_ref[0], pos_ref[1], pos_ref[2], pos_ref[3]
    blocks = means[0].shape[0]
    copies = []
    for i, ref in enumerate(means):
        from_core = core if i % C == 0 else 1 - core
        first = (lax.rem(y - i // C + Y, Y) * C + from_core) * blocks
        copies.append(pltpu.make_async_copy(ref, mean_ref.at[pl.ds(first, blocks)], sem.at[i]))
        copies[-1].start()
    for copy in copies:
        copy.wait()
    for i, offsets in enumerate(sets):
        for dx in range(X):
            for j, off in enumerate(offsets):
                sender_z = lax.rem(z + off + Z, Z)
                for c in range(cap):
                    t = tgt_ref[dx, (sender_z * X + x) * cap + c]
                    outs[i * X + dx][j * cap + c] = mean_ref[jnp.maximum(t, 0)]


def pick(sets, cap, tgt, pos, means, after):
    shapes = []
    for offsets in sets:
        shapes += [jax.ShapeDtypeStruct((len(offsets) * cap, BS, BS), BF16)] * X
    out = pl.pallas_call(
        functools.partial(pick_kernel, sets, cap),
        in_specs=[SMEM_SPEC, SMEM_SPEC] + [ANY_SPEC] * (len(means) + 1),
        out_specs=[VMEM_SPEC] * len(shapes),
        out_shape=shapes,
        scratch_shapes=[
            pltpu.VMEM((len(means) * means[0].shape[0], BS, BS), BF16),
            pltpu.SemaphoreType.DMA((len(means),)),
        ],
        compiler_params=params(8),
        cost_estimate=cost(3),
        name="pick",
    )(tgt, pos, *means, after)
    return [out[i * X : (i + 1) * X] for i in range(len(sets))]


def spread_kernel(offsets, starts, cap, cuts, after, src_ref, pos_ref, adj_ref, *refs):
    n = len(offsets)
    got, refs = refs[:X], refs[X:]
    inits = []
    for parts in starts:
        inits.append([(lo, hi, refs[i]) for i, (lo, hi) in enumerate(parts)])
        refs = refs[len(parts) :]
    outs, acc = refs[after:-1], refs[-1]
    blocks = acc.shape[1]
    z, x = pos_ref[0], pos_ref[1]
    for j in range(n):
        if len(inits[j]) == 0 or inits[j][0][:2] != (0, blocks):
            acc[j] = jnp.zeros(acc.shape[1:], F32)
        for i, (lo, hi, ref) in enumerate(inits[j]):
            if i == 0:
                acc[j, lo:hi] = ref[...].astype(F32)
            else:
                acc[j, lo:hi] += ref[...].astype(F32)
    first = lax.rem(z + offsets[0] + Z, Z)
    apart = offsets[-1] - offsets[0]

    def add(j, carry):
        sender = lax.rem(first + j * apart, Z)
        for dx in range(X):
            owner = lax.rem(x + dx, X)
            for c in range(cap):
                src = src_ref[(sender * X + owner) * cap + c]
                acc[j, src] += jnp.dot(
                    adj_ref[j, dx, c], got[dx][j * cap + c], preferred_element_type=F32
                )
        return carry

    lax.fori_loop(0, n, add, 0)
    for out, (j, lo, hi) in zip(outs, cuts):
        out[...] = acc[j, lo:hi].astype(BF16)


def spread(offsets, cap, blocks, src, pos, adj, got, starts, cuts=None, after=()):
    n = len(offsets)
    cuts = [(j, 0, blocks) for j in range(n)] if cuts is None else cuts
    return pl.pallas_call(
        functools.partial(
            spread_kernel, offsets, [[(lo, hi) for lo, hi, _ in s] for s in starts], cap, cuts, len(after)
        ),
        in_specs=[SMEM_SPEC, SMEM_SPEC] + [VMEM_SPEC] * (1 + X + sum(len(s) for s in starts))
        + [ANY_SPEC] * len(after),
        out_specs=[VMEM_SPEC] * len(cuts),
        out_shape=[jax.ShapeDtypeStruct((hi - lo, BS, BS), BF16) for _, lo, hi in cuts],
        scratch_shapes=[pltpu.VMEM((n, blocks, BS, BS), F32)],
        compiler_params=params(8),
        cost_estimate=cost(1.2 * n),
        name="spread",
    )(src, pos, adj, *got, *[a for s in starts for _, _, a in s], *after)


def halves(up, down):
    half = up.shape[0] // 2

    def kernel(up_ref, down_ref, low_ref, high_ref):
        low_ref[...] = up_ref[:half]
        high_ref[...] = down_ref[half:]

    return pl.pallas_call(
        kernel,
        in_specs=[VMEM_SPEC] * 2,
        out_specs=[VMEM_SPEC] * 2,
        out_shape=[jax.ShapeDtypeStruct((half,) + up.shape[1:], up.dtype)] * 2,
        compiler_params=params(4),
        cost_estimate=cost(0.3),
        name="halves",
    )(up, down)


def sum_copies(parts, copies):
    def kernel(in_ref, out_ref):
        total = jnp.sum(in_ref[...], axis=0)
        for i in range(copies):
            out_ref[i] = total

    return pl.pallas_call(
        kernel,
        in_specs=[VMEM_SPEC],
        out_specs=VMEM_SPEC,
        out_shape=jax.ShapeDtypeStruct((copies,) + parts.shape[1:], F32),
        compiler_params=params(4),
        cost_estimate=cost(0.5),
        name="sum_copies",
    )(parts)


def scale_split(grads, scale):
    rows, width = grads.shape
    half = rows // 2

    def kernel(in_ref, a_ref, b_ref):
        a_ref[...] = in_ref[:half] * scale
        b_ref[...] = in_ref[half:] * scale

    return pl.pallas_call(
        kernel,
        in_specs=[VMEM_SPEC],
        out_specs=[VMEM_SPEC] * 2,
        out_shape=[jax.ShapeDtypeStruct((half, width), F32)] * 2,
        compiler_params=params(4),
        cost_estimate=cost(0.5),
        name="scale_split",
    )(grads)


def own_part(grad_pre, w_self, blocks):
    def kernel(grad_ref, w_ref, out_ref):
        for i in range(blocks):
            out_ref[i] = dot_nt(grad_ref[i * BS : (i + 1) * BS, :], w_ref[...])

    return pl.pallas_call(
        kernel,
        in_specs=[VMEM_SPEC] * 2,
        out_specs=VMEM_SPEC,
        out_shape=jax.ShapeDtypeStruct((blocks, BS, BS), F32),
        compiler_params=params(8),
        cost_estimate=cost(1.5),
        name="own_part",
    )(grad_pre, w_self)


def shift(value, axis, size, by):
    return lax.ppermute(value, axis, [(i, (i + by) % size) for i in range(size)])


def shift_x(values, sign):
    return [values[0]] + [shift(values[d], "x", X, sign * d) for d in range(1, X)]


def exchange(value, axes):
    return lax.all_to_all(value, axes, split_axis=0, concat_axis=0, tiled=True)


def on_device(
    features, w_self, w_neigh, cotangent, src_block, dst_block, block_count, edge_rows, edge_cols
):
    owners, cap = src_block.shape[1:]
    edges = edge_rows.shape[-1]
    local_nodes = features.shape[0]
    blocks = local_nodes // BS
    half = blocks // 2
    groups = Y * C
    node_total = local_nodes * groups * owners
    pos = jnp.stack([lax.axis_index(a) for a in ("z", "x", "y", "c")]).astype(jnp.int32)
    feats = features.reshape(blocks, BS, -1)

    own_src = src_block[0].T
    sent = pack(own_src, dst_block[0].T, block_count, edge_rows, edge_cols)
    lists = exchange(sent, "z")
    src = lists[:, :, edges].reshape(owners * cap)
    tgt = lists[:, :, edges + 1].reshape(1, owners * cap)

    batches = [(0,), (-1, 1), (-2, 2), (-3, 3), (4,)]
    *part, adj = build(batches[0], cap, edges, own_src, pos, sent, [feats], [], own=True)
    sums, adjs = [shift_x(part, 1)], [adj]
    up, down, last = feats, feats, [part[0], lists]
    for k in range(1, 5):
        if k < 4:
            up, down = follow([shift(up, "z", Z, 1), shift(down, "z", Z, -1)], last)
            arrays = [up, down]
        else:
            low, high = halves(up, down)
            arrays = [shift(low, "z", Z, 1), shift(high, "z", Z, -1)]
        after = sums[k - 2][1:] if k > 1 else []
        *part, adj = build(batches[k], cap, edges, src, pos, lists, arrays, after, extra=[tgt] if k == 2 else ())
        sums.append(shift_x(part, 1))
        adjs.append(adj)
        last = part[:1] + (sums[0][1:] if k == 1 else [])
    keeps, sends, tgt = gather_sums(batches, cap, groups * blocks, pos, sum(sums, []))

    arrived = []
    for dy in (2, 1, 3):
        joined = join(keeps[dy], shift(sends[dy], "c", C, 1))
        arrived.append(shift(joined, "y", Y, dy))
    arrived += [keeps[0], shift(sends[0], "c", C, 1)]
    total = sum(a.astype(F32) for a in arrived)
    own_sums, own_cnt = total[:local_nodes], get_counts(total, blocks)
    divisor = jnp.maximum(own_cnt, 1.0).reshape(local_nodes, 1)
    neigh_mean = (own_sums / divisor).astype(BF16)
    preact = jnp.dot(features, w_self, preferred_element_type=F32) + jnp.dot(
        neigh_mean, w_neigh, preferred_element_type=F32
    )
    sigmoids = jax.nn.sigmoid(preact)
    activated = (preact * sigmoids).astype(BF16)
    grad_pre = (cotangent.astype(F32) * sigmoids * (1.0 + preact * (1.0 - sigmoids))).astype(BF16)
    grad_mean = (
        jnp.einsum("nh,fh->nf", grad_pre, w_neigh, preferred_element_type=F32) / divisor
    ).astype(BF16)
    grad_mean = grad_mean.reshape(blocks, BS, -1)
    means = [grad_mean] + [shift(grad_mean, "y", Y, dy) for dy in range(1, Y)]

    both = jnp.concatenate([features, neigh_mean], axis=1)
    grads = jnp.einsum("nf,nh->fh", both, grad_pre, preferred_element_type=F32)
    width = grads.shape[1]
    piece = sum_copies(exchange(grads, "x").reshape(X, -1, width), 1)[0]
    piece = sum_copies(exchange(piece, "z").reshape(Z, -1, width), groups)
    first_piece = piece
    means[1:] = follow(means[1:], [first_piece])
    means = [m for mean in means for m in (mean, shift(mean, "c", C, 1))]
    sets = [(4,), (-3, 3), (-2, 2), (-1, 1), (0,)]
    picked = pick(sets, cap, tgt, pos, means, first_piece)
    piece = sum_copies(exchange(piece, ("y", "c")), Z)
    column = sum_copies(exchange(piece, "z").reshape(1, -1, width), X)
    grads = exchange(column, "x").reshape(grads.shape)

    own_term = own_part(grad_pre, w_self, blocks)
    got = [shift_x(p, -1) for p in picked]

    def back(k, starts, cuts=None, after=()):
        return spread(
            batches[k], cap, blocks, src, pos, adjs[k], got[4 - k], starts, cuts, after
        )

    low, high = back(4, [[]], [(0, 0, half), (0, half, blocks)])
    up, down = shift(low, "z", Z, 1), shift(high, "z", Z, -1)
    down, up = back(3, [[(half, blocks, down)], [(0, half, up)]])
    for k in (2, 1):
        up, down = shift(up, "z", Z, 1), shift(down, "z", Z, -1)
        after = [piece] if k == 2 else [column]
        down, up = back(k, [[(0, blocks, down)], [(0, blocks, up)]], after=after)
    up, down = shift(up, "z", Z, 1), shift(down, "z", Z, -1)
    (grad_features,) = back(0, [[(0, blocks, own_term), (0, blocks, up), (0, blocks, down)]])
    grad_self, grad_neigh = scale_split(grads, float(node_total) ** (-0.5))
    return activated, grad_features.reshape(local_nodes, -1), grad_self, grad_neigh


def solution(mesh):
    mesh = Mesh(mesh.devices.reshape(Y, C, Z, X), ("y", "c", "z", "x"))
    every = ("y", "c", "z", "x")
    return jax.shard_map(
        on_device,
        mesh=mesh,
        in_specs=(
            P(every, None),
            P(),
            P(),
            P(every, None),
            P(every, None, None),
            P(every, None, None),
            P(every, None),
            P(every, None, None, None),
            P(every, None, None, None),
        ),
        out_specs=(P(every, None), P(every, None), P(), P()),
        check_vma=False,
    )
```

```python
import functools

import jax
import jax.numpy as jnp
from jax import lax
from jax.experimental import pallas as pl
from jax.experimental.pallas import tpu as pltpu
from jax.sharding import Mesh, PartitionSpec as P

BS = 128
TAIL = 16
Y, C, Z, X = 4, 2, 8, 4
F32 = jnp.float32
BF16 = jnp.bfloat16
MIB = 1024 * 1024
NT = (((1,), (1,)), ((), ()))
SMEM_SPEC = pl.BlockSpec(memory_space=pltpu.SMEM)
VMEM_SPEC = pl.BlockSpec(memory_space=pltpu.VMEM)
ANY_SPEC = pl.BlockSpec(memory_space=pl.ANY)
LISTS = 256
DIGITS = 3


def dot_nt(a, b):
    return lax.dot_general(a, b, NT, preferred_element_type=F32)


def params(mib):
    return pltpu.CompilerParams(vmem_limit_bytes=mib * MIB)


def cost(us):
    return pl.CostEstimate(flops=0, bytes_accessed=int(us * 3.5e6), transcendentals=0)


def one_hot_t(row, extent):
    ids = lax.broadcasted_iota(jnp.int32, (extent, row.shape[1]), 0)
    return jnp.where(ids == row, 1.0, 0.0).astype(BF16)


def build_batch(offsets, cap, edges, src_of, z, x, edge_ref, feats, sum_refs, adj_ref, tgt_ref=None):
    n = len(offsets)

    def block_of(j, src):
        if len(feats) == n:
            return feats[j][src]
        low, high = feats
        half = low.shape[0]
        return jnp.where(src < half, low[jnp.minimum(src, half - 1)], high[jnp.maximum(src - half, 0)])


    def owner_step(dx, carry):
        owner = lax.rem(x + dx, X)
        counts = jnp.zeros((TAIL, BS), F32)
        if tgt_ref is not None:
            last = lax.broadcasted_iota(jnp.int32, (TAIL, BS), 0) == TAIL - 1
            counts = jnp.where(last, tgt_ref[...].astype(F32), 0.0)
        parts = []
        for j, off in enumerate(offsets):
            row = lax.rem(z + off + Z, Z) * X + owner
            packed = edge_ref[row]
            for c in range(cap):
                k = j * cap + c
                e = packed[c : c + 1, :edges]
                rt = one_hot_t(lax.shift_right_logical(e, 7), BS)
                ct = one_hot_t(jnp.bitwise_and(e, BS - 1), BS)
                a = dot_nt(rt, ct).astype(BF16)
                adj_ref[j, dx, c] = dot_nt(ct, rt).astype(BF16)
                part = jnp.dot(a, block_of(j, src_of(row, c)), preferred_element_type=F32)
                parts.append(part.astype(BF16))
                pick = jnp.where(
                    lax.broadcasted_iota(jnp.int32, (TAIL, edges), 0) == k, 1.0, 0.0
                ).astype(BF16)
                counts = counts + dot_nt(pick, rt)
        parts.append(counts.astype(BF16))
        for d, out in enumerate(sum_refs):

            @pl.when(dx == d)
            def _(out=out):
                for k, part in enumerate(parts):
                    out[k * BS : k * BS + part.shape[0], :] = part

        return carry

    lax.fori_loop(0, X, owner_step, 0)


def batch_shapes(n, cap):
    return [jax.ShapeDtypeStruct((n * cap * BS + TAIL, BS), BF16)] * X + [
        jax.ShapeDtypeStruct((n, X, cap, BS, BS), BF16)
    ]


def pack_kernel(cap, edges, src_ref, dst_ref, used_ref, rows_ref, cols_ref, lists_ref):
    owners = rows_ref.shape[1]
    rest = LISTS - edges
    meta_slot = lax.broadcasted_iota(jnp.int32, (cap, rest), 0)
    meta_lane = lax.broadcasted_iota(jnp.int32, (cap, rest), 1)
    slot = lax.broadcasted_iota(jnp.int32, (cap, edges), 0)

    def pack(o, carry):
        packed = rows_ref[0, o] * BS + cols_ref[0, o]
        meta = jnp.zeros((cap, rest), jnp.int32)
        for c in range(cap):
            to = jnp.where(c < used_ref[0, o], dst_ref[c, o], -1)
            packed = jnp.where(jnp.logical_and(slot == c, to < 0), BS * BS, packed)
            value = jnp.where(meta_lane == 0, src_ref[c, o], to)
            meta = jnp.where(meta_slot == c, value, meta)
        lists_ref[o, :, :edges] = packed
        lists_ref[o, :, edges:] = meta
        return carry

    lax.fori_loop(0, owners, pack, 0, unroll=4)


def pack(src, dst, used, rows, cols):
    owners, cap, edges = rows.shape[1:]
    whole = pl.BlockSpec(rows.shape, lambda i: (0, 0, 0, 0))
    return pl.pallas_call(
        functools.partial(pack_kernel, cap, edges),
        grid=(1,),
        in_specs=[SMEM_SPEC] * 3 + [whole] * 2,
        out_specs=VMEM_SPEC,
        out_shape=jax.ShapeDtypeStruct((owners, cap, LISTS), jnp.int32),
        compiler_params=params(4),
        cost_estimate=cost(2),
        name="pack",
    )(src, dst, used, rows, cols)


def build_kernel(offsets, cap, edges, own, n_feats, extra, after, src_ref, pos_ref, edge_ref, *refs):
    feats, refs = refs[:n_feats], refs[n_feats:]
    tgt_ref = refs[0] if extra else None
    refs = refs[extra + after :]

    def src_of(row, c):
        if own:
            return src_ref[c, row]
        return src_ref[row * cap + c]

    build_batch(
        offsets,
        cap,
        edges,
        src_of,
        pos_ref[0],
        pos_ref[1],
        edge_ref,
        feats,
        refs[:X],
        refs[X],
        tgt_ref,
    )


def build(offsets, cap, edges, src, pos, edge_list, feats, after, own=False, extra=()):
    n = len(offsets)
    return pl.pallas_call(
        functools.partial(
            build_kernel, offsets, cap, edges, own, len(feats), len(extra), len(after)
        ),
        in_specs=[SMEM_SPEC, SMEM_SPEC] + [VMEM_SPEC] * (1 + len(feats) + len(extra)) + [ANY_SPEC] * len(after),
        out_specs=[VMEM_SPEC] * (X + 1),
        out_shape=batch_shapes(n, cap),
        compiler_params=params(8),
        cost_estimate=cost(2.5 * n),
        name="build",
    )(src, pos, edge_list, *feats, *extra, *after)


def follow(arrays, after):
    n = len(arrays)
    return pl.pallas_call(
        lambda *refs: None,
        in_specs=[ANY_SPEC] * (n + len(after)),
        out_specs=[ANY_SPEC] * n,
        out_shape=[jax.ShapeDtypeStruct(a.shape, a.dtype) for a in arrays],
        input_output_aliases={i: i for i in range(n)},
        compiler_params=params(1),
        cost_estimate=cost(0.3),
        name="follow",
    )(*arrays, *after)


def gather_kernel(batches, cap, pos_ref, *refs):
    total = len(batches) * X
    got, refs = refs[:total], refs[total:]
    keeps, sends, (tgt_out, acc, acc_c, tgt_ref, sem) = refs[:Y], refs[Y : 2 * Y], refs[2 * Y :]
    targets = acc.shape[0]
    z, x, y, core = pos_ref[0], pos_ref[1], pos_ref[2], pos_ref[3]
    rows = [got[2 * X + d][-TAIL:, :].astype(F32)[TAIL - 1 :, :] for d in range(X)]
    tgt_out[...] = jnp.concatenate(rows + rows, axis=0).astype(jnp.int32)
    copy = pltpu.make_async_copy(tgt_out, tgt_ref, sem)
    copy.start()

    def clear(i, carry):
        acc[i] = jnp.zeros((BS, BS), F32)
        return carry

    lax.fori_loop(0, targets, clear, 0, unroll=4)
    acc_c[...] = jnp.zeros_like(acc_c)
    copy.wait()
    for b, offsets in enumerate(batches):
        n = len(offsets)
        for dx in range(X):
            ref = got[b * X + dx]
            tail = ref[n * cap * BS :, :].astype(F32)
            first = lax.rem(z + offsets[0] + Z, Z)
            apart = offsets[-1] - offsets[0]

            def add(j, carry, ref=ref, dx=dx, tail=tail, first=first, apart=apart):
                sender_z = lax.rem(first + j * apart, Z)
                for c in range(cap):
                    k = j * cap + c
                    t = tgt_ref[dx, (sender_z * X + x) * cap + c]

                    @pl.when(t >= 0)
                    def _():
                        rows = ref[pl.ds(pl.multiple_of(k * BS, BS), BS), :]
                        acc[t] += rows.astype(F32)
                        here = lax.broadcasted_iota(jnp.int32, tail.shape, 0) == k
                        count = jnp.sum(jnp.where(here, tail, 0.0), axis=0, keepdims=True)
                        acc_c[pl.ds(t, 1), :] += count

                return carry

            lax.fori_loop(0, n, add, 0)

    blocks = targets // (Y * C)
    for dy in range(Y):
        for out, to_core in ((keeps[dy], core), (sends[dy], 1 - core)):
            first = (lax.rem(y + dy, Y) * C + to_core) * blocks

            def store(i, carry, out=out, first=first):
                out[pl.ds(pl.multiple_of(i * BS, BS), BS), :] = acc[first + i].astype(BF16)
                return carry

            lax.fori_loop(0, blocks, store, 0, unroll=4)
            count = acc_c[pl.ds(pl.multiple_of(first, blocks), blocks), :]
            put_counts(out, blocks * BS, count)


def put_counts(out, first, count):
    n = count.shape[0]
    for i in range(DIGITS):
        rest = jnp.floor(count * (1.0 / 256.0))
        out[first + i * n : first + (i + 1) * n, :] = (count - 256.0 * rest).astype(BF16)
        count = rest


def get_counts(digits):
    n = digits.shape[0] // DIGITS
    return sum(digits[i * n : (i + 1) * n] * 256.0**i for i in range(DIGITS))


def gather_sums(batches, cap, targets, pos, got):
    blocks = targets // (Y * C)
    part = jax.ShapeDtypeStruct((blocks * (BS + DIGITS), BS), BF16)
    out = pl.pallas_call(
        functools.partial(gather_kernel, batches, cap),
        in_specs=[SMEM_SPEC] + [VMEM_SPEC] * len(got),
        out_specs=[VMEM_SPEC] * (2 * Y + 1),
        out_shape=[part] * (2 * Y) + [jax.ShapeDtypeStruct((2 * X, BS), jnp.int32)],
        scratch_shapes=[
            pltpu.VMEM((targets, BS, BS), F32),
            pltpu.VMEM((targets, BS), F32),
            pltpu.SMEM((2 * X, BS), jnp.int32),
            pltpu.SemaphoreType.DMA,
        ],
        compiler_params=params(16),
        cost_estimate=cost(5),
        name="gather_sums",
    )(pos, *got)
    return out[:Y], out[Y : 2 * Y], out[2 * Y]


def join_kernel(kind, a_ref, b_ref, *refs):
    blocks = a_ref.shape[0] // (BS + DIGITS)
    half = blocks // 2

    def add(out_ref, first, to, n, extra_ref=None):
        def step(i, carry):
            rows = pl.ds(pl.multiple_of((first + i) * BS, BS), BS)
            value = a_ref[rows, :].astype(F32) + b_ref[rows, :].astype(F32)
            if extra_ref is not None:
                value += extra_ref[pl.ds(pl.multiple_of(i * BS, BS), BS), :].astype(F32)
            out_ref[pl.ds(pl.multiple_of((to + i) * BS, BS), BS), :] = value.astype(BF16)
            return carry

        lax.fori_loop(0, n, step, 0, unroll=2)

    digits = a_ref[blocks * BS :, :].astype(F32) + b_ref[blocks * BS :, :].astype(F32)
    if kind == "cut":
        low_ref, high_ref = refs
        add(low_ref, 0, 0, half)
        put_counts(low_ref, half * BS, get_counts(digits))
        add(high_ref, half, 0, half)
        return
    extra_ref, out_ref = refs
    add(out_ref, 0, 0, half, extra_ref if kind == "low" else None)
    add(out_ref, half, half, half, extra_ref if kind == "high" else None)
    if kind == "low":
        digits += extra_ref[half * BS :, :].astype(F32)
    put_counts(out_ref, blocks * BS, get_counts(digits))


def join(kind, a, b, *extra):
    rows = a.shape[0]
    half = rows // (BS + DIGITS) // 2 * BS
    outs = [rows - half, half] if kind == "cut" else [rows]
    return pl.pallas_call(
        functools.partial(join_kernel, kind),
        in_specs=[VMEM_SPEC] * (2 + len(extra)),
        out_specs=[VMEM_SPEC] * len(outs),
        out_shape=[jax.ShapeDtypeStruct((n, BS), BF16) for n in outs],
        compiler_params=params(4),
        cost_estimate=cost(0.6),
        name="join",
    )(a, b, *extra)


def pick_kernel(sets, cap, tgt_ref, pos_ref, *refs):
    means, outs, (mean_ref, sem) = refs[: Y * C], refs[Y * C + 1 : -2], refs[-2:]
    z, x, y, core = pos_ref[0], pos_ref[1], pos_ref[2], pos_ref[3]
    blocks = means[0].shape[0]
    copies = []
    for i, ref in enumerate(means):
        from_core = core if i % C == 0 else 1 - core
        first = (lax.rem(y - i // C + Y, Y) * C + from_core) * blocks
        copies.append(pltpu.make_async_copy(ref, mean_ref.at[pl.ds(first, blocks)], sem.at[i]))
        copies[-1].start()
    for copy in copies:
        copy.wait()
    for i, offsets in enumerate(sets):
        for dx in range(X):
            for j, off in enumerate(offsets):
                sender_z = lax.rem(z + off + Z, Z)
                for c in range(cap):
                    t = tgt_ref[dx, (sender_z * X + x) * cap + c]
                    outs[i * X + dx][j * cap + c] = mean_ref[jnp.maximum(t, 0)]


def pick(sets, cap, tgt, pos, means, after):
    shapes = []
    for offsets in sets:
        shapes += [jax.ShapeDtypeStruct((len(offsets) * cap, BS, BS), BF16)] * X
    out = pl.pallas_call(
        functools.partial(pick_kernel, sets, cap),
        in_specs=[SMEM_SPEC, SMEM_SPEC] + [ANY_SPEC] * (len(means) + 1),
        out_specs=[VMEM_SPEC] * len(shapes),
        out_shape=shapes,
        scratch_shapes=[
            pltpu.VMEM((len(means) * means[0].shape[0], BS, BS), BF16),
            pltpu.SemaphoreType.DMA((len(means),)),
        ],
        compiler_params=params(8),
        cost_estimate=cost(3),
        name="pick",
    )(tgt, pos, *means, after)
    return [out[i * X : (i + 1) * X] for i in range(len(sets))]


def spread_kernel(offsets, starts, cap, cuts, after, src_ref, pos_ref, adj_ref, *refs):
    n = len(offsets)
    got, refs = refs[:X], refs[X:]
    inits = []
    for parts in starts:
        inits.append([(lo, hi, refs[i]) for i, (lo, hi) in enumerate(parts)])
        refs = refs[len(parts) :]
    outs, acc = refs[after:-1], refs[-1]
    blocks = acc.shape[1]
    z, x = pos_ref[0], pos_ref[1]
    for j in range(n):
        if len(inits[j]) == 0 or inits[j][0][:2] != (0, blocks):
            acc[j] = jnp.zeros(acc.shape[1:], F32)
        for i, (lo, hi, ref) in enumerate(inits[j]):
            if i == 0:
                acc[j, lo:hi] = ref[...].astype(F32)
            else:
                acc[j, lo:hi] += ref[...].astype(F32)
    first = lax.rem(z + offsets[0] + Z, Z)
    apart = offsets[-1] - offsets[0]

    def add(j, carry):
        sender = lax.rem(first + j * apart, Z)
        for dx in range(X):
            owner = lax.rem(x + dx, X)
            for c in range(cap):
                src = src_ref[(sender * X + owner) * cap + c]
                acc[j, src] += jnp.dot(
                    adj_ref[j, dx, c], got[dx][j * cap + c], preferred_element_type=F32
                )
        return carry

    lax.fori_loop(0, n, add, 0)
    for out, (j, lo, hi) in zip(outs, cuts):
        out[...] = acc[j, lo:hi].astype(BF16)


def spread(offsets, cap, blocks, src, pos, adj, got, starts, cuts=None, after=()):
    n = len(offsets)
    cuts = [(j, 0, blocks) for j in range(n)] if cuts is None else cuts
    return pl.pallas_call(
        functools.partial(
            spread_kernel, offsets, [[(lo, hi) for lo, hi, _ in s] for s in starts], cap, cuts, len(after)
        ),
        in_specs=[SMEM_SPEC, SMEM_SPEC] + [VMEM_SPEC] * (1 + X + sum(len(s) for s in starts))
        + [ANY_SPEC] * len(after),
        out_specs=[VMEM_SPEC] * len(cuts),
        out_shape=[jax.ShapeDtypeStruct((hi - lo, BS, BS), BF16) for _, lo, hi in cuts],
        scratch_shapes=[pltpu.VMEM((n, blocks, BS, BS), F32)],
        compiler_params=params(8),
        cost_estimate=cost(1.2 * n),
        name="spread",
    )(src, pos, adj, *got, *[a for s in starts for _, _, a in s], *after)


def halves(up, down):
    half = up.shape[0] // 2

    def kernel(up_ref, down_ref, low_ref, high_ref):
        low_ref[...] = up_ref[:half]
        high_ref[...] = down_ref[half:]

    return pl.pallas_call(
        kernel,
        in_specs=[VMEM_SPEC] * 2,
        out_specs=[VMEM_SPEC] * 2,
        out_shape=[jax.ShapeDtypeStruct((half,) + up.shape[1:], up.dtype)] * 2,
        compiler_params=params(4),
        cost_estimate=cost(0.3),
        name="halves",
    )(up, down)


def sum_copies(parts, copies):
    def kernel(in_ref, out_ref):
        total = jnp.sum(in_ref[...], axis=0)
        for i in range(copies):
            out_ref[i] = total

    return pl.pallas_call(
        kernel,
        in_specs=[VMEM_SPEC],
        out_specs=VMEM_SPEC,
        out_shape=jax.ShapeDtypeStruct((copies,) + parts.shape[1:], F32),
        compiler_params=params(4),
        cost_estimate=cost(0.5),
        name="sum_copies",
    )(parts)


def scale_split(grads, scale):
    rows, width = grads.shape
    half = rows // 2

    def kernel(in_ref, a_ref, b_ref):
        a_ref[...] = in_ref[:half] * scale
        b_ref[...] = in_ref[half:] * scale

    return pl.pallas_call(
        kernel,
        in_specs=[VMEM_SPEC],
        out_specs=[VMEM_SPEC] * 2,
        out_shape=[jax.ShapeDtypeStruct((half, width), F32)] * 2,
        compiler_params=params(4),
        cost_estimate=cost(0.5),
        name="scale_split",
    )(grads)


def own_part(grad_pre, w_self, blocks):
    def kernel(grad_ref, w_ref, out_ref):
        for i in range(blocks):
            out_ref[i] = dot_nt(grad_ref[i * BS : (i + 1) * BS, :], w_ref[...])

    return pl.pallas_call(
        kernel,
        in_specs=[VMEM_SPEC] * 2,
        out_specs=VMEM_SPEC,
        out_shape=jax.ShapeDtypeStruct((blocks, BS, BS), F32),
        compiler_params=params(8),
        cost_estimate=cost(1.5),
        name="own_part",
    )(grad_pre, w_self)


def shift(value, axis, size, by):
    return lax.ppermute(value, axis, [(i, (i + by) % size) for i in range(size)])


def shift_x(values, sign):
    return [values[0]] + [shift(values[d], "x", X, sign * d) for d in range(1, X)]


def exchange(value, axes):
    return lax.all_to_all(value, axes, split_axis=0, concat_axis=0, tiled=True)


def on_device(
    features, w_self, w_neigh, cotangent, src_block, dst_block, block_count, edge_rows, edge_cols
):
    owners, cap = src_block.shape[1:]
    edges = edge_rows.shape[-1]
    local_nodes = features.shape[0]
    blocks = local_nodes // BS
    half = blocks // 2
    groups = Y * C
    node_total = local_nodes * groups * owners
    pos = jnp.stack([lax.axis_index(a) for a in ("z", "x", "y", "c")]).astype(jnp.int32)
    feats = features.reshape(blocks, BS, -1)

    own_src = src_block[0].T
    sent = pack(own_src, dst_block[0].T, block_count, edge_rows, edge_cols)
    lists = exchange(sent, "z")
    src = lists[:, :, edges].reshape(owners * cap)
    tgt = lists[:, :, edges + 1].reshape(1, owners * cap)

    batches = [(0,), (-1, 1), (-2, 2), (-3, 3), (4,)]
    *part, adj = build(batches[0], cap, edges, own_src, pos, sent, [feats], [], own=True)
    sums, adjs = [shift_x(part, 1)], [adj]
    up, down, last = feats, feats, [part[0], lists]
    for k in range(1, 5):
        if k < 4:
            up, down = follow([shift(up, "z", Z, 1), shift(down, "z", Z, -1)], last)
            arrays = [up, down]
        else:
            low, high = halves(up, down)
            arrays = [shift(low, "z", Z, 1), shift(high, "z", Z, -1)]
        after = sums[k - 2][1:] if k > 1 else []
        *part, adj = build(batches[k], cap, edges, src, pos, lists, arrays, after, extra=[tgt] if k == 2 else ())
        sums.append(shift_x(part, 1))
        adjs.append(adj)
        last = part[:1] + (sums[0][1:] if k == 1 else [])
    keeps, sends, tgt = gather_sums(batches, cap, groups * blocks, pos, sum(sums, []))

    crossed = [shift(sends[dy], "c", C, 1) for dy in (2, 1, 3, 0)]
    low, high = join("cut", keeps[2], crossed[0])
    low, high = shift(low, "y", Y, 1), shift(high, "y", Y, -1)
    (ahead,) = join("low", keeps[1], crossed[1], low)
    (behind,) = join("high", keeps[3], crossed[2], high)
    arrived = [keeps[0], crossed[3], shift(ahead, "y", Y, 1), shift(behind, "y", Y, -1)]
    total = sum(a.astype(F32) for a in arrived)
    own_sums, own_cnt = total[:local_nodes], get_counts(total[local_nodes:])
    divisor = jnp.maximum(own_cnt, 1.0).reshape(local_nodes, 1)
    neigh_mean = (own_sums / divisor).astype(BF16)
    preact = jnp.dot(features, w_self, preferred_element_type=F32) + jnp.dot(
        neigh_mean, w_neigh, preferred_element_type=F32
    )
    sigmoids = jax.nn.sigmoid(preact)
    activated = (preact * sigmoids).astype(BF16)
    grad_pre = (cotangent.astype(F32) * sigmoids * (1.0 + preact * (1.0 - sigmoids))).astype(BF16)
    grad_mean = (
        jnp.einsum("nh,fh->nf", grad_pre, w_neigh, preferred_element_type=F32) / divisor
    ).astype(BF16)
    grad_mean = grad_mean.reshape(blocks, BS, -1)
    means = [grad_mean] + [shift(grad_mean, "y", Y, dy) for dy in range(1, Y)]

    both = jnp.concatenate([features, neigh_mean], axis=1)
    grads = jnp.einsum("nf,nh->fh", both, grad_pre, preferred_element_type=F32)
    width = grads.shape[1]
    rows = grads.shape[0] // owners
    grads = grads.reshape(X, Z, rows, width).transpose(1, 0, 2, 3).reshape(grads.shape)
    piece = sum_copies(exchange(grads, ("z", "x")).reshape(owners, rows, width), groups)
    first_piece = piece
    means[1:] = follow(means[1:], [first_piece])
    means = [m for mean in means for m in (mean, shift(mean, "c", C, 1))]
    sets = [(4,), (-3, 3), (-2, 2), (-1, 1), (0,)]
    picked = pick(sets, cap, tgt, pos, means, first_piece)
    piece = sum_copies(exchange(piece, ("y", "c")), Z)
    column = sum_copies(exchange(piece, "z").reshape(1, -1, width), X)
    grads = exchange(column, "x").reshape(grads.shape)

    own_term = own_part(grad_pre, w_self, blocks)
    got = [shift_x(p, -1) for p in picked]

    def back(k, starts, cuts=None, after=()):
        return spread(
            batches[k], cap, blocks, src, pos, adjs[k], got[4 - k], starts, cuts, after
        )

    low, high = back(4, [[]], [(0, 0, half), (0, half, blocks)])
    up, down = shift(low, "z", Z, 1), shift(high, "z", Z, -1)
    down, up = back(3, [[(half, blocks, down)], [(0, half, up)]])
    for k in (2, 1):
        up, down = shift(up, "z", Z, 1), shift(down, "z", Z, -1)
        after = [piece] if k == 2 else [column]
        down, up = back(k, [[(0, blocks, down)], [(0, blocks, up)]], after=after)
    up, down = shift(up, "z", Z, 1), shift(down, "z", Z, -1)
    (grad_features,) = back(0, [[(0, blocks, own_term), (0, blocks, up), (0, blocks, down)]])
    grad_self, grad_neigh = scale_split(grads, float(node_total) ** (-0.5))
    return activated, grad_features.reshape(local_nodes, -1), grad_self, grad_neigh


def solution(mesh):
    mesh = Mesh(mesh.devices.reshape(Y, C, Z, X), ("y", "c", "z", "x"))
    every = ("y", "c", "z", "x")
    return jax.shard_map(
        on_device,
        mesh=mesh,
        in_specs=(
            P(every, None),
            P(),
            P(),
            P(every, None),
            P(every, None, None),
            P(every, None, None),
            P(every, None),
            P(every, None, None, None),
            P(every, None, None, None),
        ),
        out_specs=(P(every, None), P(every, None), P(), P()),
        check_vma=False,
    )
```

```python
import functools

import jax
import jax.numpy as jnp
from jax import lax
from jax.experimental import pallas as pl
from jax.experimental.pallas import tpu as pltpu
from jax.sharding import Mesh, PartitionSpec as P

BS = 128
TAIL = 16
Y, C, Z, X = 4, 2, 8, 4
F32 = jnp.float32
BF16 = jnp.bfloat16
MIB = 1024 * 1024
NT = (((1,), (1,)), ((), ()))
SMEM_SPEC = pl.BlockSpec(memory_space=pltpu.SMEM)
VMEM_SPEC = pl.BlockSpec(memory_space=pltpu.VMEM)
ANY_SPEC = pl.BlockSpec(memory_space=pl.ANY)
LISTS = 256
DIGITS = 3


def dot_nt(a, b):
    return lax.dot_general(a, b, NT, preferred_element_type=F32)


def params(mib):
    return pltpu.CompilerParams(vmem_limit_bytes=mib * MIB)


def cost(us):
    return pl.CostEstimate(flops=0, bytes_accessed=int(us * 3.5e6), transcendentals=0)


def one_hot_t(row, extent):
    ids = lax.broadcasted_iota(jnp.int32, (extent, row.shape[1]), 0)
    return jnp.where(ids == row, 1.0, 0.0).astype(BF16)


def build_batch(
    offsets, cap, edges, src_of, z, x, edge_ref, feats, sum_refs, adj_ref, tgt_ref, static
):
    n = len(offsets)

    def block_of(j, src):
        if len(feats) == n:
            return feats[j][src]
        low, high = feats
        half = low.shape[0]
        return jnp.where(src < half, low[jnp.minimum(src, half - 1)], high[jnp.maximum(src - half, 0)])


    def slots(dx):
        owner = lax.rem(x + dx, X)
        counts = jnp.zeros((TAIL, BS), F32)
        if tgt_ref is not None:
            last = lax.broadcasted_iota(jnp.int32, (TAIL, BS), 0) == TAIL - 1
            counts = jnp.where(last, tgt_ref[...].astype(F32), 0.0)
        parts = []
        for j, off in enumerate(offsets):
            row = lax.rem(z + off + Z, Z) * X + owner
            packed = edge_ref[row]
            for c in range(cap):
                k = j * cap + c
                e = packed[c : c + 1, :edges]
                rt = one_hot_t(lax.shift_right_logical(e, 7), BS)
                ct = one_hot_t(jnp.bitwise_and(e, BS - 1), BS)
                a = dot_nt(rt, ct).astype(BF16)
                adj_ref[j, dx, c] = dot_nt(ct, rt).astype(BF16)
                part = jnp.dot(a, block_of(j, src_of(row, c)), preferred_element_type=F32)
                parts.append(part.astype(BF16))
                pick = jnp.where(
                    lax.broadcasted_iota(jnp.int32, (TAIL, edges), 0) == k, 1.0, 0.0
                ).astype(BF16)
                counts = counts + dot_nt(pick, rt)
        parts.append(counts.astype(BF16))
        return parts

    def store(out, parts):
        for k, part in enumerate(parts):
            out[k * BS : k * BS + part.shape[0], :] = part

    if static:
        for d, out in enumerate(sum_refs):
            store(out, slots(d))
        return

    def owner_step(dx, carry):
        parts = slots(dx)
        for d, out in enumerate(sum_refs):
            pl.when(dx == d)(functools.partial(store, out, parts))
        return carry

    lax.fori_loop(0, X, owner_step, 0)


def batch_shapes(n, cap):
    return [jax.ShapeDtypeStruct((n * cap * BS + TAIL, BS), BF16)] * X + [
        jax.ShapeDtypeStruct((n, X, cap, BS, BS), BF16)
    ]


def pack_kernel(cap, edges, src_ref, dst_ref, used_ref, rows_ref, cols_ref, lists_ref):
    owners = rows_ref.shape[1]
    rest = LISTS - edges
    meta_slot = lax.broadcasted_iota(jnp.int32, (cap, rest), 0)
    meta_lane = lax.broadcasted_iota(jnp.int32, (cap, rest), 1)
    slot = lax.broadcasted_iota(jnp.int32, (cap, edges), 0)

    def pack(o, carry):
        packed = rows_ref[0, o] * BS + cols_ref[0, o]
        meta = jnp.zeros((cap, rest), jnp.int32)
        for c in range(cap):
            to = jnp.where(c < used_ref[0, o], dst_ref[c, o], -1)
            packed = jnp.where(jnp.logical_and(slot == c, to < 0), BS * BS, packed)
            value = jnp.where(meta_lane == 0, src_ref[c, o], to)
            meta = jnp.where(meta_slot == c, value, meta)
        lists_ref[o, :, :edges] = packed
        lists_ref[o, :, edges:] = meta
        return carry

    lax.fori_loop(0, owners, pack, 0, unroll=4)


def pack(src, dst, used, rows, cols):
    owners, cap, edges = rows.shape[1:]
    whole = pl.BlockSpec(rows.shape, lambda i: (0, 0, 0, 0))
    return pl.pallas_call(
        functools.partial(pack_kernel, cap, edges),
        grid=(1,),
        in_specs=[SMEM_SPEC] * 3 + [whole] * 2,
        out_specs=VMEM_SPEC,
        out_shape=jax.ShapeDtypeStruct((owners, cap, LISTS), jnp.int32),
        compiler_params=params(4),
        cost_estimate=cost(2),
        name="pack",
    )(src, dst, used, rows, cols)


def build_kernel(offsets, cap, edges, own, static, n_feats, extra, after, src_ref, pos_ref, edge_ref, *refs):
    feats, refs = refs[:n_feats], refs[n_feats:]
    tgt_ref = refs[0] if extra else None
    refs = refs[extra + after :]

    def src_of(row, c):
        if own:
            return src_ref[c, row]
        return src_ref[row * cap + c]

    build_batch(
        offsets,
        cap,
        edges,
        src_of,
        pos_ref[0],
        pos_ref[1],
        edge_ref,
        feats,
        refs[:X],
        refs[X],
        tgt_ref,
        static,
    )


def build(offsets, cap, edges, src, pos, edge_list, feats, after, own=False, extra=(), static=False):
    n = len(offsets)
    return pl.pallas_call(
        functools.partial(
            build_kernel, offsets, cap, edges, own, static, len(feats), len(extra), len(after)
        ),
        in_specs=[SMEM_SPEC, SMEM_SPEC] + [VMEM_SPEC] * (1 + len(feats) + len(extra)) + [ANY_SPEC] * len(after),
        out_specs=[VMEM_SPEC] * (X + 1),
        out_shape=batch_shapes(n, cap),
        compiler_params=params(8),
        cost_estimate=cost(2.5 * n),
        name="build",
    )(src, pos, edge_list, *feats, *extra, *after)


def follow(arrays, after):
    n = len(arrays)
    return pl.pallas_call(
        lambda *refs: None,
        in_specs=[ANY_SPEC] * (n + len(after)),
        out_specs=[ANY_SPEC] * n,
        out_shape=[jax.ShapeDtypeStruct(a.shape, a.dtype) for a in arrays],
        input_output_aliases={i: i for i in range(n)},
        compiler_params=params(1),
        cost_estimate=cost(0.3),
        name="follow",
    )(*arrays, *after)


def gather_kernel(batches, cap, pos_ref, *refs):
    total = len(batches) * X
    got, refs = refs[:total], refs[total:]
    keeps, sends, (tgt_out, acc, acc_c, tgt_ref, sem) = refs[:Y], refs[Y : 2 * Y], refs[2 * Y :]
    targets = acc.shape[0]
    z, x, y, core = pos_ref[0], pos_ref[1], pos_ref[2], pos_ref[3]
    rows = [got[2 * X + d][-TAIL:, :].astype(F32)[TAIL - 1 :, :] for d in range(X)]
    tgt_out[...] = jnp.concatenate(rows + rows, axis=0).astype(jnp.int32)
    copy = pltpu.make_async_copy(tgt_out, tgt_ref, sem)
    copy.start()

    def clear(i, carry):
        acc[i] = jnp.zeros((BS, BS), F32)
        return carry

    lax.fori_loop(0, targets, clear, 0, unroll=4)
    acc_c[...] = jnp.zeros_like(acc_c)
    copy.wait()
    for b, offsets in enumerate(batches):
        n = len(offsets)
        for dx in range(X):
            ref = got[b * X + dx]
            tail = ref[n * cap * BS :, :].astype(F32)
            first = lax.rem(z + offsets[0] + Z, Z)
            apart = offsets[-1] - offsets[0]

            def add(j, carry, ref=ref, dx=dx, tail=tail, first=first, apart=apart):
                sender_z = lax.rem(first + j * apart, Z)
                for c in range(cap):
                    k = j * cap + c
                    t = tgt_ref[dx, (sender_z * X + x) * cap + c]

                    @pl.when(t >= 0)
                    def _():
                        rows = ref[pl.ds(pl.multiple_of(k * BS, BS), BS), :]
                        acc[t] += rows.astype(F32)
                        here = lax.broadcasted_iota(jnp.int32, tail.shape, 0) == k
                        count = jnp.sum(jnp.where(here, tail, 0.0), axis=0, keepdims=True)
                        acc_c[pl.ds(t, 1), :] += count

                return carry

            lax.fori_loop(0, n, add, 0)

    blocks = targets // (Y * C)
    for dy in range(Y):
        for out, to_core in ((keeps[dy], core), (sends[dy], 1 - core)):
            first = (lax.rem(y + dy, Y) * C + to_core) * blocks

            def store(i, carry, out=out, first=first):
                out[pl.ds(pl.multiple_of(i * BS, BS), BS), :] = acc[first + i].astype(BF16)
                return carry

            lax.fori_loop(0, blocks, store, 0, unroll=4)
            count = acc_c[pl.ds(pl.multiple_of(first, blocks), blocks), :]
            put_counts(out, blocks * BS, count)


def put_counts(out, first, count):
    n = count.shape[0]
    for i in range(DIGITS):
        rest = jnp.floor(count * (1.0 / 256.0))
        out[first + i * n : first + (i + 1) * n, :] = (count - 256.0 * rest).astype(BF16)
        count = rest


def get_counts(digits):
    n = digits.shape[0] // DIGITS
    return sum(digits[i * n : (i + 1) * n] * 256.0**i for i in range(DIGITS))


def gather_sums(batches, cap, targets, pos, got):
    blocks = targets // (Y * C)
    part = jax.ShapeDtypeStruct((blocks * (BS + DIGITS), BS), BF16)
    out = pl.pallas_call(
        functools.partial(gather_kernel, batches, cap),
        in_specs=[SMEM_SPEC] + [VMEM_SPEC] * len(got),
        out_specs=[VMEM_SPEC] * (2 * Y + 1),
        out_shape=[part] * (2 * Y) + [jax.ShapeDtypeStruct((2 * X, BS), jnp.int32)],
        scratch_shapes=[
            pltpu.VMEM((targets, BS, BS), F32),
            pltpu.VMEM((targets, BS), F32),
            pltpu.SMEM((2 * X, BS), jnp.int32),
            pltpu.SemaphoreType.DMA,
        ],
        compiler_params=params(16),
        cost_estimate=cost(5),
        name="gather_sums",
    )(pos, *got)
    return out[:Y], out[Y : 2 * Y], out[2 * Y]


def join_kernel(kind, a_ref, b_ref, *refs):
    blocks = a_ref.shape[0] // (BS + DIGITS)
    half = blocks // 2

    def add(out_ref, first, to, n, extra_ref=None):
        def step(i, carry):
            rows = pl.ds(pl.multiple_of((first + i) * BS, BS), BS)
            value = a_ref[rows, :].astype(F32) + b_ref[rows, :].astype(F32)
            if extra_ref is not None:
                value += extra_ref[pl.ds(pl.multiple_of(i * BS, BS), BS), :].astype(F32)
            out_ref[pl.ds(pl.multiple_of((to + i) * BS, BS), BS), :] = value.astype(BF16)
            return carry

        lax.fori_loop(0, n, step, 0, unroll=2)

    digits = a_ref[blocks * BS :, :].astype(F32) + b_ref[blocks * BS :, :].astype(F32)
    if kind == "cut":
        low_ref, high_ref = refs
        add(low_ref, 0, 0, half)
        put_counts(low_ref, half * BS, get_counts(digits))
        add(high_ref, half, 0, half)
        return
    extra_ref, out_ref = refs
    add(out_ref, 0, 0, half, extra_ref if kind == "low" else None)
    add(out_ref, half, half, half, extra_ref if kind == "high" else None)
    if kind == "low":
        digits += extra_ref[half * BS :, :].astype(F32)
    put_counts(out_ref, blocks * BS, get_counts(digits))


def join(kind, a, b, *extra):
    rows = a.shape[0]
    half = rows // (BS + DIGITS) // 2 * BS
    outs = [rows - half, half] if kind == "cut" else [rows]
    return pl.pallas_call(
        functools.partial(join_kernel, kind),
        in_specs=[VMEM_SPEC] * (2 + len(extra)),
        out_specs=[VMEM_SPEC] * len(outs),
        out_shape=[jax.ShapeDtypeStruct((n, BS), BF16) for n in outs],
        compiler_params=params(4),
        cost_estimate=cost(0.6),
        name="join",
    )(a, b, *extra)


def pick_kernel(sets, cap, tgt_ref, pos_ref, *refs):
    means, outs, (mean_ref, sem) = refs[: Y * C], refs[Y * C + 1 : -2], refs[-2:]
    z, x, y, core = pos_ref[0], pos_ref[1], pos_ref[2], pos_ref[3]
    blocks = means[0].shape[0]
    copies = []
    for i, ref in enumerate(means):
        from_core = core if i % C == 0 else 1 - core
        first = (lax.rem(y - i // C + Y, Y) * C + from_core) * blocks
        copies.append(pltpu.make_async_copy(ref, mean_ref.at[pl.ds(first, blocks)], sem.at[i]))
        copies[-1].start()
    for copy in copies:
        copy.wait()
    for i, offsets in enumerate(sets):
        for dx in range(X):
            for j, off in enumerate(offsets):
                sender_z = lax.rem(z + off + Z, Z)
                for c in range(cap):
                    t = tgt_ref[dx, (sender_z * X + x) * cap + c]
                    outs[i * X + dx][j * cap + c] = mean_ref[jnp.maximum(t, 0)]


def pick(sets, cap, tgt, pos, means, after):
    shapes = []
    for offsets in sets:
        shapes += [jax.ShapeDtypeStruct((len(offsets) * cap, BS, BS), BF16)] * X
    out = pl.pallas_call(
        functools.partial(pick_kernel, sets, cap),
        in_specs=[SMEM_SPEC, SMEM_SPEC] + [ANY_SPEC] * (len(means) + 1),
        out_specs=[VMEM_SPEC] * len(shapes),
        out_shape=shapes,
        scratch_shapes=[
            pltpu.VMEM((len(means) * means[0].shape[0], BS, BS), BF16),
            pltpu.SemaphoreType.DMA((len(means),)),
        ],
        compiler_params=params(8),
        cost_estimate=cost(3),
        name="pick",
    )(tgt, pos, *means, after)
    return [out[i * X : (i + 1) * X] for i in range(len(sets))]


def spread_kernel(offsets, starts, cap, cuts, after, src_ref, pos_ref, adj_ref, *refs):
    n = len(offsets)
    got, refs = refs[:X], refs[X:]
    inits = []
    for parts in starts:
        inits.append([(lo, hi, refs[i]) for i, (lo, hi) in enumerate(parts)])
        refs = refs[len(parts) :]
    outs, acc = refs[after:-1], refs[-1]
    blocks = acc.shape[1]
    z, x = pos_ref[0], pos_ref[1]
    for j in range(n):
        if len(inits[j]) == 0 or inits[j][0][:2] != (0, blocks):
            acc[j] = jnp.zeros(acc.shape[1:], F32)
        for i, (lo, hi, ref) in enumerate(inits[j]):
            if i == 0:
                acc[j, lo:hi] = ref[...].astype(F32)
            else:
                acc[j, lo:hi] += ref[...].astype(F32)
    first = lax.rem(z + offsets[0] + Z, Z)
    apart = offsets[-1] - offsets[0]

    def add(j, carry):
        sender = lax.rem(first + j * apart, Z)
        for dx in range(X):
            owner = lax.rem(x + dx, X)
            for c in range(cap):
                src = src_ref[(sender * X + owner) * cap + c]
                acc[j, src] += jnp.dot(
                    adj_ref[j, dx, c], got[dx][j * cap + c], preferred_element_type=F32
                )
        return carry

    lax.fori_loop(0, n, add, 0)
    for out, (j, lo, hi) in zip(outs, cuts):
        out[...] = acc[j, lo:hi].astype(BF16)


def spread(offsets, cap, blocks, src, pos, adj, got, starts, cuts=None, after=()):
    n = len(offsets)
    cuts = [(j, 0, blocks) for j in range(n)] if cuts is None else cuts
    return pl.pallas_call(
        functools.partial(
            spread_kernel, offsets, [[(lo, hi) for lo, hi, _ in s] for s in starts], cap, cuts, len(after)
        ),
        in_specs=[SMEM_SPEC, SMEM_SPEC] + [VMEM_SPEC] * (1 + X + sum(len(s) for s in starts))
        + [ANY_SPEC] * len(after),
        out_specs=[VMEM_SPEC] * len(cuts),
        out_shape=[jax.ShapeDtypeStruct((hi - lo, BS, BS), BF16) for _, lo, hi in cuts],
        scratch_shapes=[pltpu.VMEM((n, blocks, BS, BS), F32)],
        compiler_params=params(8),
        cost_estimate=cost(1.2 * n),
        name="spread",
    )(src, pos, adj, *got, *[a for s in starts for _, _, a in s], *after)


def halves(up, down):
    half = up.shape[0] // 2

    def kernel(up_ref, down_ref, low_ref, high_ref):
        low_ref[...] = up_ref[:half]
        high_ref[...] = down_ref[half:]

    return pl.pallas_call(
        kernel,
        in_specs=[VMEM_SPEC] * 2,
        out_specs=[VMEM_SPEC] * 2,
        out_shape=[jax.ShapeDtypeStruct((half,) + up.shape[1:], up.dtype)] * 2,
        compiler_params=params(4),
        cost_estimate=cost(0.3),
        name="halves",
    )(up, down)


def sum_copies(parts, copies):
    def kernel(in_ref, out_ref):
        total = jnp.sum(in_ref[...], axis=0)
        for i in range(copies):
            out_ref[i] = total

    return pl.pallas_call(
        kernel,
        in_specs=[VMEM_SPEC],
        out_specs=VMEM_SPEC,
        out_shape=jax.ShapeDtypeStruct((copies,) + parts.shape[1:], F32),
        compiler_params=params(4),
        cost_estimate=cost(0.5),
        name="sum_copies",
    )(parts)


def scale_split(grads, scale):
    rows, width = grads.shape
    half = rows // 2

    def kernel(in_ref, a_ref, b_ref):
        a_ref[...] = in_ref[:half] * scale
        b_ref[...] = in_ref[half:] * scale

    return pl.pallas_call(
        kernel,
        in_specs=[VMEM_SPEC],
        out_specs=[VMEM_SPEC] * 2,
        out_shape=[jax.ShapeDtypeStruct((half, width), F32)] * 2,
        compiler_params=params(4),
        cost_estimate=cost(0.5),
        name="scale_split",
    )(grads)


def own_part(grad_pre, w_self, blocks):
    def kernel(grad_ref, w_ref, out_ref):
        for i in range(blocks):
            out_ref[i] = dot_nt(grad_ref[i * BS : (i + 1) * BS, :], w_ref[...])

    return pl.pallas_call(
        kernel,
        in_specs=[VMEM_SPEC] * 2,
        out_specs=VMEM_SPEC,
        out_shape=jax.ShapeDtypeStruct((blocks, BS, BS), F32),
        compiler_params=params(8),
        cost_estimate=cost(1.5),
        name="own_part",
    )(grad_pre, w_self)


def shift(value, axis, size, by):
    return lax.ppermute(value, axis, [(i, (i + by) % size) for i in range(size)])


def shift_x(values, sign):
    return [values[0]] + [shift(values[d], "x", X, sign * d) for d in range(1, X)]


def exchange(value, axes):
    return lax.all_to_all(value, axes, split_axis=0, concat_axis=0, tiled=True)


def on_device(
    features, w_self, w_neigh, cotangent, src_block, dst_block, block_count, edge_rows, edge_cols
):
    owners, cap = src_block.shape[1:]
    edges = edge_rows.shape[-1]
    local_nodes = features.shape[0]
    blocks = local_nodes // BS
    half = blocks // 2
    groups = Y * C
    node_total = local_nodes * groups * owners
    pos = jnp.stack([lax.axis_index(a) for a in ("z", "x", "y", "c")]).astype(jnp.int32)
    feats = features.reshape(blocks, BS, -1)

    own_src = src_block[0].T
    sent = pack(own_src, dst_block[0].T, block_count, edge_rows, edge_cols)
    lists = exchange(sent, "z")
    src = lists[:, :, edges].reshape(owners * cap)
    tgt = lists[:, :, edges + 1].reshape(1, owners * cap)

    batches = [(0,), (-1, 1), (-2, 2), (-3, 3), (4,)]
    *part, adj = build(batches[0], cap, edges, own_src, pos, sent, [feats], [], own=True)
    sums, adjs = [shift_x(part, 1)], [adj]
    up, down, last = feats, feats, [part[0], lists]
    for k in range(1, 5):
        if k < 4:
            up, down = follow([shift(up, "z", Z, 1), shift(down, "z", Z, -1)], last)
            arrays = [up, down]
        else:
            low, high = halves(up, down)
            arrays = [shift(low, "z", Z, 1), shift(high, "z", Z, -1)]
        after = sums[k - 2][1:] if k > 1 else []
        *part, adj = build(batches[k], cap, edges, src, pos, lists, arrays, after, extra=[tgt] if k == 2 else (), static=k == 1)
        sums.append(shift_x(part, 1))
        adjs.append(adj)
        last = part[:1] + (sums[0][1:] if k == 1 else [])
    keeps, sends, tgt = gather_sums(batches, cap, groups * blocks, pos, sum(sums, []))

    crossed = [shift(sends[dy], "c", C, 1) for dy in (2, 1, 3, 0)]
    low, high = join("cut", keeps[2], crossed[0])
    low, high = shift(low, "y", Y, 1), shift(high, "y", Y, -1)
    (ahead,) = join("low", keeps[1], crossed[1], low)
    (behind,) = join("high", keeps[3], crossed[2], high)
    arrived = [keeps[0], crossed[3], shift(ahead, "y", Y, 1), shift(behind, "y", Y, -1)]
    total = sum(a.astype(F32) for a in arrived)
    own_sums, own_cnt = total[:local_nodes], get_counts(total[local_nodes:])
    divisor = jnp.maximum(own_cnt, 1.0).reshape(local_nodes, 1)
    neigh_mean = (own_sums / divisor).astype(BF16)
    preact = jnp.dot(features, w_self, preferred_element_type=F32) + jnp.dot(
        neigh_mean, w_neigh, preferred_element_type=F32
    )
    sigmoids = jax.nn.sigmoid(preact)
    activated = (preact * sigmoids).astype(BF16)
    grad_pre = (cotangent.astype(F32) * sigmoids * (1.0 + preact * (1.0 - sigmoids))).astype(BF16)
    grad_mean = (
        jnp.einsum("nh,fh->nf", grad_pre, w_neigh, preferred_element_type=F32) / divisor
    ).astype(BF16)
    grad_mean = grad_mean.reshape(blocks, BS, -1)
    means = [grad_mean] + [shift(grad_mean, "y", Y, dy) for dy in range(1, Y)]

    both = jnp.concatenate([features, neigh_mean], axis=1)
    grads = jnp.einsum("nf,nh->fh", both, grad_pre, preferred_element_type=F32)
    width = grads.shape[1]
    piece = sum_copies(exchange(grads, ("x", "z")).reshape(owners, -1, width), groups)
    first_piece = piece
    means[1:] = follow(means[1:], [first_piece])
    means = [m for mean in means for m in (mean, shift(mean, "c", C, 1))]
    sets = [(4,), (-3, 3), (-2, 2), (-1, 1), (0,)]
    picked = pick(sets, cap, tgt, pos, means, first_piece)
    piece = sum_copies(exchange(piece, ("y", "c")), Z)
    column = sum_copies(exchange(piece, "z").reshape(1, -1, width), X)
    grads = exchange(column, "x").reshape(grads.shape)

    own_term = own_part(grad_pre, w_self, blocks)
    got = [shift_x(p, -1) for p in picked]

    def back(k, starts, cuts=None, after=()):
        return spread(
            batches[k], cap, blocks, src, pos, adjs[k], got[4 - k], starts, cuts, after
        )

    low, high = back(4, [[]], [(0, 0, half), (0, half, blocks)], [piece])
    up, down = shift(low, "z", Z, 1), shift(high, "z", Z, -1)
    down, up = back(3, [[(half, blocks, down)], [(0, half, up)]])
    for k in (2, 1):
        up, down = shift(up, "z", Z, 1), shift(down, "z", Z, -1)
        after = [column] if k == 2 else [grads]
        down, up = back(k, [[(0, blocks, down)], [(0, blocks, up)]], after=after)
    up, down = shift(up, "z", Z, 1), shift(down, "z", Z, -1)
    (grad_features,) = back(0, [[(0, blocks, own_term), (0, blocks, up), (0, blocks, down)]])
    grad_self, grad_neigh = scale_split(grads, float(node_total) ** (-0.5))
    return activated, grad_features.reshape(local_nodes, -1), grad_self, grad_neigh


def solution(mesh):
    mesh = Mesh(mesh.devices.reshape(Y, C, Z, X), ("y", "c", "z", "x"))
    every = ("y", "c", "z", "x")
    return jax.shard_map(
        on_device,
        mesh=mesh,
        in_specs=(
            P(every, None),
            P(),
            P(),
            P(every, None),
            P(every, None, None),
            P(every, None, None),
            P(every, None),
            P(every, None, None, None),
            P(every, None, None, None),
        ),
        out_specs=(P(every, None), P(every, None), P(), P()),
        check_vma=False,
    )
```

```python
import functools

import jax
import jax.numpy as jnp
from jax import lax
from jax.experimental import pallas as pl
from jax.experimental.pallas import tpu as pltpu
from jax.sharding import Mesh, PartitionSpec as P

BS = 128
TAIL = 16
Y, C, Z, X = 4, 2, 8, 4
F32 = jnp.float32
BF16 = jnp.bfloat16
MIB = 1024 * 1024
NT = (((1,), (1,)), ((), ()))
SMEM_SPEC = pl.BlockSpec(memory_space=pltpu.SMEM)
VMEM_SPEC = pl.BlockSpec(memory_space=pltpu.VMEM)
ANY_SPEC = pl.BlockSpec(memory_space=pl.ANY)
LISTS = 256
DIGITS = 3


def dot_nt(a, b):
    return lax.dot_general(a, b, NT, preferred_element_type=F32)


def params(mib):
    return pltpu.CompilerParams(vmem_limit_bytes=mib * MIB)


def cost(us):
    return pl.CostEstimate(flops=0, bytes_accessed=int(us * 3.5e6), transcendentals=0)


def one_hot_t(row, extent):
    ids = lax.broadcasted_iota(jnp.int32, (extent, row.shape[1]), 0)
    return jnp.where(ids == row, 1.0, 0.0).astype(BF16)


def build_batch(
    offsets, cap, edges, src_of, z, x, edge_ref, feats, sum_refs, adj_ref, tgt_ref, static
):
    n = len(offsets)

    def block_of(j, src):
        if len(feats) == n:
            return feats[j][src]
        low, high = feats
        half = low.shape[0]
        return jnp.where(src < half, low[jnp.minimum(src, half - 1)], high[jnp.maximum(src - half, 0)])


    def slots(dx):
        owner = lax.rem(x + dx, X)
        counts = jnp.zeros((TAIL, BS), F32)
        if tgt_ref is not None:
            last = lax.broadcasted_iota(jnp.int32, (TAIL, BS), 0) == TAIL - 1
            counts = jnp.where(last, tgt_ref[...].astype(F32), 0.0)
        parts = []
        for j, off in enumerate(offsets):
            row = lax.rem(z + off + Z, Z) * X + owner
            packed = edge_ref[row]
            for c in range(cap):
                k = j * cap + c
                e = packed[c : c + 1, :edges]
                rt = one_hot_t(lax.shift_right_logical(e, 7), BS)
                ct = one_hot_t(jnp.bitwise_and(e, BS - 1), BS)
                a = dot_nt(rt, ct).astype(BF16)
                adj_ref[j, dx, c] = dot_nt(ct, rt).astype(BF16)
                part = jnp.dot(a, block_of(j, src_of(row, c)), preferred_element_type=F32)
                parts.append(part.astype(BF16))
                pick = jnp.where(
                    lax.broadcasted_iota(jnp.int32, (TAIL, edges), 0) == k, 1.0, 0.0
                ).astype(BF16)
                counts = counts + dot_nt(pick, rt)
        parts.append(counts.astype(BF16))
        return parts

    def store(out, parts):
        for k, part in enumerate(parts):
            out[k * BS : k * BS + part.shape[0], :] = part

    if static:
        for d, out in enumerate(sum_refs):
            store(out, slots(d))
        return

    def owner_step(dx, carry):
        parts = slots(dx)
        for d, out in enumerate(sum_refs):
            pl.when(dx == d)(functools.partial(store, out, parts))
        return carry

    lax.fori_loop(0, X, owner_step, 0)


def batch_shapes(n, cap):
    return [jax.ShapeDtypeStruct((n * cap * BS + TAIL, BS), BF16)] * X + [
        jax.ShapeDtypeStruct((n, X, cap, BS, BS), BF16)
    ]


def pack_kernel(cap, edges, src_ref, dst_ref, used_ref, rows_ref, cols_ref, lists_ref):
    owners = rows_ref.shape[1]
    rest = LISTS - edges
    meta_slot = lax.broadcasted_iota(jnp.int32, (cap, rest), 0)
    meta_lane = lax.broadcasted_iota(jnp.int32, (cap, rest), 1)
    slot = lax.broadcasted_iota(jnp.int32, (cap, edges), 0)

    def pack(o, carry):
        packed = rows_ref[0, o] * BS + cols_ref[0, o]
        meta = jnp.zeros((cap, rest), jnp.int32)
        for c in range(cap):
            to = jnp.where(c < used_ref[0, o], dst_ref[c, o], -1)
            packed = jnp.where(jnp.logical_and(slot == c, to < 0), BS * BS, packed)
            value = jnp.where(meta_lane == 0, src_ref[c, o], to)
            meta = jnp.where(meta_slot == c, value, meta)
        lists_ref[o, :, :edges] = packed
        lists_ref[o, :, edges:] = meta
        return carry

    lax.fori_loop(0, owners, pack, 0, unroll=4)


def pack(src, dst, used, rows, cols):
    owners, cap, edges = rows.shape[1:]
    whole = pl.BlockSpec(rows.shape, lambda i: (0, 0, 0, 0))
    return pl.pallas_call(
        functools.partial(pack_kernel, cap, edges),
        grid=(1,),
        in_specs=[SMEM_SPEC] * 3 + [whole] * 2,
        out_specs=VMEM_SPEC,
        out_shape=jax.ShapeDtypeStruct((owners, cap, LISTS), jnp.int32),
        compiler_params=params(4),
        cost_estimate=cost(2),
        name="pack",
    )(src, dst, used, rows, cols)


def build_kernel(offsets, cap, edges, own, static, n_feats, extra, after, src_ref, pos_ref, edge_ref, *refs):
    feats, refs = refs[:n_feats], refs[n_feats:]
    tgt_ref = refs[0] if extra else None
    refs = refs[extra + after :]

    def src_of(row, c):
        if own:
            return src_ref[c, row]
        return src_ref[row * cap + c]

    build_batch(
        offsets,
        cap,
        edges,
        src_of,
        pos_ref[0],
        pos_ref[1],
        edge_ref,
        feats,
        refs[:X],
        refs[X],
        tgt_ref,
        static,
    )


def build(offsets, cap, edges, src, pos, edge_list, feats, after, own=False, extra=(), static=False):
    n = len(offsets)
    return pl.pallas_call(
        functools.partial(
            build_kernel, offsets, cap, edges, own, static, len(feats), len(extra), len(after)
        ),
        in_specs=[SMEM_SPEC, SMEM_SPEC] + [VMEM_SPEC] * (1 + len(feats) + len(extra)) + [ANY_SPEC] * len(after),
        out_specs=[VMEM_SPEC] * (X + 1),
        out_shape=batch_shapes(n, cap),
        compiler_params=params(8),
        cost_estimate=cost(2.5 * n),
        name="build",
    )(src, pos, edge_list, *feats, *extra, *after)


def follow(arrays, after):
    n = len(arrays)
    return pl.pallas_call(
        lambda *refs: None,
        in_specs=[ANY_SPEC] * (n + len(after)),
        out_specs=[ANY_SPEC] * n,
        out_shape=[jax.ShapeDtypeStruct(a.shape, a.dtype) for a in arrays],
        input_output_aliases={i: i for i in range(n)},
        compiler_params=params(1),
        cost_estimate=cost(0.3),
        name="follow",
    )(*arrays, *after)


def gather_kernel(batches, cap, pos_ref, *refs):
    total = len(batches) * X
    got, refs = refs[:total], refs[total:]
    keeps, sends, (tgt_out, acc, acc_c, tgt_ref, sem) = refs[:Y], refs[Y : 2 * Y], refs[2 * Y :]
    targets = acc.shape[0]
    z, x, y, core = pos_ref[0], pos_ref[1], pos_ref[2], pos_ref[3]
    rows = [got[2 * X + d][-TAIL:, :].astype(F32)[TAIL - 1 :, :] for d in range(X)]
    tgt_out[...] = jnp.concatenate(rows + rows, axis=0).astype(jnp.int32)
    copy = pltpu.make_async_copy(tgt_out, tgt_ref, sem)
    copy.start()

    def clear(i, carry):
        acc[i] = jnp.zeros((BS, BS), F32)
        return carry

    lax.fori_loop(0, targets, clear, 0, unroll=4)
    acc_c[...] = jnp.zeros_like(acc_c)
    copy.wait()
    for b, offsets in enumerate(batches):
        n = len(offsets)
        for dx in range(X):
            ref = got[b * X + dx]
            tail = ref[n * cap * BS :, :].astype(F32)
            first = lax.rem(z + offsets[0] + Z, Z)
            apart = offsets[-1] - offsets[0]

            def add(j, carry, ref=ref, dx=dx, tail=tail, first=first, apart=apart):
                sender_z = lax.rem(first + j * apart, Z)
                for c in range(cap):
                    k = j * cap + c
                    t = tgt_ref[dx, (sender_z * X + x) * cap + c]

                    @pl.when(t >= 0)
                    def _():
                        rows = ref[pl.ds(pl.multiple_of(k * BS, BS), BS), :]
                        acc[t] += rows.astype(F32)
                        here = lax.broadcasted_iota(jnp.int32, tail.shape, 0) == k
                        count = jnp.sum(jnp.where(here, tail, 0.0), axis=0, keepdims=True)
                        acc_c[pl.ds(t, 1), :] += count

                return carry

            lax.fori_loop(0, n, add, 0)

    blocks = targets // (Y * C)
    for dy in range(Y):
        for out, to_core in ((keeps[dy], core), (sends[dy], 1 - core)):
            first = (lax.rem(y + dy, Y) * C + to_core) * blocks

            def store(i, carry, out=out, first=first):
                out[pl.ds(pl.multiple_of(i * BS, BS), BS), :] = acc[first + i].astype(BF16)
                return carry

            lax.fori_loop(0, blocks, store, 0, unroll=4)
            count = acc_c[pl.ds(pl.multiple_of(first, blocks), blocks), :]
            put_counts(out, blocks * BS, count)


def put_counts(out, first, count):
    n = count.shape[0]
    for i in range(DIGITS):
        rest = jnp.floor(count * (1.0 / 256.0))
        out[first + i * n : first + (i + 1) * n, :] = (count - 256.0 * rest).astype(BF16)
        count = rest


def get_counts(digits):
    n = digits.shape[0] // DIGITS
    return sum(digits[i * n : (i + 1) * n] * 256.0**i for i in range(DIGITS))


def gather_sums(batches, cap, targets, pos, got):
    blocks = targets // (Y * C)
    part = jax.ShapeDtypeStruct((blocks * (BS + DIGITS), BS), BF16)
    out = pl.pallas_call(
        functools.partial(gather_kernel, batches, cap),
        in_specs=[SMEM_SPEC] + [VMEM_SPEC] * len(got),
        out_specs=[VMEM_SPEC] * (2 * Y + 1),
        out_shape=[part] * (2 * Y) + [jax.ShapeDtypeStruct((2 * X, BS), jnp.int32)],
        scratch_shapes=[
            pltpu.VMEM((targets, BS, BS), F32),
            pltpu.VMEM((targets, BS), F32),
            pltpu.SMEM((2 * X, BS), jnp.int32),
            pltpu.SemaphoreType.DMA,
        ],
        compiler_params=params(16),
        cost_estimate=cost(5),
        name="gather_sums",
    )(pos, *got)
    return out[:Y], out[Y : 2 * Y], out[2 * Y]


def join_kernel(kind, a_ref, b_ref, *refs):
    blocks = a_ref.shape[0] // (BS + DIGITS)
    half = blocks // 2

    def add(out_ref, first, to, n, extra_ref=None):
        def step(i, carry):
            rows = pl.ds(pl.multiple_of((first + i) * BS, BS), BS)
            value = a_ref[rows, :].astype(F32) + b_ref[rows, :].astype(F32)
            if extra_ref is not None:
                value += extra_ref[pl.ds(pl.multiple_of(i * BS, BS), BS), :].astype(F32)
            out_ref[pl.ds(pl.multiple_of((to + i) * BS, BS), BS), :] = value.astype(BF16)
            return carry

        lax.fori_loop(0, n, step, 0, unroll=2)

    digits = a_ref[blocks * BS :, :].astype(F32) + b_ref[blocks * BS :, :].astype(F32)
    if kind == "cut":
        low_ref, high_ref = refs
        add(low_ref, 0, 0, half)
        put_counts(low_ref, half * BS, get_counts(digits))
        add(high_ref, half, 0, half)
        return
    extra_ref, out_ref = refs
    add(out_ref, 0, 0, half, extra_ref if kind == "low" else None)
    add(out_ref, half, half, half, extra_ref if kind == "high" else None)
    if kind == "low":
        digits += extra_ref[half * BS :, :].astype(F32)
    put_counts(out_ref, blocks * BS, get_counts(digits))


def join(kind, a, b, *extra):
    rows = a.shape[0]
    half = rows // (BS + DIGITS) // 2 * BS
    outs = [rows - half, half] if kind == "cut" else [rows]
    return pl.pallas_call(
        functools.partial(join_kernel, kind),
        in_specs=[VMEM_SPEC] * (2 + len(extra)),
        out_specs=[VMEM_SPEC] * len(outs),
        out_shape=[jax.ShapeDtypeStruct((n, BS), BF16) for n in outs],
        compiler_params=params(4),
        cost_estimate=cost(0.6),
        name="join",
    )(a, b, *extra)


def pick_kernel(sets, cap, tgt_ref, pos_ref, *refs):
    means, outs, (mean_ref, sem) = refs[: Y * C], refs[Y * C + 1 : -2], refs[-2:]
    z, x, y, core = pos_ref[0], pos_ref[1], pos_ref[2], pos_ref[3]
    blocks = means[0].shape[0]
    copies = []
    for i, ref in enumerate(means):
        from_core = core if i % C == 0 else 1 - core
        first = (lax.rem(y - i // C + Y, Y) * C + from_core) * blocks
        copies.append(pltpu.make_async_copy(ref, mean_ref.at[pl.ds(first, blocks)], sem.at[i]))
        copies[-1].start()
    for copy in copies:
        copy.wait()
    for i, offsets in enumerate(sets):
        for dx in range(X):
            for j, off in enumerate(offsets):
                sender_z = lax.rem(z + off + Z, Z)
                for c in range(cap):
                    t = tgt_ref[dx, (sender_z * X + x) * cap + c]
                    outs[i * X + dx][j * cap + c] = mean_ref[jnp.maximum(t, 0)]


def pick(sets, cap, tgt, pos, means, after):
    shapes = []
    for offsets in sets:
        shapes += [jax.ShapeDtypeStruct((len(offsets) * cap, BS, BS), BF16)] * X
    out = pl.pallas_call(
        functools.partial(pick_kernel, sets, cap),
        in_specs=[SMEM_SPEC, SMEM_SPEC] + [ANY_SPEC] * (len(means) + 1),
        out_specs=[VMEM_SPEC] * len(shapes),
        out_shape=shapes,
        scratch_shapes=[
            pltpu.VMEM((len(means) * means[0].shape[0], BS, BS), BF16),
            pltpu.SemaphoreType.DMA((len(means),)),
        ],
        compiler_params=params(8),
        cost_estimate=cost(3),
        name="pick",
    )(tgt, pos, *means, after)
    return [out[i * X : (i + 1) * X] for i in range(len(sets))]


def spread_kernel(offsets, starts, cap, cuts, after, src_ref, pos_ref, adj_ref, *refs):
    n = len(offsets)
    got, refs = refs[:X], refs[X:]
    inits = []
    for parts in starts:
        inits.append([(lo, hi, refs[i]) for i, (lo, hi) in enumerate(parts)])
        refs = refs[len(parts) :]
    outs, acc = refs[after:-1], refs[-1]
    blocks = acc.shape[1]
    z, x = pos_ref[0], pos_ref[1]
    for j in range(n):
        if len(inits[j]) == 0 or inits[j][0][:2] != (0, blocks):
            acc[j] = jnp.zeros(acc.shape[1:], F32)
        for i, (lo, hi, ref) in enumerate(inits[j]):
            if i == 0:
                acc[j, lo:hi] = ref[...].astype(F32)
            else:
                acc[j, lo:hi] += ref[...].astype(F32)
    first = lax.rem(z + offsets[0] + Z, Z)
    apart = offsets[-1] - offsets[0]

    def add(j, carry):
        sender = lax.rem(first + j * apart, Z)
        for dx in range(X):
            owner = lax.rem(x + dx, X)
            for c in range(cap):
                src = src_ref[(sender * X + owner) * cap + c]
                acc[j, src] += jnp.dot(
                    adj_ref[j, dx, c], got[dx][j * cap + c], preferred_element_type=F32
                )
        return carry

    lax.fori_loop(0, n, add, 0)
    for out, (j, lo, hi) in zip(outs, cuts):
        out[...] = acc[j, lo:hi].astype(BF16)


def spread(offsets, cap, blocks, src, pos, adj, got, starts, cuts=None, after=()):
    n = len(offsets)
    cuts = [(j, 0, blocks) for j in range(n)] if cuts is None else cuts
    return pl.pallas_call(
        functools.partial(
            spread_kernel, offsets, [[(lo, hi) for lo, hi, _ in s] for s in starts], cap, cuts, len(after)
        ),
        in_specs=[SMEM_SPEC, SMEM_SPEC] + [VMEM_SPEC] * (1 + X + sum(len(s) for s in starts))
        + [ANY_SPEC] * len(after),
        out_specs=[VMEM_SPEC] * len(cuts),
        out_shape=[jax.ShapeDtypeStruct((hi - lo, BS, BS), BF16) for _, lo, hi in cuts],
        scratch_shapes=[pltpu.VMEM((n, blocks, BS, BS), F32)],
        compiler_params=params(8),
        cost_estimate=cost(1.2 * n),
        name="spread",
    )(src, pos, adj, *got, *[a for s in starts for _, _, a in s], *after)


def halves(up, down):
    half = up.shape[0] // 2

    def kernel(up_ref, down_ref, low_ref, high_ref):
        low_ref[...] = up_ref[:half]
        high_ref[...] = down_ref[half:]

    return pl.pallas_call(
        kernel,
        in_specs=[VMEM_SPEC] * 2,
        out_specs=[VMEM_SPEC] * 2,
        out_shape=[jax.ShapeDtypeStruct((half,) + up.shape[1:], up.dtype)] * 2,
        compiler_params=params(4),
        cost_estimate=cost(0.3),
        name="halves",
    )(up, down)


def sum_copies(parts, copies):
    def kernel(in_ref, out_ref):
        total = jnp.sum(in_ref[...], axis=0)
        for i in range(copies):
            out_ref[i] = total

    return pl.pallas_call(
        kernel,
        in_specs=[VMEM_SPEC],
        out_specs=VMEM_SPEC,
        out_shape=jax.ShapeDtypeStruct((copies,) + parts.shape[1:], F32),
        compiler_params=params(4),
        cost_estimate=cost(0.5),
        name="sum_copies",
    )(parts)


def attach(arrays, column):
    rows, width = column.shape
    n = arrays[0].shape[0]

    def kernel(*refs):
        ins, value, outs = refs[:X], refs[X][...], refs[X + 1 :]
        high = value.astype(BF16)
        low = (value - high.astype(F32)).astype(BF16)
        for in_ref, out_ref in zip(ins, outs):
            out_ref[:n] = in_ref[...]
            for i, part in enumerate((high, low)):
                for half in range(width // BS):
                    out_ref[n + i, half * rows : (half + 1) * rows, :] = part[
                        :, half * BS : (half + 1) * BS
                    ]

    return pl.pallas_call(
        kernel,
        in_specs=[VMEM_SPEC] * (X + 1),
        out_specs=[VMEM_SPEC] * X,
        out_shape=[jax.ShapeDtypeStruct((n + 2, BS, BS), BF16)] * X,
        compiler_params=params(4),
        cost_estimate=cost(0.5),
        name="attach",
    )(*arrays, column)


def detach(arrays, pos, shape, scale):
    n = arrays[0].shape[0] - 2
    rows, width = shape[0] // X, shape[1]

    def kernel(pos_ref, *refs):
        ins, (a_ref, b_ref, whole) = refs[:X], refs[X:]
        for d, ref in enumerate(ins):
            value = (ref[n].astype(F32) + ref[n + 1].astype(F32)) * scale
            first = pl.multiple_of(lax.rem(pos_ref[1] + d, X) * rows, rows)
            for half in range(width // BS):
                whole[pl.ds(first, rows), half * BS : (half + 1) * BS] = value[
                    half * rows : (half + 1) * rows, :
                ]
        a_ref[...] = whole[: shape[0] // 2]
        b_ref[...] = whole[shape[0] // 2 :]

    return pl.pallas_call(
        kernel,
        in_specs=[SMEM_SPEC] + [VMEM_SPEC] * X,
        out_specs=[VMEM_SPEC] * 2,
        out_shape=[jax.ShapeDtypeStruct((shape[0] // 2, width), F32)] * 2,
        scratch_shapes=[pltpu.VMEM(shape, F32)],
        compiler_params=params(4),
        cost_estimate=cost(0.5),
        name="detach",
    )(pos, *arrays)


def own_part(grad_pre, w_self, blocks):
    def kernel(grad_ref, w_ref, out_ref):
        for i in range(blocks):
            out_ref[i] = dot_nt(grad_ref[i * BS : (i + 1) * BS, :], w_ref[...])

    return pl.pallas_call(
        kernel,
        in_specs=[VMEM_SPEC] * 2,
        out_specs=VMEM_SPEC,
        out_shape=jax.ShapeDtypeStruct((blocks, BS, BS), F32),
        compiler_params=params(8),
        cost_estimate=cost(1.5),
        name="own_part",
    )(grad_pre, w_self)


def shift(value, axis, size, by):
    return lax.ppermute(value, axis, [(i, (i + by) % size) for i in range(size)])


def shift_x(values, sign):
    return [values[0]] + [shift(values[d], "x", X, sign * d) for d in range(1, X)]


def exchange(value, axes):
    return lax.all_to_all(value, axes, split_axis=0, concat_axis=0, tiled=True)


def on_device(
    features, w_self, w_neigh, cotangent, src_block, dst_block, block_count, edge_rows, edge_cols
):
    owners, cap = src_block.shape[1:]
    edges = edge_rows.shape[-1]
    local_nodes = features.shape[0]
    blocks = local_nodes // BS
    half = blocks // 2
    groups = Y * C
    node_total = local_nodes * groups * owners
    pos = jnp.stack([lax.axis_index(a) for a in ("z", "x", "y", "c")]).astype(jnp.int32)
    feats = features.reshape(blocks, BS, -1)

    own_src = src_block[0].T
    sent = pack(own_src, dst_block[0].T, block_count, edge_rows, edge_cols)
    lists = exchange(sent, "z")
    src = lists[:, :, edges].reshape(owners * cap)
    tgt = lists[:, :, edges + 1].reshape(1, owners * cap)

    batches = [(0,), (-1, 1), (-2, 2), (-3, 3), (4,)]
    *part, adj = build(batches[0], cap, edges, own_src, pos, sent, [feats], [], own=True)
    sums, adjs = [shift_x(part, 1)], [adj]
    up, down, last = feats, feats, [part[0], lists]
    for k in range(1, 5):
        if k < 4:
            up, down = follow([shift(up, "z", Z, 1), shift(down, "z", Z, -1)], last)
            arrays = [up, down]
        else:
            low, high = halves(up, down)
            arrays = [shift(low, "z", Z, 1), shift(high, "z", Z, -1)]
        after = sums[k - 2][1:] if k > 1 else []
        *part, adj = build(batches[k], cap, edges, src, pos, lists, arrays, after, extra=[tgt] if k == 2 else (), static=k == 1)
        sums.append(shift_x(part, 1))
        adjs.append(adj)
        last = part[:1] + (sums[0][1:] if k == 1 else [])
    keeps, sends, tgt = gather_sums(batches, cap, groups * blocks, pos, sum(sums, []))

    crossed = [shift(sends[dy], "c", C, 1) for dy in (2, 1, 3, 0)]
    low, high = join("cut", keeps[2], crossed[0])
    low, high = shift(low, "y", Y, 1), shift(high, "y", Y, -1)
    (ahead,) = join("low", keeps[1], crossed[1], low)
    (behind,) = join("high", keeps[3], crossed[2], high)
    arrived = [keeps[0], crossed[3], shift(ahead, "y", Y, 1), shift(behind, "y", Y, -1)]
    total = sum(a.astype(F32) for a in arrived)
    own_sums, own_cnt = total[:local_nodes], get_counts(total[local_nodes:])
    divisor = jnp.maximum(own_cnt, 1.0).reshape(local_nodes, 1)
    neigh_mean = (own_sums / divisor).astype(BF16)
    preact = jnp.dot(features, w_self, preferred_element_type=F32) + jnp.dot(
        neigh_mean, w_neigh, preferred_element_type=F32
    )
    sigmoids = jax.nn.sigmoid(preact)
    activated = (preact * sigmoids).astype(BF16)
    grad_pre = (cotangent.astype(F32) * sigmoids * (1.0 + preact * (1.0 - sigmoids))).astype(BF16)
    grad_mean = (
        jnp.einsum("nh,fh->nf", grad_pre, w_neigh, preferred_element_type=F32) / divisor
    ).astype(BF16)
    grad_mean = grad_mean.reshape(blocks, BS, -1)
    means = [grad_mean] + [shift(grad_mean, "y", Y, dy) for dy in range(1, Y)]

    both = jnp.concatenate([features, neigh_mean], axis=1)
    grads = jnp.einsum("nf,nh->fh", both, grad_pre, preferred_element_type=F32)
    width = grads.shape[1]
    piece = sum_copies(exchange(grads, ("x", "z")).reshape(owners, -1, width), groups)
    first_piece = piece
    means[1:] = follow(means[1:], [first_piece])
    means = [m for mean in means for m in (mean, shift(mean, "c", C, 1))]
    sets = [(4,), (-3, 3), (-2, 2), (-1, 1), (0,)]
    picked = pick(sets, cap, tgt, pos, means, first_piece)
    piece = sum_copies(exchange(piece, ("y", "c")), Z)
    column = exchange(piece, "z").reshape(-1, width)
    picked[4] = attach(picked[4], column)

    own_term = own_part(grad_pre, w_self, blocks)
    got = [shift_x(p, -1) for p in picked]

    def back(k, starts, cuts=None, after=()):
        return spread(
            batches[k], cap, blocks, src, pos, adjs[k], got[4 - k], starts, cuts, after
        )

    low, high = back(4, [[]], [(0, 0, half), (0, half, blocks)])
    up, down = shift(low, "z", Z, 1), shift(high, "z", Z, -1)
    down, up = back(3, [[(half, blocks, down)], [(0, half, up)]])
    for k in (2, 1):
        up, down = shift(up, "z", Z, 1), shift(down, "z", Z, -1)
        after = [piece] if k == 2 else [column]
        down, up = back(k, [[(0, blocks, down)], [(0, blocks, up)]], after=after)
    up, down = shift(up, "z", Z, 1), shift(down, "z", Z, -1)
    (grad_features,) = back(0, [[(0, blocks, own_term), (0, blocks, up), (0, blocks, down)]])
    grad_self, grad_neigh = detach(got[4], pos, grads.shape, float(node_total) ** (-0.5))
    return activated, grad_features.reshape(local_nodes, -1), grad_self, grad_neigh


def solution(mesh):
    mesh = Mesh(mesh.devices.reshape(Y, C, Z, X), ("y", "c", "z", "x"))
    every = ("y", "c", "z", "x")
    return jax.shard_map(
        on_device,
        mesh=mesh,
        in_specs=(
            P(every, None),
            P(),
            P(),
            P(every, None),
            P(every, None, None),
            P(every, None, None),
            P(every, None),
            P(every, None, None, None),
            P(every, None, None, None),
        ),
        out_specs=(P(every, None), P(every, None), P(), P()),
        check_vma=False,
    )
```

```python
import functools

import jax
import jax.numpy as jnp
from jax import lax
from jax.experimental import pallas as pl
from jax.experimental.pallas import tpu as pltpu
from jax.sharding import Mesh, PartitionSpec as P

BS = 128
TAIL = 16
Y, C, Z, X = 4, 2, 8, 4
F32 = jnp.float32
BF16 = jnp.bfloat16
MIB = 1024 * 1024
NT = (((1,), (1,)), ((), ()))
SMEM_SPEC = pl.BlockSpec(memory_space=pltpu.SMEM)
VMEM_SPEC = pl.BlockSpec(memory_space=pltpu.VMEM)
ANY_SPEC = pl.BlockSpec(memory_space=pl.ANY)
LISTS = 256
DIGITS = 3


def dot_nt(a, b):
    return lax.dot_general(a, b, NT, preferred_element_type=F32)


def params(mib):
    return pltpu.CompilerParams(vmem_limit_bytes=mib * MIB)


def cost(us):
    return pl.CostEstimate(flops=0, bytes_accessed=int(us * 3.5e6), transcendentals=0)


def one_hot_t(row, extent):
    ids = lax.broadcasted_iota(jnp.int32, (extent, row.shape[1]), 0)
    return jnp.where(ids == row, 1.0, 0.0).astype(BF16)


def build_batch(
    offsets, cap, edges, src_of, z, x, edge_ref, feats, sum_refs, adj_ref, tgt_ref, static
):
    n = len(offsets)

    def block_of(j, src):
        if len(feats) == n:
            return feats[j][src]
        low, high = feats
        half = low.shape[0]
        return jnp.where(src < half, low[jnp.minimum(src, half - 1)], high[jnp.maximum(src - half, 0)])


    def slots(dx):
        owner = lax.rem(x + dx, X)
        counts = jnp.zeros((TAIL, BS), F32)
        if tgt_ref is not None:
            last = lax.broadcasted_iota(jnp.int32, (TAIL, BS), 0) == TAIL - 1
            counts = jnp.where(last, tgt_ref[...].astype(F32), 0.0)
        parts = []
        for j, off in enumerate(offsets):
            row = lax.rem(z + off + Z, Z) * X + owner
            packed = edge_ref[row]
            for c in range(cap):
                k = j * cap + c
                e = packed[c : c + 1, :edges]
                rt = one_hot_t(lax.shift_right_logical(e, 7), BS)
                ct = one_hot_t(jnp.bitwise_and(e, BS - 1), BS)
                a = dot_nt(rt, ct).astype(BF16)
                adj_ref[j, dx, c] = dot_nt(ct, rt).astype(BF16)
                part = jnp.dot(a, block_of(j, src_of(row, c)), preferred_element_type=F32)
                parts.append(part.astype(BF16))
                pick = jnp.where(
                    lax.broadcasted_iota(jnp.int32, (TAIL, edges), 0) == k, 1.0, 0.0
                ).astype(BF16)
                counts = counts + dot_nt(pick, rt)
        parts.append(counts.astype(BF16))
        return parts

    def store(out, parts):
        for k, part in enumerate(parts):
            out[k * BS : k * BS + part.shape[0], :] = part

    if static:
        for d, out in enumerate(sum_refs):
            store(out, slots(d))
        return

    def owner_step(dx, carry):
        parts = slots(dx)
        for d, out in enumerate(sum_refs):
            pl.when(dx == d)(functools.partial(store, out, parts))
        return carry

    lax.fori_loop(0, X, owner_step, 0)


def batch_shapes(n, cap):
    return [jax.ShapeDtypeStruct((n * cap * BS + TAIL, BS), BF16)] * X + [
        jax.ShapeDtypeStruct((n, X, cap, BS, BS), BF16)
    ]


def pack_kernel(cap, edges, src_ref, dst_ref, used_ref, rows_ref, cols_ref, lists_ref):
    owners = rows_ref.shape[1]
    rest = LISTS - edges
    meta_slot = lax.broadcasted_iota(jnp.int32, (cap, rest), 0)
    meta_lane = lax.broadcasted_iota(jnp.int32, (cap, rest), 1)
    slot = lax.broadcasted_iota(jnp.int32, (cap, edges), 0)

    def pack(o, carry):
        packed = rows_ref[0, o] * BS + cols_ref[0, o]
        meta = jnp.zeros((cap, rest), jnp.int32)
        for c in range(cap):
            to = jnp.where(c < used_ref[0, o], dst_ref[c, o], -1)
            packed = jnp.where(jnp.logical_and(slot == c, to < 0), BS * BS, packed)
            value = jnp.where(meta_lane == 0, src_ref[c, o], to)
            meta = jnp.where(meta_slot == c, value, meta)
        lists_ref[o, :, :edges] = packed
        lists_ref[o, :, edges:] = meta
        return carry

    lax.fori_loop(0, owners, pack, 0, unroll=4)


def pack(src, dst, used, rows, cols):
    owners, cap, edges = rows.shape[1:]
    whole = pl.BlockSpec(rows.shape, lambda i: (0, 0, 0, 0))
    return pl.pallas_call(
        functools.partial(pack_kernel, cap, edges),
        grid=(1,),
        in_specs=[SMEM_SPEC] * 3 + [whole] * 2,
        out_specs=VMEM_SPEC,
        out_shape=jax.ShapeDtypeStruct((owners, cap, LISTS), jnp.int32),
        compiler_params=params(4),
        cost_estimate=cost(2),
        name="pack",
    )(src, dst, used, rows, cols)


def build_kernel(offsets, cap, edges, own, static, n_feats, extra, after, src_ref, pos_ref, edge_ref, *refs):
    feats, refs = refs[:n_feats], refs[n_feats:]
    tgt_ref = refs[0] if extra else None
    refs = refs[extra + after :]

    def src_of(row, c):
        if own:
            return src_ref[c, row]
        return src_ref[row * cap + c]

    build_batch(
        offsets,
        cap,
        edges,
        src_of,
        pos_ref[0],
        pos_ref[1],
        edge_ref,
        feats,
        refs[:X],
        refs[X],
        tgt_ref,
        static,
    )


def build(offsets, cap, edges, src, pos, edge_list, feats, after, own=False, extra=(), static=False):
    n = len(offsets)
    return pl.pallas_call(
        functools.partial(
            build_kernel, offsets, cap, edges, own, static, len(feats), len(extra), len(after)
        ),
        in_specs=[SMEM_SPEC, SMEM_SPEC] + [VMEM_SPEC] * (1 + len(feats) + len(extra)) + [ANY_SPEC] * len(after),
        out_specs=[VMEM_SPEC] * (X + 1),
        out_shape=batch_shapes(n, cap),
        compiler_params=params(8),
        cost_estimate=cost(2.5 * n),
        name="build",
    )(src, pos, edge_list, *feats, *extra, *after)


def follow(arrays, after):
    n = len(arrays)
    return pl.pallas_call(
        lambda *refs: None,
        in_specs=[ANY_SPEC] * (n + len(after)),
        out_specs=[ANY_SPEC] * n,
        out_shape=[jax.ShapeDtypeStruct(a.shape, a.dtype) for a in arrays],
        input_output_aliases={i: i for i in range(n)},
        compiler_params=params(1),
        cost_estimate=cost(0.3),
        name="follow",
    )(*arrays, *after)


def gather_kernel(batches, cap, pos_ref, *refs):
    total = len(batches) * X
    got, refs = refs[:total], refs[total:]
    keeps, sends, (tgt_out, acc, acc_c, tgt_ref, sem) = refs[:Y], refs[Y : 2 * Y], refs[2 * Y :]
    targets = acc.shape[0]
    z, x, y, core = pos_ref[0], pos_ref[1], pos_ref[2], pos_ref[3]
    rows = [got[2 * X + d][-TAIL:, :].astype(F32)[TAIL - 1 :, :] for d in range(X)]
    tgt_out[...] = jnp.concatenate(rows + rows, axis=0).astype(jnp.int32)
    copy = pltpu.make_async_copy(tgt_out, tgt_ref, sem)
    copy.start()

    def clear(i, carry):
        acc[i] = jnp.zeros((BS, BS), F32)
        return carry

    lax.fori_loop(0, targets, clear, 0, unroll=4)
    acc_c[...] = jnp.zeros_like(acc_c)
    copy.wait()
    for b, offsets in enumerate(batches):
        n = len(offsets)
        for dx in range(X):
            ref = got[b * X + dx]
            tail = ref[n * cap * BS :, :].astype(F32)
            first = lax.rem(z + offsets[0] + Z, Z)
            apart = offsets[-1] - offsets[0]

            def add(j, carry, ref=ref, dx=dx, tail=tail, first=first, apart=apart):
                sender_z = lax.rem(first + j * apart, Z)
                for c in range(cap):
                    k = j * cap + c
                    t = tgt_ref[dx, (sender_z * X + x) * cap + c]

                    @pl.when(t >= 0)
                    def _():
                        rows = ref[pl.ds(pl.multiple_of(k * BS, BS), BS), :]
                        acc[t] += rows.astype(F32)
                        here = lax.broadcasted_iota(jnp.int32, tail.shape, 0) == k
                        count = jnp.sum(jnp.where(here, tail, 0.0), axis=0, keepdims=True)
                        acc_c[pl.ds(t, 1), :] += count

                return carry

            lax.fori_loop(0, n, add, 0)

    blocks = targets // (Y * C)
    for dy in range(Y):
        for out, to_core in ((keeps[dy], core), (sends[dy], 1 - core)):
            first = (lax.rem(y + dy, Y) * C + to_core) * blocks

            def store(i, carry, out=out, first=first):
                out[pl.ds(pl.multiple_of(i * BS, BS), BS), :] = acc[first + i].astype(BF16)
                return carry

            lax.fori_loop(0, blocks, store, 0, unroll=4)
            count = acc_c[pl.ds(pl.multiple_of(first, blocks), blocks), :]
            put_counts(out, blocks * BS, count)


def put_counts(out, first, count):
    n = count.shape[0]
    for i in range(DIGITS):
        rest = jnp.floor(count * (1.0 / 256.0))
        out[first + i * n : first + (i + 1) * n, :] = (count - 256.0 * rest).astype(BF16)
        count = rest


def get_counts(digits):
    n = digits.shape[0] // DIGITS
    return sum(digits[i * n : (i + 1) * n] * 256.0**i for i in range(DIGITS))


def gather_sums(batches, cap, targets, pos, got):
    blocks = targets // (Y * C)
    part = jax.ShapeDtypeStruct((blocks * (BS + DIGITS), BS), BF16)
    out = pl.pallas_call(
        functools.partial(gather_kernel, batches, cap),
        in_specs=[SMEM_SPEC] + [VMEM_SPEC] * len(got),
        out_specs=[VMEM_SPEC] * (2 * Y + 1),
        out_shape=[part] * (2 * Y) + [jax.ShapeDtypeStruct((2 * X, BS), jnp.int32)],
        scratch_shapes=[
            pltpu.VMEM((targets, BS, BS), F32),
            pltpu.VMEM((targets, BS), F32),
            pltpu.SMEM((2 * X, BS), jnp.int32),
            pltpu.SemaphoreType.DMA,
        ],
        compiler_params=params(16),
        cost_estimate=cost(5),
        name="gather_sums",
    )(pos, *got)
    return out[:Y], out[Y : 2 * Y], out[2 * Y]


def join_kernel(kind, a_ref, b_ref, *refs):
    blocks = a_ref.shape[0] // (BS + DIGITS)
    half = blocks // 2

    def add(out_ref, first, to, n, extra_ref=None):
        def step(i, carry):
            rows = pl.ds(pl.multiple_of((first + i) * BS, BS), BS)
            value = a_ref[rows, :].astype(F32) + b_ref[rows, :].astype(F32)
            if extra_ref is not None:
                value += extra_ref[pl.ds(pl.multiple_of(i * BS, BS), BS), :].astype(F32)
            out_ref[pl.ds(pl.multiple_of((to + i) * BS, BS), BS), :] = value.astype(BF16)
            return carry

        lax.fori_loop(0, n, step, 0, unroll=2)

    digits = a_ref[blocks * BS :, :].astype(F32) + b_ref[blocks * BS :, :].astype(F32)
    if kind == "cut":
        low_ref, high_ref = refs
        add(low_ref, 0, 0, half)
        put_counts(low_ref, half * BS, get_counts(digits))
        add(high_ref, half, 0, half)
        return
    extra_ref, out_ref = refs
    add(out_ref, 0, 0, half, extra_ref if kind == "low" else None)
    add(out_ref, half, half, half, extra_ref if kind == "high" else None)
    if kind == "low":
        digits += extra_ref[half * BS :, :].astype(F32)
    put_counts(out_ref, blocks * BS, get_counts(digits))


def join(kind, a, b, *extra):
    rows = a.shape[0]
    half = rows // (BS + DIGITS) // 2 * BS
    outs = [rows - half, half] if kind == "cut" else [rows]
    return pl.pallas_call(
        functools.partial(join_kernel, kind),
        in_specs=[VMEM_SPEC] * (2 + len(extra)),
        out_specs=[VMEM_SPEC] * len(outs),
        out_shape=[jax.ShapeDtypeStruct((n, BS), BF16) for n in outs],
        compiler_params=params(4),
        cost_estimate=cost(0.6),
        name="join",
    )(a, b, *extra)


def pick_kernel(sets, cap, tgt_ref, pos_ref, *refs):
    means, outs, (mean_ref, sem) = refs[: Y * C], refs[Y * C + 1 : -2], refs[-2:]
    z, x, y, core = pos_ref[0], pos_ref[1], pos_ref[2], pos_ref[3]
    blocks = means[0].shape[0]
    copies = []
    for i, ref in enumerate(means):
        from_core = core if i % C == 0 else 1 - core
        first = (lax.rem(y - i // C + Y, Y) * C + from_core) * blocks
        copies.append(pltpu.make_async_copy(ref, mean_ref.at[pl.ds(first, blocks)], sem.at[i]))
        copies[-1].start()
    for copy in copies:
        copy.wait()
    for i, offsets in enumerate(sets):
        for dx in range(X):
            for j, off in enumerate(offsets):
                sender_z = lax.rem(z + off + Z, Z)
                for c in range(cap):
                    t = tgt_ref[dx, (sender_z * X + x) * cap + c]
                    outs[i * X + dx][j * cap + c] = mean_ref[jnp.maximum(t, 0)]


def pick(sets, cap, tgt, pos, means, after):
    shapes = []
    for offsets in sets:
        shapes += [jax.ShapeDtypeStruct((len(offsets) * cap, BS, BS), BF16)] * X
    out = pl.pallas_call(
        functools.partial(pick_kernel, sets, cap),
        in_specs=[SMEM_SPEC, SMEM_SPEC] + [ANY_SPEC] * (len(means) + 1),
        out_specs=[VMEM_SPEC] * len(shapes),
        out_shape=shapes,
        scratch_shapes=[
            pltpu.VMEM((len(means) * means[0].shape[0], BS, BS), BF16),
            pltpu.SemaphoreType.DMA((len(means),)),
        ],
        compiler_params=params(8),
        cost_estimate=cost(3),
        name="pick",
    )(tgt, pos, *means, after)
    return [out[i * X : (i + 1) * X] for i in range(len(sets))]


def spread_kernel(offsets, starts, cap, cuts, after, src_ref, pos_ref, adj_ref, *refs):
    n = len(offsets)
    got, refs = refs[:X], refs[X:]
    inits = []
    for parts in starts:
        inits.append([(lo, hi, refs[i]) for i, (lo, hi) in enumerate(parts)])
        refs = refs[len(parts) :]
    outs, acc = refs[after:-1], refs[-1]
    blocks = acc.shape[1]
    z, x = pos_ref[0], pos_ref[1]
    for j in range(n):
        if len(inits[j]) == 0 or inits[j][0][:2] != (0, blocks):
            acc[j] = jnp.zeros(acc.shape[1:], F32)
        for i, (lo, hi, ref) in enumerate(inits[j]):
            if i == 0:
                acc[j, lo:hi] = ref[...].astype(F32)
            else:
                acc[j, lo:hi] += ref[...].astype(F32)
    first = lax.rem(z + offsets[0] + Z, Z)
    apart = offsets[-1] - offsets[0]

    def add(j, carry):
        sender = lax.rem(first + j * apart, Z)
        for dx in range(X):
            owner = lax.rem(x + dx, X)
            for c in range(cap):
                src = src_ref[(sender * X + owner) * cap + c]
                acc[j, src] += jnp.dot(
                    adj_ref[j, dx, c], got[dx][j * cap + c], preferred_element_type=F32
                )
        return carry

    lax.fori_loop(0, n, add, 0)
    for out, (j, lo, hi) in zip(outs, cuts):
        out[...] = acc[j, lo:hi].astype(BF16)


def spread(offsets, cap, blocks, src, pos, adj, got, starts, cuts=None, after=()):
    n = len(offsets)
    cuts = [(j, 0, blocks) for j in range(n)] if cuts is None else cuts
    return pl.pallas_call(
        functools.partial(
            spread_kernel, offsets, [[(lo, hi) for lo, hi, _ in s] for s in starts], cap, cuts, len(after)
        ),
        in_specs=[SMEM_SPEC, SMEM_SPEC] + [VMEM_SPEC] * (1 + X + sum(len(s) for s in starts))
        + [ANY_SPEC] * len(after),
        out_specs=[VMEM_SPEC] * len(cuts),
        out_shape=[jax.ShapeDtypeStruct((hi - lo, BS, BS), BF16) for _, lo, hi in cuts],
        scratch_shapes=[pltpu.VMEM((n, blocks, BS, BS), F32)],
        compiler_params=params(8),
        cost_estimate=cost(1.2 * n),
        name="spread",
    )(src, pos, adj, *got, *[a for s in starts for _, _, a in s], *after)


def halves(up, down):
    half = up.shape[0] // 2

    def kernel(up_ref, down_ref, low_ref, high_ref):
        low_ref[...] = up_ref[:half]
        high_ref[...] = down_ref[half:]

    return pl.pallas_call(
        kernel,
        in_specs=[VMEM_SPEC] * 2,
        out_specs=[VMEM_SPEC] * 2,
        out_shape=[jax.ShapeDtypeStruct((half,) + up.shape[1:], up.dtype)] * 2,
        compiler_params=params(4),
        cost_estimate=cost(0.3),
        name="halves",
    )(up, down)


def sum_copies(parts, copies):
    def kernel(in_ref, out_ref):
        total = jnp.sum(in_ref[...], axis=0)
        for i in range(copies):
            out_ref[i] = total

    return pl.pallas_call(
        kernel,
        in_specs=[VMEM_SPEC],
        out_specs=VMEM_SPEC,
        out_shape=jax.ShapeDtypeStruct((copies,) + parts.shape[1:], F32),
        compiler_params=params(4),
        cost_estimate=cost(0.5),
        name="sum_copies",
    )(parts)


def attach(arrays, column):
    rows, width = column.shape
    n = arrays[0].shape[0]

    def kernel(*refs):
        ins, value, outs = refs[:X], refs[X][...], refs[X + 1 :]
        high = value.astype(BF16)
        low = (value - high.astype(F32)).astype(BF16)
        for in_ref, out_ref in zip(ins, outs):
            out_ref[:n] = in_ref[...]
            for i, part in enumerate((high, low)):
                for half in range(width // BS):
                    out_ref[n + i, half * rows : (half + 1) * rows, :] = part[
                        :, half * BS : (half + 1) * BS
                    ]

    return pl.pallas_call(
        kernel,
        in_specs=[VMEM_SPEC] * (X + 1),
        out_specs=[VMEM_SPEC] * X,
        out_shape=[jax.ShapeDtypeStruct((n + 2, BS, BS), BF16)] * X,
        compiler_params=params(4),
        cost_estimate=cost(0.5),
        name="attach",
    )(*arrays, column)


def detach(arrays, pos, shape, scale):
    n = arrays[0].shape[0] - 2
    rows, width = shape[0] // X, shape[1]

    def kernel(pos_ref, *refs):
        ins, (a_ref, b_ref, whole) = refs[:X], refs[X:]
        for d, ref in enumerate(ins):
            value = (ref[n].astype(F32) + ref[n + 1].astype(F32)) * scale
            first = pl.multiple_of(lax.rem(pos_ref[1] + d, X) * rows, rows)
            for half in range(width // BS):
                whole[pl.ds(first, rows), half * BS : (half + 1) * BS] = value[
                    half * rows : (half + 1) * rows, :
                ]
        a_ref[...] = whole[: shape[0] // 2]
        b_ref[...] = whole[shape[0] // 2 :]

    return pl.pallas_call(
        kernel,
        in_specs=[SMEM_SPEC] + [VMEM_SPEC] * X,
        out_specs=[VMEM_SPEC] * 2,
        out_shape=[jax.ShapeDtypeStruct((shape[0] // 2, width), F32)] * 2,
        scratch_shapes=[pltpu.VMEM(shape, F32)],
        compiler_params=params(4),
        cost_estimate=cost(0.5),
        name="detach",
    )(pos, *arrays)


def own_part(grad_pre, w_self, blocks):
    def kernel(grad_ref, w_ref, out_ref):
        for i in range(blocks):
            out_ref[i] = dot_nt(grad_ref[i * BS : (i + 1) * BS, :], w_ref[...])

    return pl.pallas_call(
        kernel,
        in_specs=[VMEM_SPEC] * 2,
        out_specs=VMEM_SPEC,
        out_shape=jax.ShapeDtypeStruct((blocks, BS, BS), F32),
        compiler_params=params(8),
        cost_estimate=cost(1.5),
        name="own_part",
    )(grad_pre, w_self)


def shift(value, axis, size, by):
    return lax.ppermute(value, axis, [(i, (i + by) % size) for i in range(size)])


def shift_x(values, sign):
    return [values[0]] + [shift(values[d], "x", X, sign * d) for d in range(1, X)]


def exchange(value, axes):
    return lax.all_to_all(value, axes, split_axis=0, concat_axis=0, tiled=True)


def on_device(
    features, w_self, w_neigh, cotangent, src_block, dst_block, block_count, edge_rows, edge_cols
):
    owners, cap = src_block.shape[1:]
    edges = edge_rows.shape[-1]
    local_nodes = features.shape[0]
    blocks = local_nodes // BS
    half = blocks // 2
    groups = Y * C
    node_total = local_nodes * groups * owners
    pos = jnp.stack([lax.axis_index(a) for a in ("z", "x", "y", "c")]).astype(jnp.int32)
    feats = features.reshape(blocks, BS, -1)

    own_src = src_block[0].T
    sent = pack(own_src, dst_block[0].T, block_count, edge_rows, edge_cols)
    lists = exchange(sent, "z")
    src = lists[:, :, edges].reshape(owners * cap)
    tgt = lists[:, :, edges + 1].reshape(1, owners * cap)

    batches = [(0,), (-1, 1), (-2, 2), (-3, 3), (4,)]
    *part, adj = build(batches[0], cap, edges, own_src, pos, sent, [feats], [], own=True)
    sums, adjs = [shift_x(part, 1)], [adj]
    up, down, last = feats, feats, [part[0], lists]
    for k in range(1, 5):
        if k < 4:
            up, down = follow([shift(up, "z", Z, 1), shift(down, "z", Z, -1)], last)
            arrays = [up, down]
        else:
            low, high = halves(up, down)
            arrays = [shift(low, "z", Z, 1), shift(high, "z", Z, -1)]
        after = sums[k - 2][1:] if k > 1 else []
        *part, adj = build(batches[k], cap, edges, src, pos, lists, arrays, after, extra=[tgt] if k == 2 else (), static=k == 1)
        sums.append(shift_x(part, 1))
        adjs.append(adj)
        last = part[:1] + (sums[0][1:] if k == 1 else [])
    keeps, sends, tgt = gather_sums(batches, cap, groups * blocks, pos, sum(sums, []))

    crossed = [shift(sends[dy], "c", C, 1) for dy in (2, 1, 3, 0)]
    low, high = join("cut", keeps[2], crossed[0])
    low, high = shift(low, "y", Y, 1), shift(high, "y", Y, -1)
    (ahead,) = join("low", keeps[1], crossed[1], low)
    (behind,) = join("high", keeps[3], crossed[2], high)
    arrived = [keeps[0], crossed[3], shift(ahead, "y", Y, 1), shift(behind, "y", Y, -1)]
    total = sum(a.astype(F32) for a in arrived)
    own_sums, own_cnt = total[:local_nodes], get_counts(total[local_nodes:])
    divisor = jnp.maximum(own_cnt, 1.0).reshape(local_nodes, 1)
    neigh_mean = (own_sums / divisor).astype(BF16)
    preact = jnp.dot(features, w_self, preferred_element_type=F32) + jnp.dot(
        neigh_mean, w_neigh, preferred_element_type=F32
    )
    sigmoids = jax.nn.sigmoid(preact)
    activated = (preact * sigmoids).astype(BF16)
    grad_pre = (cotangent.astype(F32) * sigmoids * (1.0 + preact * (1.0 - sigmoids))).astype(BF16)
    grad_mean = (
        jnp.einsum("nh,fh->nf", grad_pre, w_neigh, preferred_element_type=F32) / divisor
    ).astype(BF16)
    grad_mean = grad_mean.reshape(blocks, BS, -1)
    means = [grad_mean] + [shift(grad_mean, "y", Y, dy) for dy in range(1, Y)]

    both = jnp.concatenate([features, neigh_mean], axis=1)
    grads = jnp.einsum("nf,nh->fh", both, grad_pre, preferred_element_type=F32)
    width = grads.shape[1]
    piece = sum_copies(exchange(grads, ("x", "z")).reshape(owners, -1, width), groups)
    first_piece = piece
    means[2:3] = follow(means[2:3], [first_piece])
    means = [m for mean in means for m in (mean, shift(mean, "c", C, 1))]
    sets = [(4,), (-3, 3), (-2, 2), (-1, 1), (0,)]
    picked = pick(sets, cap, tgt, pos, means, first_piece)
    piece = sum_copies(exchange(piece, ("y", "c")), Z)
    column = exchange(piece, "z").reshape(-1, width)
    picked[4] = attach(picked[4], column)

    own_term = own_part(grad_pre, w_self, blocks)
    got = [shift_x(p, -1) for p in picked]

    def back(k, starts, cuts=None, after=()):
        return spread(
            batches[k], cap, blocks, src, pos, adjs[k], got[4 - k], starts, cuts, after
        )

    low, high = back(4, [[]], [(0, 0, half), (0, half, blocks)])
    up, down = shift(low, "z", Z, 1), shift(high, "z", Z, -1)
    down, up = back(3, [[(half, blocks, down)], [(0, half, up)]])
    for k in (2, 1):
        up, down = shift(up, "z", Z, 1), shift(down, "z", Z, -1)
        after = [piece] if k == 2 else [column]
        down, up = back(k, [[(0, blocks, down)], [(0, blocks, up)]], after=after)
    up, down = shift(up, "z", Z, 1), shift(down, "z", Z, -1)
    (grad_features,) = back(0, [[(0, blocks, own_term), (0, blocks, up), (0, blocks, down)]])
    grad_self, grad_neigh = detach(got[4], pos, grads.shape, float(node_total) ** (-0.5))
    return activated, grad_features.reshape(local_nodes, -1), grad_self, grad_neigh


def solution(mesh):
    mesh = Mesh(mesh.devices.reshape(Y, C, Z, X), ("y", "c", "z", "x"))
    every = ("y", "c", "z", "x")
    return jax.shard_map(
        on_device,
        mesh=mesh,
        in_specs=(
            P(every, None),
            P(),
            P(),
            P(every, None),
            P(every, None, None),
            P(every, None, None),
            P(every, None),
            P(every, None, None, None),
            P(every, None, None, None),
        ),
        out_specs=(P(every, None), P(every, None), P(), P()),
        check_vma=False,
    )
```
